32 devices in a mesh: sub: 2 (over y), front: 16 (over z, x, core).
Axes of the slice: x: 2, y: 2, z: 4, core: 2. Of those that a mesh axis runs over, the one named last changes fastest.
Arguments:
- rhs_root: float32 [22528, 128], P(('sub', 'front')), may hold values from -6 to 6
- rhs_level: float32 [11264, 128], P(('sub', 'front')), may hold values from -6 to 6
- root_inverse: bfloat16 [22528, 22528], P('front', 'sub'), as said below
- level_inverse: bfloat16 [11264, 11264], P('front', 'sub'), as said below
- coupling_t: bfloat16 [11264, 2816], P('front', 'sub'), may hold values from -0.078125 to 0.078125
- coupling_rows: int32 [16, 22], P('front', 'sub'), may hold values from 0 to 175, as said below
Outputs:
- root_potential: float32 [22528, 128], P(('sub', 'front'))
- level_potential: float32 [11264, 128], P(('sub', 'front'))
The draws below stay inside these ranges and needn't reach their ends.
Inputs may be any that keep to these rules, and one draw needn't show every extreme that they name: `root_inverse`: zero above the diagonal; diagonal entries between 0.5 and 1.5. `level_inverse`: zero above the diagonal; diagonal entries between 0.5 and 1.5. `coupling_rows`: entry [p, j] lies in the range of 88 blocks that starts at block (j // 11) * 88; the 11 entries of one panel in one range are distinct; every row block is named by some panel.
All inputs are finite; a program needn't handle non-finite values.
Results may differ from the reference program's by a relative error of at most 0.02.
Values may be sent and summed in bfloat16 or wider, within the bound.
No kernel may reach another device: no remote copies, remote signals or barrier semaphores. Data moves between devices by JAX's collectives and lax.ppermute only.
A program may use at most 128 MiB of HBM per device.

```python
import math
import jax
import jax.numpy as jnp
from jax import lax

W0 = 22528
W1 = 11264
NRHS = 128
RB = 128
KEEP = 11
PANELS = 16
PANEL = 704
SLOTS = 22
ROW_BLOCKS = 176
BPS = 88


def lower_inverse(key, order, marker):
    entries = jax.random.normal(jax.random.fold_in(key, marker), (order, order), jnp.float32)
    diagonal = jax.random.uniform(jax.random.fold_in(key, marker + 1), (order,), jnp.float32, 0.5, 1.5)
    row_index = lax.broadcasted_iota(jnp.int32, (order, order), 0)
    col_index = lax.broadcasted_iota(jnp.int32, (order, order), 1)
    below = jnp.where(row_index > col_index, entries * (1.0 / math.sqrt(order)), 0.0)
    return jnp.where(row_index == col_index, diagonal[None, :], below).astype(jnp.bfloat16)


def draw_root_inverse(key, part):
    return lower_inverse(key, W0, 101)


def draw_level_inverse(key, part):
    return lower_inverse(key, W1, 203)


def draw_coupling_rows(key, part):
    groups = SLOTS // KEEP
    first_count = (BPS + PANELS - 1) // PANELS
    base_scores = jax.random.randint(jax.random.fold_in(key, 307), (groups, BPS), 0, 1 << 20)
    base_scores = base_scores * BPS + lax.broadcasted_iota(jnp.int32, (groups, BPS), 1)
    orders = jnp.argsort(base_scores, axis=1).astype(jnp.int32)
    ranks = jnp.argsort(orders, axis=1).astype(jnp.int32)
    panel_index = lax.broadcasted_iota(jnp.int32, (groups, PANELS, BPS), 1)
    forced = (ranks[:, None, :] - panel_index * first_count) % BPS < first_count
    panel_scores = jax.random.randint(jax.random.fold_in(key, 311), (groups, PANELS, BPS), 0, 1 << 20)
    panel_scores = panel_scores * BPS + lax.broadcasted_iota(jnp.int32, (groups, PANELS, BPS), 2)
    panel_scores = jnp.where(forced, panel_scores, panel_scores + (1 << 20) * BPS)
    chosen = jnp.argsort(panel_scores, axis=2)[:, :, :KEEP].astype(jnp.int32)
    chosen = chosen + lax.broadcasted_iota(jnp.int32, (groups, PANELS, KEEP), 0) * BPS
    return jnp.transpose(chosen, (1, 0, 2)).reshape(PANELS, SLOTS).astype(jnp.int32)


def steps_of(stream_key, shape, split, least, largest):
    gain = 1.0
    for dim, shards_of in split:
        steps = jax.random.uniform(jax.random.fold_in(jax.random.fold_in(stream_key, 6), dim), (shards_of,), jnp.float32, least / len(split), largest / len(split))
        gain = gain * jnp.repeat(jnp.exp(steps), shape[dim] // shards_of).reshape((-1,) + (1,) * (len(shape) - 1 - dim))
    return gain


def normal_values(key, shape, deviation, most, split=(), kind=jnp.bfloat16):
    level = steps_of(key, shape, split, -0.22, 0.18) if split else 1.0
    result = jax.random.normal(key, shape, jnp.float32) * deviation * level
    return jnp.minimum(jnp.maximum(result, -most), most).astype(kind)


def setup_inputs(seed: int = 0) -> dict:
    key_list = jax.random.split(jax.random.key(seed), 7)
    rhs_root = normal_values(key_list[0], (W0, NRHS), 1.0, 6.0, ((0, 32),), jnp.float32)
    rhs_level = normal_values(key_list[1], (W1, NRHS), 1.0, 6.0, ((0, 32),), jnp.float32)
    root_inverse = draw_root_inverse(jax.random.fold_in(key_list[6], 71), 0)
    level_inverse = draw_level_inverse(jax.random.fold_in(key_list[6], 71), 0)
    coupling_t = normal_values(key_list[4], (W1, SLOTS * RB), (W1 // 2) ** -0.5, 0.078125, ((0, 16), (1, 2)))
    coupling_rows = draw_coupling_rows(jax.random.fold_in(key_list[6], 71), 0)
    return dict(rhs_root=rhs_root, rhs_level=rhs_level, root_inverse=root_inverse, level_inverse=level_inverse, coupling_t=coupling_t, coupling_rows=coupling_rows)


def reference(rhs_root, rhs_level, root_inverse, level_inverse, coupling_t, coupling_rows):
    highest = lax.Precision.HIGHEST
    forward_level = jnp.dot(level_inverse, rhs_level.astype(jnp.bfloat16), preferred_element_type=jnp.float32)
    forward_level_b = forward_level.astype(jnp.bfloat16)
    blocks = coupling_t.reshape(PANELS, PANEL, SLOTS, RB).astype(jnp.float32)
    level_panels = forward_level_b.reshape(PANELS, PANEL, NRHS).astype(jnp.float32)
    pushed = jnp.einsum("pcsi,pcn->psin", blocks, level_panels, precision=highest)
    selector = (coupling_rows[:, :, None] == jnp.arange(ROW_BLOCKS, dtype=jnp.int32)[None, None, :]).astype(jnp.float32)
    update = jnp.einsum("psb,psin->bin", selector, pushed, precision=highest).reshape(W0, NRHS)
    shifted_b = (rhs_root - update).astype(jnp.bfloat16)
    forward_root = jnp.dot(root_inverse, shifted_b, preferred_element_type=jnp.float32)
    forward_root_b = forward_root.astype(jnp.bfloat16)
    root_potential = jnp.dot(root_inverse.T, forward_root_b, preferred_element_type=jnp.float32)
    root_potential_b = root_potential.astype(jnp.bfloat16)
    picked = root_potential_b.reshape(ROW_BLOCKS, RB, NRHS)[coupling_rows].astype(jnp.float32)
    pulled = jnp.einsum("pcsi,psin->pcn", blocks, picked, precision=highest).reshape(W1, NRHS)
    corrected_b = (forward_level - pulled).astype(jnp.bfloat16)
    level_potential = jnp.dot(level_inverse.T, corrected_b, preferred_element_type=jnp.float32)
    return (root_potential, level_potential)
```

```python
import functools

import jax
import jax.numpy as jnp
from jax import lax
from jax.experimental import pallas as pl
from jax.experimental.pallas import tpu as pltpu
from jax.sharding import PartitionSpec as P

RB = 128
NX = 2
NC = 2
F32 = jnp.float32
BF16 = jnp.bfloat16
HIGHEST_PRECISION = lax.Precision.HIGHEST
VMEM = pl.BlockSpec(memory_space=pltpu.VMEM)
SMEM = pl.BlockSpec(memory_space=pltpu.SMEM)
VMEM_LIMIT = 48 * 1024 * 1024


def transposed_product(matrix, vector):
    return lax.dot_general(
        matrix, vector, (((0,), (0,)), ((), ())), preferred_element_type=jnp.float32
    )


def gather_columns(pieces):
    return lax.all_gather(pieces, "front", axis=0, tiled=True)


def gather_rows(pieces):
    return lax.all_gather(pieces, "sub", axis=0, tiled=True)


def share_sub(summand):
    return lax.psum_scatter(
        summand.astype(jnp.bfloat16), "sub", scatter_dimension=0, tiled=True
    ).astype(jnp.float32)


def share_front(summand):
    return lax.psum_scatter(summand, "front", scatter_dimension=0, tiled=True)


def general_body(rhs_root, rhs_level, root_inverse, level_inverse, coupling_t, coupling_rows):
    rhs_count = rhs_root.shape[1]
    block_count = root_inverse.shape[1] // RB
    slot_count = coupling_t.shape[1] // RB
    level_cols = gather_columns(rhs_level.astype(jnp.bfloat16))
    forward_level = share_sub(
        jnp.dot(level_inverse, level_cols, preferred_element_type=jnp.float32)
    )
    level_rows = gather_rows(forward_level.astype(jnp.bfloat16))
    local_block = coupling_rows[0] % block_count
    selector = (
        lax.broadcasted_iota(jnp.int32, (block_count, slot_count), 0) == local_block[None, :]
    ).astype(jnp.float32)
    pushed = transposed_product(coupling_t, level_rows).reshape(slot_count, RB, rhs_count)
    update = jnp.einsum("bk,kin->bin", selector, pushed, precision=HIGHEST_PRECISION).reshape(
        block_count * RB, rhs_count
    )
    shifted = rhs_root - share_front(update)
    root_cols = gather_columns(shifted.astype(jnp.bfloat16))
    forward_root = share_sub(jnp.dot(root_inverse, root_cols, preferred_element_type=jnp.float32))
    root_rows = gather_rows(forward_root.astype(jnp.bfloat16))
    root_potential = share_front(transposed_product(root_inverse, root_rows))
    potential_cols = gather_columns(root_potential.astype(jnp.bfloat16))
    picked = potential_cols.reshape(block_count, RB, rhs_count)[local_block]
    pulled = jnp.dot(
        coupling_t, picked.reshape(slot_count * RB, rhs_count), preferred_element_type=jnp.float32
    )
    corrected = forward_level - share_sub(pulled)
    corrected_rows = gather_rows(corrected.astype(jnp.bfloat16))
    level_potential = share_front(transposed_product(level_inverse, corrected_rows))
    return (root_potential, level_potential)


def z_shift(value, shift, nz):
    width = NX * NC
    count = nz * width
    return lax.ppermute(
        value, "front", [(i, (i + shift * width) % count) for i in range(count)]
    )


def x_swap(value, nz):
    return lax.ppermute(value, "front", [(i, i ^ NC) for i in range(nz * NX * NC)])


def c_swap(value, nz):
    return lax.ppermute(value, "front", [(i, i ^ 1) for i in range(nz * NX * NC)])


def sub_swap(value):
    return lax.ppermute(value, "sub", [(0, 1), (1, 0)])


def gather_pieces(own, nz):
    along_z = [own] + [z_shift(own, -k, nz) for k in range(1, nz)]
    pieces = []
    for held in along_z:
        across = x_swap(held, nz)
        pieces += [held, c_swap(held, nz), across, c_swap(across, nz)]
    return pieces


def scatter_sum(keep, send, nz):
    total = None
    for k in list(range(1, nz)) + [0]:
        arrived = c_swap(send[k], nz)
        near = keep[k][0].astype(F32) + arrived[0].astype(F32)
        far = keep[k][1].astype(F32) + arrived[1].astype(F32)
        partial = near + x_swap(far.astype(BF16), nz).astype(F32)
        if k:
            partial = z_shift(partial.astype(BF16), k, nz).astype(F32)
        total = partial if total is None else total + partial
    return total


def places(nz):
    me = lax.axis_index("front")
    z, x, c = me // (NX * NC), (me // NC) % NX, me % NC
    return jnp.stack(
        [
            (((z + k) % nz) * NX + (x ^ xr)) * NC + (c ^ cr)
            for k in range(nz)
            for xr in range(NX)
            for cr in range(NC)
        ]
    ).astype(jnp.int32)


def assemble(place, pieces, whole):
    rows = pieces[0].shape[0]
    for i, piece in enumerate(pieces):
        whole[pl.ds(pl.multiple_of(place[i] * rows, rows), rows), :] = piece[...]


def distribute(place, whole, keep, send):
    nz = len(keep)
    rows = keep[0].shape[1]
    for k in range(nz):
        for xr in range(NX):
            for cr, out in ((0, keep[k]), (1, send[k])):
                i = (k * NX + xr) * NC + cr
                out[xr] = whole[
                    pl.ds(pl.multiple_of(place[i] * rows, rows), rows), :
                ].astype(out.dtype)


def forward_kernel(count, place, *refs):
    pieces, (matrix, out, out_b, whole) = refs[:count], refs[count:]
    step = pl.program_id(0)
    depth = matrix.shape[1]

    @pl.when(step == 0)
    def _():
        assemble(place, pieces, whole)
        out[...] = jnp.zeros_like(out)

    cols = whole[pl.ds(pl.multiple_of(step * depth, depth), depth), :]
    out[...] += jnp.dot(matrix[...], cols, preferred_element_type=F32)

    @pl.when(step == pl.num_programs(0) - 1)
    def _():
        out_b[...] = out[...].astype(BF16)


def forward_product(place, pieces, matrix, depth):
    rows, width = matrix.shape
    n = pieces[0].shape[1]
    whole_spec = lambda shape: pl.BlockSpec(shape, lambda i, *_: (0,) * len(shape))
    return pl.pallas_call(
        functools.partial(forward_kernel, len(pieces)),
        out_shape=(
            jax.ShapeDtypeStruct((rows, n), F32),
            jax.ShapeDtypeStruct((rows, n), BF16),
        ),
        grid_spec=pltpu.PrefetchScalarGridSpec(
            num_scalar_prefetch=1,
            grid=(width // depth,),
            in_specs=[whole_spec(p.shape) for p in pieces]
            + [pl.BlockSpec((rows, depth), lambda i, *_: (0, i))],
            out_specs=(whole_spec((rows, n)), whole_spec((rows, n))),
            scratch_shapes=[pltpu.VMEM((width, n), BF16)],
        ),
        compiler_params=pltpu.CompilerParams(vmem_limit_bytes=VMEM_LIMIT),
        cost_estimate=pl.CostEstimate(
            flops=2 * rows * width * n, bytes_accessed=2 * rows * width, transcendentals=0
        ),
        name="forward_product",
    )(place, *pieces, matrix)


def backward_kernel(nz, subtract, place, own, arrived, base, matrix, *refs):
    keep, send, (vector, whole) = refs[:nz], refs[nz : 2 * nz], refs[2 * nz :]
    step = pl.program_id(0)
    width = matrix.shape[1]

    @pl.when(step == 0)
    def _():
        total = own[...] + arrived[...].astype(F32)
        if subtract:
            total = base[...] - total
        vector[...] = total.T.astype(BF16)

    product = jnp.dot(vector[...], matrix[...], preferred_element_type=F32)
    whole[pl.ds(pl.multiple_of(step * width, width), width), :] = product.T

    @pl.when(step == pl.num_programs(0) - 1)
    def _():
        distribute(place, whole, keep, send)


def backward_product(place, own, arrived, base, matrix, block, nz):
    rows, width = matrix.shape
    n = own.shape[1]
    part = width // (nz * NX * NC)
    subtract = base is not None
    if base is None:
        base = jnp.zeros((8, 128), F32)
    whole_spec = lambda shape: pl.BlockSpec(shape, lambda i, *_: (0,) * len(shape))
    outs = pl.pallas_call(
        functools.partial(backward_kernel, nz, subtract),
        out_shape=[jax.ShapeDtypeStruct((NX, part, n), F32)] * nz
        + [jax.ShapeDtypeStruct((NX, part, n), BF16)] * nz,
        grid_spec=pltpu.PrefetchScalarGridSpec(
            num_scalar_prefetch=1,
            grid=(width // block,),
            in_specs=[whole_spec(own.shape), whole_spec(own.shape), whole_spec(base.shape)]
            + [pl.BlockSpec((rows, block), lambda i, *_: (0, i))],
            out_specs=[whole_spec((NX, part, n))] * (2 * nz),
            scratch_shapes=[pltpu.VMEM((n, rows), BF16), pltpu.VMEM((width, n), F32)],
        ),
        compiler_params=pltpu.CompilerParams(vmem_limit_bytes=VMEM_LIMIT),
        cost_estimate=pl.CostEstimate(
            flops=2 * rows * width * n, bytes_accessed=2 * rows * width, transcendentals=0
        ),
        name="backward_product",
    )(place, own, arrived, base, matrix)
    return outs[:nz], outs[nz:]


def push_kernel(nz, place, block, own, arrived, coupling, *refs):
    total_out, keep, send, (whole,) = refs[0], refs[1 : nz + 1], refs[nz + 1 : 2 * nz + 1], refs[2 * nz + 1 :]
    total = own[...] + arrived[...].astype(F32)
    total_out[...] = total
    pushed = jnp.dot(total.T.astype(BF16), coupling[...], preferred_element_type=F32).T
    whole[...] = jnp.zeros_like(whole)
    for j in range(coupling.shape[1] // RB):
        start = pl.multiple_of(block[j] * RB, RB)
        whole[pl.ds(start, RB), :] = pushed[j * RB : (j + 1) * RB, :]
    distribute(place, whole, keep, send)


def push_product(place, block, own, arrived, coupling, width, nz):
    n = own.shape[1]
    part = width // (nz * NX * NC)
    outs = pl.pallas_call(
        functools.partial(push_kernel, nz),
        out_shape=[jax.ShapeDtypeStruct(own.shape, F32)]
        + [jax.ShapeDtypeStruct((NX, part, n), F32)] * nz
        + [jax.ShapeDtypeStruct((NX, part, n), BF16)] * nz,
        in_specs=[SMEM, SMEM, VMEM, VMEM, VMEM],
        out_specs=[VMEM] * (2 * nz + 1),
        scratch_shapes=[pltpu.VMEM((width, n), F32)],
        compiler_params=pltpu.CompilerParams(vmem_limit_bytes=VMEM_LIMIT),
        name="push_product",
    )(place, block, own, arrived, coupling)
    return outs[0], outs[1 : nz + 1], outs[nz + 1 :]


def pull_kernel(count, place, block, *refs):
    pieces, (coupling, out, out_b, whole, picked) = refs[:count], refs[count:]
    assemble(place, pieces, whole)
    for j in range(coupling.shape[1] // RB):
        start = pl.multiple_of(block[j] * RB, RB)
        picked[j * RB : (j + 1) * RB, :] = whole[pl.ds(start, RB), :]
    out[...] = jnp.dot(coupling[...], picked[...], preferred_element_type=F32)
    out_b[...] = out[...].astype(BF16)


def pull_product(place, block, pieces, coupling):
    rows, width = coupling.shape
    part, n = pieces[0].shape
    return pl.pallas_call(
        functools.partial(pull_kernel, len(pieces)),
        out_shape=(
            jax.ShapeDtypeStruct((rows, n), F32),
            jax.ShapeDtypeStruct((rows, n), BF16),
        ),
        in_specs=[SMEM, SMEM] + [VMEM] * (len(pieces) + 1),
        out_specs=(VMEM, VMEM),
        scratch_shapes=[
            pltpu.VMEM((part * len(pieces), n), BF16),
            pltpu.VMEM((width, n), BF16),
        ],
        compiler_params=pltpu.CompilerParams(vmem_limit_bytes=VMEM_LIMIT),
        name="pull_product",
    )(place, block, *pieces, coupling)


def column_block(width):
    for parts in (8, 4, 2, 1):
        if width % (parts * 128) == 0 and width // parts >= 1024:
            return width // parts
    return width


def two_level_body(rhs_root, rhs_level, root_inverse, level_inverse, coupling_t, coupling_rows):
    nz = lax.axis_size("front") // (NX * NC)
    width = root_inverse.shape[1]
    place = places(nz)
    block = coupling_rows[0] % (width // RB)

    level_pieces = gather_pieces(rhs_level.astype(BF16), nz)
    own, own_b = forward_product(
        place, level_pieces, level_inverse, column_block(level_inverse.shape[1])
    )
    forward_level, keep, send = push_product(
        place, block, own, sub_swap(own_b), coupling_t, width, nz
    )
    shifted = rhs_root - scatter_sum(keep, send, nz)

    root_pieces = gather_pieces(shifted.astype(BF16), nz)
    own, own_b = forward_product(place, root_pieces, root_inverse, column_block(width))
    keep, send = backward_product(
        place, own, sub_swap(own_b), None, root_inverse, column_block(width), nz
    )
    root_potential = scatter_sum(keep, send, nz)

    potential_pieces = gather_pieces(root_potential.astype(BF16), nz)
    own, own_b = pull_product(place, block, potential_pieces, coupling_t)
    keep, send = backward_product(
        place,
        own,
        sub_swap(own_b),
        forward_level,
        level_inverse,
        column_block(level_inverse.shape[1]),
        nz,
    )
    level_potential = scatter_sum(keep, send, nz)
    return (root_potential, level_potential)


def body(rhs_root, rhs_level, root_inverse, level_inverse, coupling_t, coupling_rows):
    fits = (
        lax.axis_size("sub") == 2
        and lax.axis_size("front") % (2 * NX * NC) == 0
        and all(a.shape[0] % 16 == 0 for a in (rhs_root, rhs_level, root_inverse, level_inverse))
        and all(a.shape[1] % 128 == 0 for a in (rhs_root, root_inverse, level_inverse, coupling_t))
        and root_inverse.size * 2 <= 34 * 1024 * 1024
    )
    chosen = two_level_body if fits else general_body
    return chosen(rhs_root, rhs_level, root_inverse, level_inverse, coupling_t, coupling_rows)


def solution(mesh):
    return jax.shard_map(
        body,
        mesh=mesh,
        in_specs=(
            P(("sub", "front"), None),
            P(("sub", "front"), None),
            P("front", "sub"),
            P("front", "sub"),
            P("front", "sub"),
            P("front", "sub"),
        ),
        out_specs=(P(("sub", "front"), None), P(("sub", "front"), None)),
        check_vma=False,
    )
```

```python
import functools

import jax
import jax.numpy as jnp
from jax import lax
from jax.experimental import pallas as pl
from jax.experimental.pallas import tpu as pltpu
from jax.sharding import PartitionSpec as P

RB = 128
NX = 2
NC = 2
F32 = jnp.float32
BF16 = jnp.bfloat16
HIGHEST_PRECISION = lax.Precision.HIGHEST
VMEM = pl.BlockSpec(memory_space=pltpu.VMEM)
SMEM = pl.BlockSpec(memory_space=pltpu.SMEM)
VMEM_LIMIT = 14 * 1024 * 1024


def transposed_product(matrix, vector):
    return lax.dot_general(
        matrix, vector, (((0,), (0,)), ((), ())), preferred_element_type=jnp.float32
    )


def gather_columns(pieces):
    return lax.all_gather(pieces, "front", axis=0, tiled=True)


def gather_rows(pieces):
    return lax.all_gather(pieces, "sub", axis=0, tiled=True)


def share_sub(summand):
    return lax.psum_scatter(
        summand.astype(jnp.bfloat16), "sub", scatter_dimension=0, tiled=True
    ).astype(jnp.float32)


def share_front(summand):
    return lax.psum_scatter(summand, "front", scatter_dimension=0, tiled=True)


def general_body(rhs_root, rhs_level, root_inverse, level_inverse, coupling_t, coupling_rows):
    rhs_count = rhs_root.shape[1]
    block_count = root_inverse.shape[1] // RB
    slot_count = coupling_t.shape[1] // RB
    level_cols = gather_columns(rhs_level.astype(jnp.bfloat16))
    forward_level = share_sub(
        jnp.dot(level_inverse, level_cols, preferred_element_type=jnp.float32)
    )
    level_rows = gather_rows(forward_level.astype(jnp.bfloat16))
    local_block = coupling_rows[0] % block_count
    selector = (
        lax.broadcasted_iota(jnp.int32, (block_count, slot_count), 0) == local_block[None, :]
    ).astype(jnp.float32)
    pushed = transposed_product(coupling_t, level_rows).reshape(slot_count, RB, rhs_count)
    update = jnp.einsum("bk,kin->bin", selector, pushed, precision=HIGHEST_PRECISION).reshape(
        block_count * RB, rhs_count
    )
    shifted = rhs_root - share_front(update)
    root_cols = gather_columns(shifted.astype(jnp.bfloat16))
    forward_root = share_sub(jnp.dot(root_inverse, root_cols, preferred_element_type=jnp.float32))
    root_rows = gather_rows(forward_root.astype(jnp.bfloat16))
    root_potential = share_front(transposed_product(root_inverse, root_rows))
    potential_cols = gather_columns(root_potential.astype(jnp.bfloat16))
    picked = potential_cols.reshape(block_count, RB, rhs_count)[local_block]
    pulled = jnp.dot(
        coupling_t, picked.reshape(slot_count * RB, rhs_count), preferred_element_type=jnp.float32
    )
    corrected = forward_level - share_sub(pulled)
    corrected_rows = gather_rows(corrected.astype(jnp.bfloat16))
    level_potential = share_front(transposed_product(level_inverse, corrected_rows))
    return (root_potential, level_potential)


def z_shift(value, shift, nz):
    width = NX * NC
    count = nz * width
    return lax.ppermute(
        value, "front", [(i, (i + shift * width) % count) for i in range(count)]
    )


def x_swap(value, nz):
    return lax.ppermute(value, "front", [(i, i ^ NC) for i in range(nz * NX * NC)])


def c_swap(value, nz):
    return lax.ppermute(value, "front", [(i, i ^ 1) for i in range(nz * NX * NC)])


def sub_swap(value):
    return lax.ppermute(value, "sub", [(0, 1), (1, 0)])


def gather_pieces(own, nz):
    along_z = [own] + [z_shift(own, -k, nz) for k in range(1, nz)]
    pieces = []
    for held in along_z:
        across = x_swap(held, nz)
        pieces += [held, c_swap(held, nz), across, c_swap(across, nz)]
    return pieces


def scatter_order(nz):
    return sorted(range(nz), key=lambda k: -min(k, nz - k))


def scatter_sum(keep, send, nz):
    total = None
    for k in scatter_order(nz):
        arrived = c_swap(send[k], nz)
        near = keep[k][0].astype(F32) + arrived[0].astype(F32)
        far = keep[k][1].astype(F32) + arrived[1].astype(F32)
        partial = near + x_swap(far.astype(BF16), nz).astype(F32)
        if k:
            partial = z_shift(partial.astype(BF16), k, nz).astype(F32)
        total = partial if total is None else total + partial
    return total


def places(nz):
    me = lax.axis_index("front")
    z, x, c = me // (NX * NC), (me // NC) % NX, me % NC
    return jnp.stack(
        [
            (((z + k) % nz) * NX + (x ^ xr)) * NC + (c ^ cr)
            for k in range(nz)
            for xr in range(NX)
            for cr in range(NC)
        ]
    ).astype(jnp.int32)


def assemble(place, pieces, whole):
    rows = pieces[0].shape[0]
    for i, piece in enumerate(pieces):
        whole[pl.ds(pl.multiple_of(place[i] * rows, rows), rows), :] = piece[...]


def distribute(place, whole, keep, send):
    nz = len(keep)
    rows = keep[0].shape[1]
    for k in range(nz):
        for xr in range(NX):
            for cr, out in ((0, keep[k]), (1, send[k])):
                i = (k * NX + xr) * NC + cr
                out[xr] = whole[
                    pl.ds(pl.multiple_of(place[i] * rows, rows), rows), :
                ].astype(out.dtype)


def column_step(width):
    for step in (1408, 1024, 704, 512, 256):
        if width % step == 0 and step % 128 == 0:
            return step
    return width


def forward_kernel(k, fresh, last, place, *refs):
    pieces, (matrix, acc, out, *outs_b), (cols,) = refs[: NX * NC], refs[NX * NC : -1], refs[-1:]
    rows = pieces[0].shape[0]
    depth = NX * NC * rows
    for i, piece in enumerate(pieces):
        at = place[k * NX * NC + i] % (NX * NC)
        cols[pl.ds(pl.multiple_of(at * rows, rows), rows), :] = piece[...]
    total = None if fresh else acc[...]
    step = column_step(depth)
    for j in range(depth // step):
        product = jnp.dot(
            matrix[:, j * step : (j + 1) * step],
            cols[j * step : (j + 1) * step, :],
            preferred_element_type=F32,
        )
        total = product if total is None else total + product
    out[...] = total
    if last:
        outs_b[0][...] = total.astype(BF16)


def forward_product(place, pieces, blocks, nz):
    rows = blocks[0].shape[0]
    part, n = pieces[0].shape
    group = NX * NC
    acc = jnp.zeros((8, n), F32)
    order = [0, 1, nz - 1] + list(range(2, nz - 1)) if nz > 2 else list(range(nz))
    for i, k in enumerate(order):
        fresh, last = i == 0, i == nz - 1
        outs = pl.pallas_call(
            functools.partial(forward_kernel, k, fresh, last),
            out_shape=[jax.ShapeDtypeStruct((rows, n), F32)]
            + [jax.ShapeDtypeStruct((rows, n), BF16)] * last,
            in_specs=[SMEM] + [VMEM] * (group + 2),
            out_specs=[VMEM] * (1 + last),
            scratch_shapes=[pltpu.VMEM((group * part, n), BF16)],
            compiler_params=pltpu.CompilerParams(vmem_limit_bytes=VMEM_LIMIT),
            cost_estimate=pl.CostEstimate(
                flops=2 * rows * group * part * n,
                bytes_accessed=2 * rows * group * part,
                transcendentals=0,
            ),
            name="forward_product",
        )(place, *pieces[k * group : (k + 1) * group], blocks[k], acc)
        acc = outs[0]
    return outs


def backward_kernel(k, place, vector, matrix, keep, send, whole):
    part = keep.shape[1]
    depth = NX * NC * part
    step = column_step(depth)
    for j in range(depth // step):
        whole[j * step : (j + 1) * step, :] = jnp.dot(
            vector[...], matrix[:, j * step : (j + 1) * step], preferred_element_type=F32
        ).T
    for xr in range(NX):
        for cr, out in ((0, keep), (1, send)):
            at = place[(k * NX + xr) * NC + cr] % (NX * NC)
            out[xr] = whole[pl.ds(pl.multiple_of(at * part, part), part), :].astype(out.dtype)


def backward_product(place, vector, blocks, nz):
    rows, depth = blocks[0].shape
    n = vector.shape[0]
    group = NX * NC
    part = depth // group
    keep, send = [None] * nz, [None] * nz
    for k in scatter_order(nz):
        keep[k], send[k] = pl.pallas_call(
            functools.partial(backward_kernel, k),
            out_shape=[
                jax.ShapeDtypeStruct((NX, part, n), F32),
                jax.ShapeDtypeStruct((NX, part, n), BF16),
            ],
            in_specs=[SMEM, VMEM, VMEM],
            out_specs=[VMEM, VMEM],
            scratch_shapes=[pltpu.VMEM((group * part, n), F32)],
            compiler_params=pltpu.CompilerParams(vmem_limit_bytes=VMEM_LIMIT),
            cost_estimate=pl.CostEstimate(
                flops=2 * rows * group * part * n,
                bytes_accessed=2 * rows * group * part,
                transcendentals=0,
            ),
            name="backward_product",
        )(place, vector, blocks[k])
    return keep, send


def turn_kernel(subtract, own, arrived, base, vector):
    total = own[...] + arrived[...].astype(F32)
    if subtract:
        total = base[...] - total
    vector[...] = total.T.astype(BF16)


def turn(own, arrived, base=None):
    rows, n = own.shape
    subtract = base is not None
    return pl.pallas_call(
        functools.partial(turn_kernel, subtract),
        out_shape=jax.ShapeDtypeStruct((n, rows), BF16),
        in_specs=[VMEM] * 3,
        out_specs=VMEM,
        name="turn",
    )(own, arrived, base if subtract else jnp.zeros((8, n), F32))


def push_kernel(nz, place, block, own, arrived, coupling, *refs):
    total_out, keep, send, (whole,) = refs[0], refs[1 : nz + 1], refs[nz + 1 : 2 * nz + 1], refs[2 * nz + 1 :]
    total = own[...] + arrived[...].astype(F32)
    total_out[...] = total
    pushed = jnp.dot(total.T.astype(BF16), coupling[...], preferred_element_type=F32).T
    whole[...] = jnp.zeros_like(whole)
    for j in range(coupling.shape[1] // RB):
        start = pl.multiple_of(block[j] * RB, RB)
        whole[pl.ds(start, RB), :] = pushed[j * RB : (j + 1) * RB, :]
    distribute(place, whole, keep, send)


def push_product(place, block, own, arrived, coupling, width, nz):
    n = own.shape[1]
    part = width // (nz * NX * NC)
    outs = pl.pallas_call(
        functools.partial(push_kernel, nz),
        out_shape=[jax.ShapeDtypeStruct(own.shape, F32)]
        + [jax.ShapeDtypeStruct((NX, part, n), F32)] * nz
        + [jax.ShapeDtypeStruct((NX, part, n), BF16)] * nz,
        in_specs=[SMEM, SMEM, VMEM, VMEM, VMEM],
        out_specs=[VMEM] * (2 * nz + 1),
        scratch_shapes=[pltpu.VMEM((width, n), F32)],
        compiler_params=pltpu.CompilerParams(vmem_limit_bytes=VMEM_LIMIT),
        name="push_product",
    )(place, block, own, arrived, coupling)
    return outs[0], outs[1 : nz + 1], outs[nz + 1 :]


def pull_kernel(count, place, block, *refs):
    pieces, (coupling, out, out_b, whole, picked) = refs[:count], refs[count:]
    assemble(place, pieces, whole)
    for j in range(coupling.shape[1] // RB):
        start = pl.multiple_of(block[j] * RB, RB)
        picked[j * RB : (j + 1) * RB, :] = whole[pl.ds(start, RB), :]
    out[...] = jnp.dot(coupling[...], picked[...], preferred_element_type=F32)
    out_b[...] = out[...].astype(BF16)


def pull_product(place, block, pieces, coupling):
    rows, width = coupling.shape
    part, n = pieces[0].shape
    return pl.pallas_call(
        functools.partial(pull_kernel, len(pieces)),
        out_shape=(
            jax.ShapeDtypeStruct((rows, n), F32),
            jax.ShapeDtypeStruct((rows, n), BF16),
        ),
        in_specs=[SMEM, SMEM] + [VMEM] * (len(pieces) + 1),
        out_specs=(VMEM, VMEM),
        scratch_shapes=[
            pltpu.VMEM((part * len(pieces), n), BF16),
            pltpu.VMEM((width, n), BF16),
        ],
        compiler_params=pltpu.CompilerParams(vmem_limit_bytes=VMEM_LIMIT),
        name="pull_product",
    )(place, block, *pieces, coupling)


def load_kernel(k, parts, place, matrix, out, arrived):
    rows, depth = out.shape
    first = place[k * NX * NC] // (NX * NC)
    cols = pl.ds(pl.multiple_of(first * depth, 128), depth)
    height = rows // parts
    copies = [
        pltpu.make_async_copy(
            matrix.at[pl.ds(i * height, height), cols],
            out.at[pl.ds(i * height, height), :],
            arrived.at[i],
        )
        for i in range(parts)
    ]
    for copy in copies:
        copy.start()
    for copy in copies:
        copy.wait()


def load_block(place, matrix, k, nz, name):
    rows, width = matrix.shape
    depth = width // nz
    parts = max(p for p in (1, 2, 4, 8, 11) if rows % (16 * p) == 0)
    block = pl.pallas_call(
        functools.partial(load_kernel, k, parts),
        out_shape=pltpu.VMEM((rows, depth), matrix.dtype),
        in_specs=[SMEM, pl.BlockSpec(memory_space=pltpu.HBM)],
        out_specs=VMEM,
        scratch_shapes=[pltpu.SemaphoreType.DMA((parts,))],
        compiler_params=pltpu.CompilerParams(vmem_limit_bytes=VMEM_LIMIT),
        cost_estimate=pl.CostEstimate(
            flops=0, bytes_accessed=4 * rows * depth, transcendentals=0
        ),
        name=name,
    )(place, pltpu.with_memory_space_constraint(matrix, pltpu.HBM))
    return pltpu.with_memory_space_constraint(block, pltpu.VMEM)


def two_level_body(rhs_root, rhs_level, root_inverse, level_inverse, coupling_t, coupling_rows):
    nz = lax.axis_size("front") // (NX * NC)
    width = root_inverse.shape[1]
    place = places(nz)
    block = coupling_rows[0] % (width // RB)
    level_blocks = [load_block(place, level_inverse, k, nz, "load_level") for k in range(nz)]
    level_again = [load_block(place, level_inverse, k, nz, "load_level_again") for k in range(nz)]
    root_blocks = [load_block(place, root_inverse, k, nz, "load_root") for k in range(nz)]

    level_pieces = gather_pieces(rhs_level.astype(BF16), nz)
    own, own_b = forward_product(place, level_pieces, level_blocks, nz)
    forward_level, keep, send = push_product(
        place, block, own, sub_swap(own_b), coupling_t, width, nz
    )
    shifted = rhs_root - scatter_sum(keep, send, nz)

    root_pieces = gather_pieces(shifted.astype(BF16), nz)
    own, own_b = forward_product(place, root_pieces, root_blocks, nz)
    keep, send = backward_product(place, turn(own, sub_swap(own_b)), root_blocks, nz)
    root_potential = scatter_sum(keep, send, nz)

    potential_pieces = gather_pieces(root_potential.astype(BF16), nz)
    own, own_b = pull_product(place, block, potential_pieces, coupling_t)
    keep, send = backward_product(
        place, turn(own, sub_swap(own_b), forward_level), level_again, nz
    )
    level_potential = scatter_sum(keep, send, nz)
    return (root_potential, level_potential)


def body(rhs_root, rhs_level, root_inverse, level_inverse, coupling_t, coupling_rows):
    fits = (
        lax.axis_size("sub") == 2
        and lax.axis_size("front") % (2 * NX * NC) == 0
        and all(a.shape[0] % 16 == 0 for a in (rhs_root, rhs_level, root_inverse, level_inverse))
        and all(a.shape[1] % 128 == 0 for a in (rhs_root, root_inverse, level_inverse, coupling_t))
        and root_inverse.size * 2 <= 34 * 1024 * 1024
    )
    chosen = two_level_body if fits else general_body
    return chosen(rhs_root, rhs_level, root_inverse, level_inverse, coupling_t, coupling_rows)


def solution(mesh):
    return jax.shard_map(
        body,
        mesh=mesh,
        in_specs=(
            P(("sub", "front"), None),
            P(("sub", "front"), None),
            P("front", "sub"),
            P("front", "sub"),
            P("front", "sub"),
            P("front", "sub"),
        ),
        out_specs=(P(("sub", "front"), None), P(("sub", "front"), None)),
        check_vma=False,
    )
```

```python
import functools

import jax
import jax.numpy as jnp
import numpy as np
from jax import lax
from jax.experimental import pallas as pl
from jax.experimental.pallas import tpu as pltpu
from jax.sharding import PartitionSpec as P

RB = 128
NX = 2
NC = 2
F32 = jnp.float32
BF16 = jnp.bfloat16
HIGHEST_PRECISION = lax.Precision.HIGHEST
VMEM = pl.BlockSpec(memory_space=pltpu.VMEM)
SMEM = pl.BlockSpec(memory_space=pltpu.SMEM)
VMEM_LIMIT = 32 * 1024 * 1024


def transposed_product(matrix, vector):
    return lax.dot_general(
        matrix, vector, (((0,), (0,)), ((), ())), preferred_element_type=jnp.float32
    )


def gather_columns(pieces):
    return lax.all_gather(pieces, "front", axis=0, tiled=True)


def gather_rows(pieces):
    return lax.all_gather(pieces, "sub", axis=0, tiled=True)


def share_sub(summand):
    return lax.psum_scatter(
        summand.astype(jnp.bfloat16), "sub", scatter_dimension=0, tiled=True
    ).astype(jnp.float32)


def share_front(summand):
    return lax.psum_scatter(summand, "front", scatter_dimension=0, tiled=True)


def general_body(rhs_root, rhs_level, root_inverse, level_inverse, coupling_t, coupling_rows):
    rhs_count = rhs_root.shape[1]
    block_count = root_inverse.shape[1] // RB
    slot_count = coupling_t.shape[1] // RB
    level_cols = gather_columns(rhs_level.astype(jnp.bfloat16))
    forward_level = share_sub(
        jnp.dot(level_inverse, level_cols, preferred_element_type=jnp.float32)
    )
    level_rows = gather_rows(forward_level.astype(jnp.bfloat16))
    local_block = coupling_rows[0] % block_count
    selector = (
        lax.broadcasted_iota(jnp.int32, (block_count, slot_count), 0) == local_block[None, :]
    ).astype(jnp.float32)
    pushed = transposed_product(coupling_t, level_rows).reshape(slot_count, RB, rhs_count)
    update = jnp.einsum("bk,kin->bin", selector, pushed, precision=HIGHEST_PRECISION).reshape(
        block_count * RB, rhs_count
    )
    shifted = rhs_root - share_front(update)
    root_cols = gather_columns(shifted.astype(jnp.bfloat16))
    forward_root = share_sub(jnp.dot(root_inverse, root_cols, preferred_element_type=jnp.float32))
    root_rows = gather_rows(forward_root.astype(jnp.bfloat16))
    root_potential = share_front(transposed_product(root_inverse, root_rows))
    potential_cols = gather_columns(root_potential.astype(jnp.bfloat16))
    picked = potential_cols.reshape(block_count, RB, rhs_count)[local_block]
    pulled = jnp.dot(
        coupling_t, picked.reshape(slot_count * RB, rhs_count), preferred_element_type=jnp.float32
    )
    corrected = forward_level - share_sub(pulled)
    corrected_rows = gather_rows(corrected.astype(jnp.bfloat16))
    level_potential = share_front(transposed_product(level_inverse, corrected_rows))
    return (root_potential, level_potential)


def z_shift(value, shift, nz):
    width = NX * NC
    count = nz * width
    return lax.ppermute(
        value, "front", [(i, (i + shift * width) % count) for i in range(count)]
    )


def x_swap(value, nz):
    return lax.ppermute(value, "front", [(i, i ^ NC) for i in range(nz * NX * NC)])


def c_swap(value, nz):
    return lax.ppermute(value, "front", [(i, i ^ 1) for i in range(nz * NX * NC)])


def sub_swap(value):
    return lax.ppermute(value, "sub", [(0, 1), (1, 0)])


def after(value, *others):
    return lax.optimization_barrier((value, *others))[0]


def gather_pieces(own, nz):
    order = near_first(nz)
    held = {0: own}
    for k in order[1:]:
        held[k] = z_shift(own, -k, nz)
    pieces = {}
    for k in order:
        across = x_swap(held[k], nz)
        pieces[k] = [held[k], c_swap(held[k], nz), across, c_swap(across, nz)]
    return [piece for k in range(nz) for piece in pieces[k]]


def by_arrival(items, nz):
    group = NX * NC
    return [items[k * group + i] for k in near_first(nz) for i in range(group)]


def near_first(nz):
    return sorted(range(nz), key=lambda k: min(k, nz - k))


def gather_product(place, own, matrix, nz):
    group = NX * NC
    at = Spots(nz)
    pieces = gather_pieces(own, nz)
    acc = acc_b = jnp.zeros((matrix.shape[0], own.shape[1]), F32)
    for k in near_first(nz):
        block = pieces[k * group : (k + 1) * group]
        acc, acc_b = unit_product(place, [at.blocks + k], at.near, [block], matrix, acc)
    return acc, acc_b


def ring_step(value, way, nz):
    count = NX * nz
    chip = lambda p: (p * NX if p < nz else (count - 1 - p) * NX + 1)
    pairs = [
        (chip(p) * NC + c, chip((p + way) % count) * NC + c)
        for p in range(count)
        for c in range(NC)
    ]
    return lax.ppermute(value, "front", pairs)


def ring_product(place, own, matrix, nz):
    count = NX * nz
    at = Spots(nz)
    acc = acc_b = jnp.zeros((matrix.shape[0], own.shape[1]), F32)
    held = {0: own}
    for step in range(nz + 1):
        if step:
            held = {j: after(piece, acc) for j, piece in held.items()}
        units = [[piece, c_swap(piece, nz)] for piece in held.values()]
        following = {}
        if step < nz:
            following[(-step - 1) % count] = ring_step(held[(-step) % count], 1, nz)
            if step < nz - 1:
                following[step + 1] = ring_step(held[step], -1, nz)
        acc, acc_b = unit_product(place, [at.ring + j for j in held], at.core, units, matrix, acc)
        held = following
    return acc, acc_b


def far_first(nz):
    return near_first(nz)[::-1]


def scatter_sum(keep, send, nz):
    total = None
    for k in far_first(nz):
        arrived = c_swap(send[k], nz)
        near = keep[k][0].astype(F32) + arrived[0].astype(F32)
        far = keep[k][1].astype(F32) + arrived[1].astype(F32)
        partial = near + x_swap(far.astype(BF16), nz).astype(F32)
        if k:
            partial = z_shift(partial.astype(BF16), k, nz).astype(F32)
        total = partial if total is None else total + partial
    return total


def places(nz):
    count = NX * nz
    table = []
    for me in range(count * NC):
        z, x, c = me // (NX * NC), (me // NC) % NX, me % NC
        near = [(x ^ xr) * NC + (c ^ cr) for xr in range(NX) for cr in range(NC)]
        blocks = [(z + k) % nz for k in range(nz)]
        row = [b * NX * NC + i for b in blocks for i in near]
        spot = z if x == 0 else count - 1 - z
        for j in range(count):
            p = (spot + j) % count
            row.append(p * NX if p < nz else (count - 1 - p) * NX + 1)
        table.append(row + blocks + near + [c, 1 - c])
    return lax.dynamic_index_in_dim(
        jnp.asarray(np.array(table, np.int32)), lax.axis_index("front"), 0, keepdims=False
    )


class Spots:
    def __init__(self, nz):
        group = NX * NC
        self.ring = nz * group
        self.blocks = self.ring + NX * nz
        self.near = self.blocks + nz
        self.core = self.near + group


def assemble(place, pieces, whole):
    rows = pieces[0].shape[0]
    for i, piece in enumerate(pieces):
        whole[pl.ds(pl.multiple_of(place[i] * rows, rows), rows), :] = piece[...]


def distribute(place, whole, keep, send):
    nz = len(keep)
    rows = keep[0].shape[1]
    for k in range(nz):
        for xr in range(NX):
            for cr, out in ((0, keep[k]), (1, send[k])):
                i = (k * NX + xr) * NC + cr
                out[xr] = whole[
                    pl.ds(pl.multiple_of(place[i] * rows, rows), rows), :
                ].astype(out.dtype)


def row_step(rows):
    for step in (352, 256, 128):
        if rows % step == 0:
            return step
    return rows


def unit_kernel(units, count, spots, place, *refs):
    pieces, (matrix, acc, out, out_b, cols) = refs[: units * count], refs[units * count :]
    rows = pieces[0].shape[0]
    unit = pl.program_id(1)

    @pl.when((pl.program_id(0) == 0) & (unit == 0))
    def _():
        for i, piece in enumerate(pieces):
            at = place[spots + i % count]
            cols[i // count, pl.ds(pl.multiple_of(at * rows, rows), rows), :] = piece[...]

    product = jnp.dot(matrix[...], cols[unit], preferred_element_type=F32)

    @pl.when(unit == 0)
    def _():
        out[...] = acc[...] + product

    @pl.when(unit > 0)
    def _():
        out[...] += product

    @pl.when(unit == units - 1)
    def _():
        out_b[...] = out[...].astype(BF16)


def unit_product(place, blocks, spots, units, matrix, acc):
    rows = matrix.shape[0]
    part, n = units[0][0].shape
    count = len(units[0])
    depth = count * part
    step = row_step(rows)
    first, then = blocks[0], blocks[-1]
    return pl.pallas_call(
        functools.partial(unit_kernel, len(units), count, spots),
        out_shape=(jax.ShapeDtypeStruct((rows, n), F32), jax.ShapeDtypeStruct((rows, n), BF16)),
        grid_spec=pltpu.PrefetchScalarGridSpec(
            num_scalar_prefetch=1,
            grid=(rows // step, len(units)),
            in_specs=[pl.BlockSpec((part, n), lambda i, u, place: (0, 0))] * (count * len(units))
            + [
                pl.BlockSpec(
                    (step, depth),
                    lambda i, u, place: (i, jnp.where(u == 0, place[first], place[then])),
                ),
                pl.BlockSpec((step, n), lambda i, u, place: (i, 0)),
            ],
            out_specs=[pl.BlockSpec((step, n), lambda i, u, place: (i, 0))] * 2,
            scratch_shapes=[pltpu.VMEM((len(units), depth, n), BF16)],
        ),
        compiler_params=pltpu.CompilerParams(vmem_limit_bytes=VMEM_LIMIT),
        cost_estimate=pl.CostEstimate(
            flops=2 * rows * depth * n * len(units),
            bytes_accessed=2 * rows * depth * len(units),
            transcendentals=0,
        ),
        name="unit_product",
    )(place, *[piece for unit in units for piece in unit], in_hbm(matrix), acc)


def backward_kernel(k, place, vector, matrix, keep, send, whole):
    step = pl.program_id(0)
    width = matrix.shape[1]
    part = keep.shape[1]
    product = jnp.dot(vector[...], matrix[...], preferred_element_type=F32)
    whole[pl.ds(pl.multiple_of(step * width, width), width), :] = product.T

    @pl.when(step == pl.num_programs(0) - 1)
    def _():
        for xr in range(NX):
            for cr, out in ((0, keep), (1, send)):
                at = place[(k * NX + xr) * NC + cr] % (NX * NC)
                out[xr] = whole[pl.ds(pl.multiple_of(at * part, part), part), :].astype(out.dtype)


def backward_block(place, k, vector, matrix, nz):
    rows, width = matrix.shape
    n = vector.shape[0]
    depth = width // nz
    part = depth // (NX * NC)
    step = depth // 2 if depth // 2 % 128 == 0 else depth // 11 if depth % (11 * 128) == 0 else depth
    steps = depth // step
    return pl.pallas_call(
        functools.partial(backward_kernel, k),
        out_shape=[
            jax.ShapeDtypeStruct((NX, part, n), F32),
            jax.ShapeDtypeStruct((NX, part, n), BF16),
        ],
        grid_spec=pltpu.PrefetchScalarGridSpec(
            num_scalar_prefetch=1,
            grid=(steps,),
            in_specs=[
                pl.BlockSpec((n, rows), lambda i, *_: (0, 0)),
                pl.BlockSpec(
                    (rows, step),
                    lambda i, place: (0, place[k * NX * NC] // (NX * NC) * steps + i),
                ),
            ],
            out_specs=[pl.BlockSpec((NX, part, n), lambda i, *_: (0, 0, 0))] * 2,
            scratch_shapes=[pltpu.VMEM((depth, n), F32)],
        ),
        compiler_params=pltpu.CompilerParams(vmem_limit_bytes=VMEM_LIMIT),
        cost_estimate=pl.CostEstimate(
            flops=2 * rows * depth * n, bytes_accessed=2 * rows * depth, transcendentals=0
        ),
        name="backward_block",
    )(place, vector, in_hbm(matrix))


def product_scatter(place, vector, matrix, nz):
    order = far_first(nz)
    blocks, stage_c, stage_x, stage_z = [], [], [], []
    for i in range(nz + 2):
        started = []
        if 0 <= i - 2 < nz:
            keep, arrived = blocks[i - 2][0], stage_c[i - 2]
            far = (keep[1] + arrived[1].astype(F32)).astype(BF16)
            started.append(far)
            stage_x.append(x_swap(far, nz))
        if 0 <= i - 3 < nz - 1:
            partial = leave(blocks[i - 3][0], stage_c[i - 3], stage_x[i - 3])
            started.append(partial)
            stage_z.append(z_shift(partial, order[i - 3], nz).astype(F32))
        if i < nz:
            tied = after(vector, *started) if started else vector
            blocks.append(backward_block(place, order[i], tied, matrix, nz))
            stage_c.append(c_swap(blocks[i][1], nz))
    total = blocks[-1][0][0] + stage_c[-1][0].astype(F32) + stage_x[-1].astype(F32)
    for partial in stage_z:
        total = total + partial
    return total


def leave(keep, arrived, across):
    partial = keep[0] + arrived[0].astype(F32) + across.astype(F32)
    return partial.astype(BF16)


def turn_kernel(subtract, own, arrived, base, vector):
    total = own[...] + arrived[...].astype(F32)
    if subtract:
        total = base[...] - total
    vector[...] = total.T.astype(BF16)


def turn(own, arrived, base=None):
    rows, n = own.shape
    subtract = base is not None
    return pl.pallas_call(
        functools.partial(turn_kernel, subtract),
        out_shape=jax.ShapeDtypeStruct((n, rows), BF16),
        in_specs=[VMEM] * 3,
        out_specs=VMEM,
        name="turn",
    )(own, arrived, base if subtract else jnp.zeros((8, n), F32))


def push_kernel(nz, place, block, own, arrived, coupling, *refs):
    total_out, keep, send, (whole,) = refs[0], refs[1 : nz + 1], refs[nz + 1 : 2 * nz + 1], refs[2 * nz + 1 :]
    total = own[...] + arrived[...].astype(F32)
    total_out[...] = total
    pushed = jnp.dot(total.T.astype(BF16), coupling[...], preferred_element_type=F32).T
    whole[...] = jnp.zeros_like(whole)
    for j in range(coupling.shape[1] // RB):
        start = pl.multiple_of(block[j] * RB, RB)
        whole[pl.ds(start, RB), :] = pushed[j * RB : (j + 1) * RB, :]
    distribute(place, whole, keep, send)


def push_product(place, block, own, arrived, coupling, width, nz):
    n = own.shape[1]
    part = width // (nz * NX * NC)
    outs = pl.pallas_call(
        functools.partial(push_kernel, nz),
        out_shape=[jax.ShapeDtypeStruct(own.shape, F32)]
        + [jax.ShapeDtypeStruct((NX, part, n), F32)] * nz
        + [jax.ShapeDtypeStruct((NX, part, n), BF16)] * nz,
        in_specs=[SMEM, SMEM, VMEM, VMEM, VMEM],
        out_specs=[VMEM] * (2 * nz + 1),
        scratch_shapes=[pltpu.VMEM((width, n), F32)],
        compiler_params=pltpu.CompilerParams(vmem_limit_bytes=VMEM_LIMIT),
        name="push_product",
    )(place, block, own, arrived, coupling)
    return outs[0], outs[1 : nz + 1], outs[nz + 1 :]


def pull_kernel(order, place, block, *refs):
    pieces, (coupling, out, out_b, whole, picked) = refs[: len(order)], refs[len(order) :]
    assemble([place[i] for i in order], pieces, whole)
    for j in range(coupling.shape[1] // RB):
        start = pl.multiple_of(block[j] * RB, RB)
        picked[j * RB : (j + 1) * RB, :] = whole[pl.ds(start, RB), :]
    out[...] = jnp.dot(coupling[...], picked[...], preferred_element_type=F32)
    out_b[...] = out[...].astype(BF16)


def pull_product(place, block, pieces, coupling, nz):
    rows, width = coupling.shape
    part, n = pieces[0].shape
    return pl.pallas_call(
        functools.partial(pull_kernel, by_arrival(range(len(pieces)), nz)),
        out_shape=(
            jax.ShapeDtypeStruct((rows, n), F32),
            jax.ShapeDtypeStruct((rows, n), BF16),
        ),
        in_specs=[SMEM, SMEM] + [VMEM] * (len(pieces) + 1),
        out_specs=(VMEM, VMEM),
        scratch_shapes=[
            pltpu.VMEM((part * len(pieces), n), BF16),
            pltpu.VMEM((width, n), BF16),
        ],
        compiler_params=pltpu.CompilerParams(vmem_limit_bytes=VMEM_LIMIT),
        name="pull_product",
    )(place, block, *pieces, coupling)


def in_hbm(matrix):
    return pltpu.with_memory_space_constraint(matrix, pltpu.HBM)


def two_level_body(rhs_root, rhs_level, root_inverse, level_inverse, coupling_t, coupling_rows):
    nz = lax.axis_size("front") // (NX * NC)
    width = root_inverse.shape[1]
    place = places(nz)
    block = coupling_rows[0] % (width // RB)

    own, own_b = gather_product(place, rhs_level.astype(BF16), level_inverse, nz)
    forward_level, keep, send = push_product(
        place, block, own, sub_swap(own_b), coupling_t, width, nz
    )
    shifted = rhs_root - scatter_sum(keep, send, nz)

    own, own_b = ring_product(place, shifted.astype(BF16), root_inverse, nz)
    root_potential = product_scatter(place, turn(own, sub_swap(own_b)), root_inverse, nz)

    potential_pieces = gather_pieces(root_potential.astype(BF16), nz)
    own, own_b = pull_product(
        place, block, by_arrival(potential_pieces, nz), coupling_t, nz
    )
    level_potential = product_scatter(
        place, turn(own, sub_swap(own_b), forward_level), level_inverse, nz
    )
    return (root_potential, level_potential)


def body(rhs_root, rhs_level, root_inverse, level_inverse, coupling_t, coupling_rows):
    fits = (
        lax.axis_size("sub") == 2
        and lax.axis_size("front") % (2 * NX * NC) == 0
        and all(a.shape[0] % 16 == 0 for a in (rhs_root, rhs_level, root_inverse, level_inverse))
        and all(a.shape[1] % 128 == 0 for a in (rhs_root, root_inverse, level_inverse, coupling_t))
        and NC * rhs_root.shape[0] % 128 == 0
        and NX * NC * rhs_level.shape[0] % 128 == 0
        and root_inverse.size * 2 <= 34 * 1024 * 1024
    )
    chosen = two_level_body if fits else general_body
    return chosen(rhs_root, rhs_level, root_inverse, level_inverse, coupling_t, coupling_rows)


def solution(mesh):
    return jax.shard_map(
        body,
        mesh=mesh,
        in_specs=(
            P(("sub", "front"), None),
            P(("sub", "front"), None),
            P("front", "sub"),
            P("front", "sub"),
            P("front", "sub"),
            P("front", "sub"),
        ),
        out_specs=(P(("sub", "front"), None), P(("sub", "front"), None)),
        check_vma=False,
    )
```

```python
import functools

import jax
import jax.numpy as jnp
import numpy as np
from jax import lax
from jax.experimental import pallas as pl
from jax.experimental.pallas import tpu as pltpu
from jax.sharding import PartitionSpec as P

RB = 128
NX = 2
NC = 2
F32 = jnp.float32
BF16 = jnp.bfloat16
HIGHEST_PRECISION = lax.Precision.HIGHEST
VMEM = pl.BlockSpec(memory_space=pltpu.VMEM)
SMEM = pl.BlockSpec(memory_space=pltpu.SMEM)
HBM = pl.BlockSpec(memory_space=pltpu.HBM)
VMEM_LIMIT = 32 * 1024 * 1024
CHUNK = 512


def transposed_product(matrix, vector):
    return lax.dot_general(
        matrix, vector, (((0,), (0,)), ((), ())), preferred_element_type=jnp.float32
    )


def gather_columns(pieces):
    return lax.all_gather(pieces, "front", axis=0, tiled=True)


def gather_rows(pieces):
    return lax.all_gather(pieces, "sub", axis=0, tiled=True)


def share_sub(summand):
    return lax.psum_scatter(
        summand.astype(jnp.bfloat16), "sub", scatter_dimension=0, tiled=True
    ).astype(jnp.float32)


def share_front(summand):
    return lax.psum_scatter(summand, "front", scatter_dimension=0, tiled=True)


def general_body(rhs_root, rhs_level, root_inverse, level_inverse, coupling_t, coupling_rows):
    rhs_count = rhs_root.shape[1]
    block_count = root_inverse.shape[1] // RB
    slot_count = coupling_t.shape[1] // RB
    level_cols = gather_columns(rhs_level.astype(jnp.bfloat16))
    forward_level = share_sub(
        jnp.dot(level_inverse, level_cols, preferred_element_type=jnp.float32)
    )
    level_rows = gather_rows(forward_level.astype(jnp.bfloat16))
    local_block = coupling_rows[0] % block_count
    selector = (
        lax.broadcasted_iota(jnp.int32, (block_count, slot_count), 0) == local_block[None, :]
    ).astype(jnp.float32)
    pushed = transposed_product(coupling_t, level_rows).reshape(slot_count, RB, rhs_count)
    update = jnp.einsum("bk,kin->bin", selector, pushed, precision=HIGHEST_PRECISION).reshape(
        block_count * RB, rhs_count
    )
    shifted = rhs_root - share_front(update)
    root_cols = gather_columns(shifted.astype(jnp.bfloat16))
    forward_root = share_sub(jnp.dot(root_inverse, root_cols, preferred_element_type=jnp.float32))
    root_rows = gather_rows(forward_root.astype(jnp.bfloat16))
    root_potential = share_front(transposed_product(root_inverse, root_rows))
    potential_cols = gather_columns(root_potential.astype(jnp.bfloat16))
    picked = potential_cols.reshape(block_count, RB, rhs_count)[local_block]
    pulled = jnp.dot(
        coupling_t, picked.reshape(slot_count * RB, rhs_count), preferred_element_type=jnp.float32
    )
    corrected = forward_level - share_sub(pulled)
    corrected_rows = gather_rows(corrected.astype(jnp.bfloat16))
    level_potential = share_front(transposed_product(level_inverse, corrected_rows))
    return (root_potential, level_potential)


def z_shift(value, shift, nz):
    width = NX * NC
    count = nz * width
    return lax.ppermute(
        value, "front", [(i, (i + shift * width) % count) for i in range(count)]
    )


def x_swap(value, nz):
    return lax.ppermute(value, "front", [(i, i ^ NC) for i in range(nz * NX * NC)])


def c_swap(value, nz):
    return lax.ppermute(value, "front", [(i, i ^ 1) for i in range(nz * NX * NC)])


def sub_swap(value):
    return lax.ppermute(value, "sub", [(0, 1), (1, 0)])


def after(value, *others):
    return lax.optimization_barrier((value, *others))[0]


def gather_pieces(own, nz):
    order = near_first(nz)
    held = {0: own}
    for k in order[1:]:
        held[k] = z_shift(own, -k, nz)
    pieces = {}
    for k in order:
        across = x_swap(held[k], nz)
        pieces[k] = [held[k], c_swap(held[k], nz), across, c_swap(across, nz)]
    return [piece for k in range(nz) for piece in pieces[k]]


def by_arrival(items, nz):
    group = NX * NC
    return [items[k * group + i] for k in near_first(nz) for i in range(group)]


def near_first(nz):
    return sorted(range(nz), key=lambda k: min(k, nz - k))


def gather_product(place, own, matrix, nz):
    group = NX * NC
    at = Spots(nz)
    pieces = gather_pieces(own, nz)
    order = near_first(nz)
    units = [pieces[k * group : (k + 1) * group] for k in order]
    return unit_product(place, [at.blocks + k for k in order], at.near, units, matrix, None, True)


def ring_step(value, way, nz):
    count = NX * nz
    chip = lambda p: (p * NX if p < nz else (count - 1 - p) * NX + 1)
    pairs = [
        (chip(p) * NC + c, chip((p + way) % count) * NC + c)
        for p in range(count)
        for c in range(NC)
    ]
    return lax.ppermute(value, "front", pairs)


def ring_product(place, own, matrix, nz):
    count = NX * nz
    at = Spots(nz)
    acc = None
    held = {0: own}
    for step in range(nz + 1):
        if step:
            held = {j: after(piece, acc) for j, piece in held.items()}
        units = [[piece, c_swap(piece, nz)] for piece in held.values()]
        following = {}
        if step < nz:
            following[(-step - 1) % count] = ring_step(held[(-step) % count], 1, nz)
            if step < nz - 1:
                following[step + 1] = ring_step(held[step], -1, nz)
        blocks = [at.ring + j for j in held]
        acc, *acc_b = unit_product(place, blocks, at.core, units, matrix, acc, step == nz)
        held = following
    return acc, acc_b[0]


def far_first(nz):
    return near_first(nz)[::-1]


def scatter_sum(keep, send, nz):
    total = None
    for k in far_first(nz):
        arrived = c_swap(send[k], nz)
        near = keep[k][0].astype(F32) + arrived[0].astype(F32)
        far = keep[k][1].astype(F32) + arrived[1].astype(F32)
        partial = near + x_swap(far.astype(BF16), nz).astype(F32)
        if k:
            partial = z_shift(partial.astype(BF16), k, nz).astype(F32)
        total = partial if total is None else total + partial
    return total


def places(nz):
    count = NX * nz
    table = []
    for me in range(count * NC):
        z, x, c = me // (NX * NC), (me // NC) % NX, me % NC
        near = [(x ^ xr) * NC + (c ^ cr) for xr in range(NX) for cr in range(NC)]
        blocks = [(z + k) % nz for k in range(nz)]
        row = [b * NX * NC + i for b in blocks for i in near]
        spot = z if x == 0 else count - 1 - z
        for j in range(count):
            p = (spot + j) % count
            row.append(p * NX if p < nz else (count - 1 - p) * NX + 1)
        table.append(row + blocks + near + [c, 1 - c])
    return lax.dynamic_index_in_dim(
        jnp.asarray(np.array(table, np.int32)), lax.axis_index("front"), 0, keepdims=False
    )


class Spots:
    def __init__(self, nz):
        self.nz = nz
        group = NX * NC
        self.ring = nz * group
        self.blocks = self.ring + NX * nz
        self.near = self.blocks + nz
        self.core = self.near + group


def assemble(place, pieces, whole):
    rows = pieces[0].shape[0]
    for i, piece in enumerate(pieces):
        whole[pl.ds(pl.multiple_of(place[i] * rows, rows), rows), :] = piece[...]


def distribute(place, whole, keep, send):
    nz = len(keep)
    rows = keep[0].shape[1]
    for k in range(nz):
        for xr in range(NX):
            for cr, out in ((0, keep[k]), (1, send[k])):
                i = (k * NX + xr) * NC + cr
                out[xr] = whole[
                    pl.ds(pl.multiple_of(place[i] * rows, rows), rows), :
                ].astype(out.dtype)


def row_chunks(rows):
    return [(start, min(CHUNK, rows - start)) for start in range(0, rows, CHUNK)]


def start_blocks(matrix, firsts, buffer, arrived):
    rows, depth = buffer.shape[1:]
    copies = []
    for u, first in enumerate(firsts):
        cols = pl.ds(pl.multiple_of(first * depth, 128), depth)
        copies.append(
            [
                pltpu.make_async_copy(
                    matrix.at[pl.ds(start, height), cols],
                    buffer.at[u, pl.ds(start, height), :],
                    arrived.at[u, i],
                )
                for i, (start, height) in enumerate(row_chunks(rows))
            ]
        )
    for column in copies:
        for copy in column:
            copy.start()
    return copies


def buffers(units, rows, depth, dtype):
    return [
        pltpu.VMEM((units, rows, depth), dtype),
        pltpu.SemaphoreType.DMA((units, len(row_chunks(rows)))),
    ]


def unit_kernel(blocks, spots, count, fresh, last, place, *refs):
    units = len(blocks)
    pieces, refs = refs[: units * count], refs[units * count :]
    if not fresh:
        acc, refs = refs[0], refs[1:]
    matrix, out = refs[0], refs[1]
    cols, buffer, arrived = refs[-3:]
    copies = start_blocks(matrix, [place[b] for b in blocks], buffer, arrived)
    rows = pieces[0].shape[0]
    for i, piece in enumerate(pieces):
        at = place[spots + i % count]
        cols[i // count, pl.ds(pl.multiple_of(at * rows, rows), rows), :] = piece[...]
    for u in range(units):
        for i, (start, height) in enumerate(row_chunks(buffer.shape[1])):
            copies[u][i].wait()
            here = slice(start, start + height)
            total = jnp.dot(buffer[u, here, :], cols[u], preferred_element_type=F32)
            if u:
                total += out[here, :]
            elif not fresh:
                total += acc[here, :]
            out[here, :] = total
            if last and u == units - 1:
                refs[2][here, :] = total.astype(BF16)


def unit_product(place, blocks, spots, units, matrix, acc, last):
    rows = matrix.shape[0]
    part, n = units[0][0].shape
    count = len(units[0])
    depth = count * part
    pieces = [piece for unit in units for piece in unit]
    start = [] if acc is None else [acc]
    return pl.pallas_call(
        functools.partial(unit_kernel, blocks, spots, count, acc is None, last),
        out_shape=[jax.ShapeDtypeStruct((rows, n), F32)]
        + [jax.ShapeDtypeStruct((rows, n), BF16)] * last,
        in_specs=[SMEM] + [VMEM] * (len(pieces) + len(start)) + [HBM],
        out_specs=[VMEM] * (1 + last),
        scratch_shapes=[pltpu.VMEM((len(units), depth, n), BF16)]
        + buffers(len(units), rows, depth, matrix.dtype),
        compiler_params=pltpu.CompilerParams(vmem_limit_bytes=VMEM_LIMIT),
        cost_estimate=pl.CostEstimate(
            flops=2 * rows * depth * n * len(units),
            bytes_accessed=2 * rows * depth * len(units),
            transcendentals=0,
        ),
        name="unit_product",
    )(place, *pieces, *start, in_hbm(matrix))


def backward_kernel(ks, at, count, place, *refs):
    inputs, refs = refs[:count], refs[count:]
    matrix, outs = refs[0], refs[1 : 1 + 2 * len(ks)]
    whole, buffer, arrived = refs[-3:]
    copies = start_blocks(matrix, [place[at.blocks + k] for k in ks], buffer, arrived)
    if count == 1:
        vector = inputs[0]
    else:
        vector = refs[1 + 2 * len(ks)]
        total = inputs[0][...] + inputs[1][...].astype(F32)
        if count == 3:
            total = inputs[2][...] - total
        vector[...] = total.T.astype(BF16)
    for u, k in enumerate(ks):
        total = None
        for i, (start, height) in enumerate(row_chunks(buffer.shape[1])):
            copies[u][i].wait()
            here = slice(start, start + height)
            product = jnp.dot(vector[:, here], buffer[u, here, :], preferred_element_type=F32)
            total = product if total is None else total + product
        whole[...] = total.T
        part = outs[2 * u].shape[1]
        for xr in range(NX):
            for cr in range(NC):
                out = outs[2 * u + cr]
                spot = place[at.near + xr * NC + cr]
                out[xr] = whole[pl.ds(pl.multiple_of(spot * part, part), part), :].astype(out.dtype)


def backward_blocks(place, ks, inputs, matrix, nz):
    rows, width = matrix.shape
    n = inputs[0].shape[0] if len(inputs) == 1 else inputs[0].shape[1]
    depth = width // nz
    part = depth // (NX * NC)
    fresh = len(inputs) > 1
    outs = pl.pallas_call(
        functools.partial(backward_kernel, ks, Spots(nz), len(inputs)),
        out_shape=[
            jax.ShapeDtypeStruct((NX, part, n), F32),
            jax.ShapeDtypeStruct((NX, part, n), BF16),
        ]
        * len(ks)
        + [jax.ShapeDtypeStruct((n, rows), BF16)] * fresh,
        in_specs=[SMEM] + [VMEM] * len(inputs) + [HBM],
        out_specs=[VMEM] * (2 * len(ks) + fresh),
        scratch_shapes=[pltpu.VMEM((depth, n), F32)]
        + buffers(len(ks), rows, depth, matrix.dtype),
        compiler_params=pltpu.CompilerParams(vmem_limit_bytes=VMEM_LIMIT),
        cost_estimate=pl.CostEstimate(
            flops=2 * rows * depth * n * len(ks),
            bytes_accessed=2 * rows * depth * len(ks),
            transcendentals=0,
        ),
        name="backward_blocks",
    )(place, *inputs, in_hbm(matrix))
    pairs = {k: (outs[2 * u], outs[2 * u + 1]) for u, k in enumerate(ks)}
    return pairs, outs[-1] if fresh else inputs[0]


def product_scatter(place, inputs, matrix, groups, nz):
    keep, moved, across, left = {}, {}, {}, {}
    for g in range(len(groups) + 3):
        started = []
        for k in groups[g - 2] if 0 <= g - 2 < len(groups) else []:
            far = (keep[k][1] + moved[k][1].astype(F32)).astype(BF16)
            started.append(far)
            across[k] = x_swap(far, nz)
        for k in groups[g - 3] if 0 <= g - 3 < len(groups) else []:
            partial = keep[k][0] + moved[k][0].astype(F32) + across[k].astype(F32)
            if k:
                partial = partial.astype(BF16)
                started.append(partial)
                partial = z_shift(partial, k, nz).astype(F32)
            left[k] = partial
        if g < len(groups):
            tied = [after(inputs[0], *started), *inputs[1:]] if started else inputs
            pairs, vector = backward_blocks(place, groups[g], tied, matrix, nz)
            inputs = [vector]
            for k, (mine, sent) in pairs.items():
                keep[k] = mine
                moved[k] = c_swap(sent, nz)
    total = left[0]
    for k in far_first(nz)[:-1]:
        total = total + left[k]
    return total


def push_kernel(nz, place, block, own, arrived, coupling, *refs):
    total_out, keep, send, (whole,) = refs[0], refs[1 : nz + 1], refs[nz + 1 : 2 * nz + 1], refs[2 * nz + 1 :]
    total = own[...] + arrived[...].astype(F32)
    total_out[...] = total
    pushed = jnp.dot(total.T.astype(BF16), coupling[...], preferred_element_type=F32).T
    whole[...] = jnp.zeros_like(whole)
    for j in range(coupling.shape[1] // RB):
        start = pl.multiple_of(block[j] * RB, RB)
        whole[pl.ds(start, RB), :] = pushed[j * RB : (j + 1) * RB, :]
    distribute(place, whole, keep, send)


def push_product(place, block, own, arrived, coupling, width, nz):
    n = own.shape[1]
    part = width // (nz * NX * NC)
    outs = pl.pallas_call(
        functools.partial(push_kernel, nz),
        out_shape=[jax.ShapeDtypeStruct(own.shape, F32)]
        + [jax.ShapeDtypeStruct((NX, part, n), F32)] * nz
        + [jax.ShapeDtypeStruct((NX, part, n), BF16)] * nz,
        in_specs=[SMEM, SMEM, VMEM, VMEM, VMEM],
        out_specs=[VMEM] * (2 * nz + 1),
        scratch_shapes=[pltpu.VMEM((width, n), F32)],
        compiler_params=pltpu.CompilerParams(vmem_limit_bytes=VMEM_LIMIT),
        name="push_product",
    )(place, block, own, arrived, coupling)
    return outs[0], outs[1 : nz + 1], outs[nz + 1 :]


def pull_kernel(order, place, block, *refs):
    pieces, (coupling, out, out_b, whole, picked) = refs[: len(order)], refs[len(order) :]
    assemble([place[i] for i in order], pieces, whole)
    for j in range(coupling.shape[1] // RB):
        start = pl.multiple_of(block[j] * RB, RB)
        picked[j * RB : (j + 1) * RB, :] = whole[pl.ds(start, RB), :]
    out[...] = jnp.dot(coupling[...], picked[...], preferred_element_type=F32)
    out_b[...] = out[...].astype(BF16)


def pull_product(place, block, pieces, coupling, nz):
    rows, width = coupling.shape
    part, n = pieces[0].shape
    return pl.pallas_call(
        functools.partial(pull_kernel, by_arrival(range(len(pieces)), nz)),
        out_shape=(
            jax.ShapeDtypeStruct((rows, n), F32),
            jax.ShapeDtypeStruct((rows, n), BF16),
        ),
        in_specs=[SMEM, SMEM] + [VMEM] * (len(pieces) + 1),
        out_specs=(VMEM, VMEM),
        scratch_shapes=[
            pltpu.VMEM((part * len(pieces), n), BF16),
            pltpu.VMEM((width, n), BF16),
        ],
        compiler_params=pltpu.CompilerParams(vmem_limit_bytes=VMEM_LIMIT),
        name="pull_product",
    )(place, block, *pieces, coupling)


def in_hbm(matrix):
    return pltpu.with_memory_space_constraint(matrix, pltpu.HBM)


def two_level_body(rhs_root, rhs_level, root_inverse, level_inverse, coupling_t, coupling_rows):
    nz = lax.axis_size("front") // (NX * NC)
    width = root_inverse.shape[1]
    place = places(nz)
    block = coupling_rows[0] % (width // RB)

    own, own_b = gather_product(place, rhs_level.astype(BF16), level_inverse, nz)
    forward_level, keep, send = push_product(
        place, block, own, sub_swap(own_b), coupling_t, width, nz
    )
    shifted = rhs_root - scatter_sum(keep, send, nz)

    own, own_b = ring_product(place, shifted.astype(BF16), root_inverse, nz)
    root_potential = product_scatter(
        place, [own, sub_swap(own_b)], root_inverse, [[k] for k in far_first(nz)], nz
    )

    potential_pieces = gather_pieces(root_potential.astype(BF16), nz)
    own, own_b = pull_product(
        place, block, by_arrival(potential_pieces, nz), coupling_t, nz
    )
    far = far_first(nz)
    level_potential = product_scatter(
        place,
        [own, sub_swap(own_b), forward_level],
        level_inverse,
        [far[: nz // 2], far[nz // 2 :]],
        nz,
    )
    return (root_potential, level_potential)


def body(rhs_root, rhs_level, root_inverse, level_inverse, coupling_t, coupling_rows):
    fits = (
        lax.axis_size("sub") == 2
        and lax.axis_size("front") % (2 * NX * NC) == 0
        and all(a.shape[0] % 16 == 0 for a in (rhs_root, rhs_level, root_inverse, level_inverse))
        and all(a.shape[1] % 128 == 0 for a in (rhs_root, root_inverse, level_inverse, coupling_t))
        and NC * rhs_root.shape[0] % 128 == 0
        and NX * NC * rhs_level.shape[0] % 128 == 0
        and root_inverse.size * 2 <= 34 * 1024 * 1024
    )
    chosen = two_level_body if fits else general_body
    return chosen(rhs_root, rhs_level, root_inverse, level_inverse, coupling_t, coupling_rows)


def solution(mesh):
    return jax.shard_map(
        body,
        mesh=mesh,
        in_specs=(
            P(("sub", "front"), None),
            P(("sub", "front"), None),
            P("front", "sub"),
            P("front", "sub"),
            P("front", "sub"),
            P("front", "sub"),
        ),
        out_specs=(P(("sub", "front"), None), P(("sub", "front"), None)),
        check_vma=False,
    )
```

```python
import functools

import jax
import jax.numpy as jnp
import numpy as np
from jax import lax
from jax.experimental import pallas as pl
from jax.experimental.pallas import tpu as pltpu
from jax.sharding import PartitionSpec as P

RB = 128
NX = 2
NC = 2
F32 = jnp.float32
BF16 = jnp.bfloat16
HIGHEST_PRECISION = lax.Precision.HIGHEST
VMEM = pl.BlockSpec(memory_space=pltpu.VMEM)
SMEM = pl.BlockSpec(memory_space=pltpu.SMEM)
HBM = pl.BlockSpec(memory_space=pltpu.HBM)
ANY = pl.BlockSpec(memory_space=pl.ANY)
VMEM_LIMIT = 16 * 1024 * 1024


def transposed_product(matrix, vector):
    return lax.dot_general(
        matrix, vector, (((0,), (0,)), ((), ())), preferred_element_type=jnp.float32
    )


def gather_columns(pieces):
    return lax.all_gather(pieces, "front", axis=0, tiled=True)


def gather_rows(pieces):
    return lax.all_gather(pieces, "sub", axis=0, tiled=True)


def share_sub(summand):
    return lax.psum_scatter(
        summand.astype(jnp.bfloat16), "sub", scatter_dimension=0, tiled=True
    ).astype(jnp.float32)


def share_front(summand):
    return lax.psum_scatter(summand, "front", scatter_dimension=0, tiled=True)


def general_body(rhs_root, rhs_level, root_inverse, level_inverse, coupling_t, coupling_rows):
    rhs_count = rhs_root.shape[1]
    block_count = root_inverse.shape[1] // RB
    slot_count = coupling_t.shape[1] // RB
    level_cols = gather_columns(rhs_level.astype(jnp.bfloat16))
    forward_level = share_sub(
        jnp.dot(level_inverse, level_cols, preferred_element_type=jnp.float32)
    )
    level_rows = gather_rows(forward_level.astype(jnp.bfloat16))
    local_block = coupling_rows[0] % block_count
    selector = (
        lax.broadcasted_iota(jnp.int32, (block_count, slot_count), 0) == local_block[None, :]
    ).astype(jnp.float32)
    pushed = transposed_product(coupling_t, level_rows).reshape(slot_count, RB, rhs_count)
    update = jnp.einsum("bk,kin->bin", selector, pushed, precision=HIGHEST_PRECISION).reshape(
        block_count * RB, rhs_count
    )
    shifted = rhs_root - share_front(update)
    root_cols = gather_columns(shifted.astype(jnp.bfloat16))
    forward_root = share_sub(jnp.dot(root_inverse, root_cols, preferred_element_type=jnp.float32))
    root_rows = gather_rows(forward_root.astype(jnp.bfloat16))
    root_potential = share_front(transposed_product(root_inverse, root_rows))
    potential_cols = gather_columns(root_potential.astype(jnp.bfloat16))
    picked = potential_cols.reshape(block_count, RB, rhs_count)[local_block]
    pulled = jnp.dot(
        coupling_t, picked.reshape(slot_count * RB, rhs_count), preferred_element_type=jnp.float32
    )
    corrected = forward_level - share_sub(pulled)
    corrected_rows = gather_rows(corrected.astype(jnp.bfloat16))
    level_potential = share_front(transposed_product(level_inverse, corrected_rows))
    return (root_potential, level_potential)


def z_shift(value, shift, nz):
    width = NX * NC
    count = nz * width
    return lax.ppermute(
        value, "front", [(i, (i + shift * width) % count) for i in range(count)]
    )


def x_swap(value, nz):
    return lax.ppermute(value, "front", [(i, i ^ NC) for i in range(nz * NX * NC)])


def c_swap(value, nz):
    return lax.ppermute(value, "front", [(i, i ^ 1) for i in range(nz * NX * NC)])


def sub_swap(value):
    return lax.ppermute(value, "sub", [(0, 1), (1, 0)])


def gather_pieces(own, mark, nz):
    group = NX * NC
    order = near_first(nz)
    held = {0: own}
    for k in order[1:]:
        held[k] = z_shift(own, -k, nz)
    mark, *arrived = ahead_of(mark, *[held[k] for k in order[1:-1]])
    held.update(zip(order[1:-1], arrived))
    across = {}
    for k in order:
        across[k] = x_swap(held[k], nz)
    lanes = [(k * group, held[k]) for k in order], [(k * group + NC, across[k]) for k in order]
    pieces = lanes[0] + lanes[1]
    out = [(piece, [spot]) for spot, piece in pieces]
    for batch in (lanes[0] + lanes[1][:-1], lanes[1][-1:]):
        sent = [piece for _, piece in batch]
        sent = jnp.concatenate(sent) if len(sent) > 1 else sent[0]
        out.append((c_swap(sent, nz), [spot + 1 for spot, _ in batch]))
    return out, mark


def near_first(nz):
    return sorted(range(nz), key=lambda k: min(k, nz - k))


def ring_step(value, way, nz):
    count = NX * nz
    chip = lambda p: (p * NX if p < nz else (count - 1 - p) * NX + 1)
    pairs = [
        (chip(p) * NC + c, chip((p + way) % count) * NC + c)
        for p in range(count)
        for c in range(NC)
    ]
    return lax.ppermute(value, "front", pairs)


def ring_product(place, own, matrix, mark, nz):
    count = NX * nz
    at = Spots(nz)
    acc = None
    held = {0: own}
    for step in range(nz + 1):
        if step:
            acc, *arrived = ahead_of(acc, *held.values())
            held = dict(zip(held, arrived))
        following = {}
        if step < nz:
            following[(-step - 1) % count] = ring_step(held[(-step) % count], 1, nz)
            if step < nz - 1:
                following[step + 1] = ring_step(held[step], -1, nz)
        units = [[piece, c_swap(piece, nz)] for piece in held.values()]
        blocks = [at.ring + j for j in held]
        acc, *acc_b = unit_product(
            place, blocks, at.core, units, matrix, mark, acc, step == nz
        )
        held = following
    return acc, acc_b[0]


def far_first(nz):
    return near_first(nz)[::-1]


def scatter_sum(keep, send, load, nz):
    order = far_first(nz)
    moved = {k: c_swap(send[k], nz) for k in order}
    across, partial = {}, {}
    for k in order:
        far = (keep[k][1].astype(F32) + moved[k][1].astype(F32)).astype(BF16)
        across[k] = x_swap(far, nz)
    for k in order:
        partial[k] = keep[k][0].astype(F32) + moved[k][0].astype(F32) + across[k].astype(F32)
    total = partial[0]
    leaving = {k: partial[k].astype(BF16) for k in order[:-1]}
    mark = load(leaving[order[-2]])
    arrived = [z_shift(leaving[k], k, nz) for k in order[:-1]]
    mark, *arrived = ahead_of(mark, *arrived)
    for value in arrived:
        total = total + value.astype(F32)
    return total, mark


def places(nz):
    count = NX * nz
    table = []
    for me in range(count * NC):
        z, x, c = me // (NX * NC), (me // NC) % NX, me % NC
        near = [(x ^ xr) * NC + (c ^ cr) for xr in range(NX) for cr in range(NC)]
        blocks = [(z + k) % nz for k in range(nz)]
        row = [b * NX * NC + i for b in blocks for i in near]
        spot = z if x == 0 else count - 1 - z
        for j in range(count):
            p = (spot + j) % count
            row.append(p * NX if p < nz else (count - 1 - p) * NX + 1)
        table.append(row + blocks + near + [c, 1 - c])
    return lax.dynamic_index_in_dim(
        jnp.asarray(np.array(table, np.int32)), lax.axis_index("front"), 0, keepdims=False
    )


class Spots:
    def __init__(self, nz):
        self.nz = nz
        group = NX * NC
        self.ring = nz * group
        self.blocks = self.ring + NX * nz
        self.near = self.blocks + nz
        self.core = self.near + group


def assemble(place, pieces, spots, whole):
    for piece, parts in zip(pieces, spots):
        rows = piece.shape[0] // len(parts)
        for i, spot in enumerate(parts):
            start = pl.multiple_of(place[spot] * rows, rows)
            whole[pl.ds(start, rows), :] = piece[i * rows : (i + 1) * rows, :]


def distribute(place, whole, keep, send):
    nz = len(keep)
    rows = keep[0].shape[1]
    for k in range(nz):
        for xr in range(NX):
            for cr, out in ((0, keep[k]), (1, send[k])):
                i = (k * NX + xr) * NC + cr
                out[xr] = whole[
                    pl.ds(pl.multiple_of(place[i] * rows, rows), rows), :
                ].astype(out.dtype)


def load_kernel(start, count, matrix, *refs):
    out, mark, arrived = refs[-3:]
    rows, width = out.shape
    height = rows // count
    copies = []
    for i in range(count):
        here = pl.ds(i * height, height)
        copies.append(
            pltpu.make_async_copy(
                matrix.at[here, pl.ds(start, width)], out.at[here, :], arrived.at[i]
            )
        )
    for copy in copies:
        copy.start()
    for copy in copies:
        copy.wait()
    mark[...] = jnp.zeros_like(mark)


def load_columns(matrix, part, parts, *others):
    rows, width = matrix.shape
    width //= parts
    count = max(p for p in range(1, 13) if rows % (16 * p) == 0)
    return pl.pallas_call(
        functools.partial(load_kernel, part * width, count),
        out_shape=(
            pltpu.VMEM((rows, width), matrix.dtype),
            jax.ShapeDtypeStruct((8, 128), F32),
        ),
        in_specs=[HBM] + [ANY] * len(others),
        out_specs=(VMEM, VMEM),
        scratch_shapes=[pltpu.SemaphoreType.DMA((count,))],
        compiler_params=pltpu.CompilerParams(vmem_limit_bytes=VMEM_LIMIT),
        cost_estimate=pl.CostEstimate(
            flops=0, bytes_accessed=4 * rows * width, transcendentals=0
        ),
        name="load_columns",
    )(in_hbm(matrix), *others)


def ahead_of(mark, *values):
    return lax.optimization_barrier((mark, *values))


def whole_kernel(spots, step, place, *refs):
    pieces, (matrix, _, out, out_b, cols) = refs[: len(spots)], refs[len(spots) :]
    assemble(place, pieces, spots, cols)
    total = None
    for start in range(0, cols.shape[0], step):
        here = slice(start, start + step)
        product = jnp.dot(matrix[:, here], cols[here, :], preferred_element_type=F32)
        total = product if total is None else total + product
    out[...] = total
    out_b[...] = total.astype(BF16)


def whole_product(place, pieces, matrix, mark, step):
    rows, width = matrix.shape
    n = pieces[0][0].shape[1]
    return pl.pallas_call(
        functools.partial(whole_kernel, [spots for _, spots in pieces], step),
        out_shape=(jax.ShapeDtypeStruct((rows, n), F32), jax.ShapeDtypeStruct((rows, n), BF16)),
        in_specs=[SMEM] + [VMEM] * (len(pieces) + 1) + [ANY],
        out_specs=(VMEM, VMEM),
        scratch_shapes=[pltpu.VMEM((width, n), BF16)],
        compiler_params=pltpu.CompilerParams(vmem_limit_bytes=VMEM_LIMIT),
        cost_estimate=pl.CostEstimate(
            flops=2 * rows * width * n, bytes_accessed=2 * rows * width, transcendentals=0
        ),
        name="whole_product",
    )(place, *[piece for piece, _ in pieces], in_vmem(matrix), mark)


def unit_kernel(blocks, spots, count, fresh, last, parts, place, *refs):
    units = len(blocks)
    pieces, refs = refs[: units * count], refs[units * count :]
    if not fresh:
        acc, refs = refs[0], refs[1:]
    matrix, refs = refs[:parts], refs[parts + 1 :]
    out, cols = refs[0], refs[-1]
    rows = pieces[0].shape[0]
    depth = cols.shape[1]
    for i, piece in enumerate(pieces):
        at = place[spots + i % count]
        cols[i // count, pl.ds(pl.multiple_of(at * rows, rows), rows), :] = piece[...]
    if not fresh:
        out[...] = acc[...]
    each = matrix[0].shape[1] // depth
    for u in range(units):
        index = place[blocks[u]]
        for part in range(parts):

            @pl.when(index // each == part)
            def _(u=u, part=part, index=index):
                here = pl.ds(pl.multiple_of(index % each * depth, 128), depth)
                product = jnp.dot(matrix[part][:, here], cols[u], preferred_element_type=F32)
                if fresh and u == 0:
                    out[...] = product
                else:
                    out[...] += product

    if last:
        refs[1][...] = out[...].astype(BF16)


def unit_product(place, blocks, spots, units, matrix, mark, acc, last):
    rows = matrix[0].shape[0]
    part, n = units[0][0].shape
    count = len(units[0])
    depth = count * part
    pieces = [piece for unit in units for piece in unit]
    start = [] if acc is None else [acc]
    return pl.pallas_call(
        functools.partial(
            unit_kernel, blocks, spots, count, acc is None, last, len(matrix)
        ),
        out_shape=[jax.ShapeDtypeStruct((rows, n), F32)]
        + [jax.ShapeDtypeStruct((rows, n), BF16)] * last,
        in_specs=[SMEM] + [VMEM] * (len(pieces) + len(start) + len(matrix)) + [ANY],
        out_specs=[VMEM] * (1 + last),
        scratch_shapes=[pltpu.VMEM((len(units), depth, n), BF16)],
        compiler_params=pltpu.CompilerParams(vmem_limit_bytes=VMEM_LIMIT),
        cost_estimate=pl.CostEstimate(
            flops=2 * rows * depth * n * len(units),
            bytes_accessed=2 * rows * depth * len(units),
            transcendentals=0,
        ),
        name="unit_product",
    )(place, *pieces, *start, *[in_vmem(m) for m in matrix], mark)


def backward_kernel(ks, at, count, parts, others, place, *refs):
    inputs, matrix = refs[:count], refs[count : count + parts]
    refs = refs[count + parts + others :]
    outs = refs[: 2 * len(ks)]
    whole = refs[-1]
    if count == 1:
        vector = inputs[0]
    else:
        vector = refs[2 * len(ks)]
        total = inputs[0][...] + inputs[1][...].astype(F32)
        if count == 3:
            total = inputs[2][...] - total
        vector[...] = total.T.astype(BF16)
    depth = whole.shape[0]
    half = depth // 2 if depth // 2 % 128 == 0 else depth
    each = matrix[0].shape[1] // depth
    for u, k in enumerate(ks):
        index = place[at.blocks + k]
        for part in range(parts):

            @pl.when(index // each == part)
            def _(part=part, index=index):
                for start in range(0, depth, half):
                    here = pl.ds(pl.multiple_of(index % each * depth + start, 128), half)
                    product = jnp.dot(
                        vector[...], matrix[part][:, here], preferred_element_type=F32
                    )
                    whole[start : start + half, :] = product.T

        part = outs[2 * u].shape[1]
        for xr in range(NX):
            for cr in range(NC):
                out = outs[2 * u + cr]
                spot = place[at.near + xr * NC + cr]
                out[xr] = whole[pl.ds(pl.multiple_of(spot * part, part), part), :].astype(out.dtype)


def backward_blocks(place, ks, inputs, others, matrix, nz):
    rows, width = matrix[0].shape
    width *= len(matrix)
    n = inputs[0].shape[0] if len(inputs) == 1 else inputs[0].shape[1]
    depth = width // nz
    part = depth // (NX * NC)
    fresh = len(inputs) > 1
    outs = pl.pallas_call(
        functools.partial(
            backward_kernel, ks, Spots(nz), len(inputs), len(matrix), len(others)
        ),
        out_shape=[
            jax.ShapeDtypeStruct((NX, part, n), F32),
            jax.ShapeDtypeStruct((NX, part, n), BF16),
        ]
        * len(ks)
        + [jax.ShapeDtypeStruct((n, rows), BF16)] * fresh,
        in_specs=[SMEM] + [VMEM] * (len(inputs) + len(matrix)) + [ANY] * len(others),
        out_specs=[VMEM] * (2 * len(ks) + fresh),
        scratch_shapes=[pltpu.VMEM((depth, n), F32)],
        compiler_params=pltpu.CompilerParams(vmem_limit_bytes=VMEM_LIMIT),
        cost_estimate=pl.CostEstimate(
            flops=2 * rows * depth * n * len(ks),
            bytes_accessed=2 * rows * depth * len(ks),
            transcendentals=0,
        ),
        name="backward_blocks",
    )(place, *inputs, *[in_vmem(m) for m in matrix], *others)
    pairs = {k: (outs[2 * u], outs[2 * u + 1]) for u, k in enumerate(ks)}
    return pairs, outs[-1] if fresh else inputs[0]


def product_scatter(place, inputs, matrix, groups, nz):
    keep, moved, across, left = {}, {}, {}, {}
    for g in range(len(groups) + 3):
        started = []
        for k in groups[g - 2] if 0 <= g - 2 < len(groups) else []:
            far = (keep[k][1] + moved[k][1].astype(F32)).astype(BF16)
            started.append(far)
            across[k] = x_swap(far, nz)
        for k in groups[g - 3] if 0 <= g - 3 < len(groups) else []:
            partial = keep[k][0] + moved[k][0].astype(F32) + across[k].astype(F32)
            if k:
                partial = partial.astype(BF16)
                started.append(partial)
                partial = z_shift(partial, k, nz).astype(F32)
            left[k] = partial
        if g < len(groups):
            pairs, vector = backward_blocks(place, groups[g], inputs, started, matrix, nz)
            inputs = [vector]
            for k, (mine, sent) in pairs.items():
                keep[k] = mine
                moved[k] = c_swap(sent, nz)
    total = left[0]
    for k in far_first(nz)[:-1]:
        total = total + left[k]
    return total


def push_kernel(nz, place, block, own, arrived, coupling, mark, *refs):
    total_out, keep, send, (whole,) = refs[0], refs[1 : nz + 1], refs[nz + 1 : 2 * nz + 1], refs[2 * nz + 1 :]
    total = own[...] + arrived[...].astype(F32)
    total_out[...] = total
    pushed = jnp.dot(total.T.astype(BF16), coupling[...], preferred_element_type=F32).T
    whole[...] = jnp.zeros_like(whole)
    for j in range(coupling.shape[1] // RB):
        start = pl.multiple_of(block[j] * RB, RB)
        whole[pl.ds(start, RB), :] = pushed[j * RB : (j + 1) * RB, :]
    distribute(place, whole, keep, send)


def push_product(place, block, own, arrived, coupling, mark, width, nz):
    n = own.shape[1]
    part = width // (nz * NX * NC)
    outs = pl.pallas_call(
        functools.partial(push_kernel, nz),
        out_shape=[jax.ShapeDtypeStruct(own.shape, F32)]
        + [jax.ShapeDtypeStruct((NX, part, n), F32)] * nz
        + [jax.ShapeDtypeStruct((NX, part, n), BF16)] * nz,
        in_specs=[SMEM, SMEM, VMEM, VMEM, VMEM, ANY],
        out_specs=[VMEM] * (2 * nz + 1),
        scratch_shapes=[pltpu.VMEM((width, n), F32)],
        compiler_params=pltpu.CompilerParams(vmem_limit_bytes=VMEM_LIMIT),
        name="push_product",
    )(place, block, own, arrived, coupling, mark)
    return outs[0], outs[1 : nz + 1], outs[nz + 1 :]


def pull_kernel(spots, place, block, *refs):
    pieces, (coupling, _, out, out_b, whole, picked) = refs[: len(spots)], refs[len(spots) :]
    assemble(place, pieces, spots, whole)
    for j in range(coupling.shape[1] // RB):
        start = pl.multiple_of(block[j] * RB, RB)
        picked[j * RB : (j + 1) * RB, :] = whole[pl.ds(start, RB), :]
    out[...] = jnp.dot(coupling[...], picked[...], preferred_element_type=F32)
    out_b[...] = out[...].astype(BF16)


def pull_product(place, block, pieces, coupling, mark, height):
    rows, width = coupling.shape
    n = pieces[0][0].shape[1]
    return pl.pallas_call(
        functools.partial(pull_kernel, [spots for _, spots in pieces]),
        out_shape=(
            jax.ShapeDtypeStruct((rows, n), F32),
            jax.ShapeDtypeStruct((rows, n), BF16),
        ),
        in_specs=[SMEM, SMEM] + [VMEM] * (len(pieces) + 1) + [ANY],
        out_specs=(VMEM, VMEM),
        scratch_shapes=[pltpu.VMEM((height, n), BF16), pltpu.VMEM((width, n), BF16)],
        compiler_params=pltpu.CompilerParams(vmem_limit_bytes=VMEM_LIMIT),
        name="pull_product",
    )(place, block, *[piece for piece, _ in pieces], coupling, mark)


def in_hbm(matrix):
    return pltpu.with_memory_space_constraint(matrix, pltpu.HBM)


def in_vmem(matrix):
    return pltpu.with_memory_space_constraint(matrix, pltpu.VMEM)


def two_level_body(rhs_root, rhs_level, root_inverse, level_inverse, coupling_t, coupling_rows):
    nz = lax.axis_size("front") // (NX * NC)
    width = root_inverse.shape[1]
    place = places(nz)
    block = coupling_rows[0] % (width // RB)

    level_vmem, mark = load_columns(level_inverse, 0, 1, place, block)
    pieces, mark = gather_pieces(rhs_level.astype(BF16), mark, nz)
    own, own_b = whole_product(place, pieces, level_vmem, mark, level_inverse.shape[1] // nz)
    arrived = sub_swap(own_b)
    left, mark = load_columns(root_inverse, 0, 2, own_b)
    forward_level, keep, send = push_product(
        place, block, own, arrived, coupling_t, mark, width, nz
    )
    halves = [left]

    def load(value):
        right, mark = load_columns(root_inverse, 1, 2, value)
        halves.append(right)
        return mark

    update, mark = scatter_sum(keep, send, load, nz)
    shifted = rhs_root - update

    own, own_b = ring_product(place, shifted.astype(BF16), halves, mark, nz)
    root_potential = product_scatter(
        place, [own, sub_swap(own_b)], halves, [[k] for k in far_first(nz)], nz
    )

    level_vmem, mark = load_columns(level_inverse, 0, 1, root_potential)
    pieces, mark = gather_pieces(root_potential.astype(BF16), mark, nz)
    own, own_b = pull_product(place, block, pieces, coupling_t, mark, width)
    far = far_first(nz)
    level_potential = product_scatter(
        place,
        [own, sub_swap(own_b), forward_level],
        [level_vmem],
        [far[: nz // 2], far[nz // 2 :]],
        nz,
    )
    return (root_potential, level_potential)


def body(rhs_root, rhs_level, root_inverse, level_inverse, coupling_t, coupling_rows):
    fits = (
        lax.axis_size("sub") == 2
        and lax.axis_size("front") % (2 * NX * NC) == 0
        and all(a.shape[0] % 16 == 0 for a in (rhs_root, rhs_level, root_inverse, level_inverse))
        and all(a.shape[1] % 128 == 0 for a in (rhs_root, root_inverse, level_inverse, coupling_t))
        and NC * rhs_root.shape[0] % 128 == 0
        and NX * NC * rhs_level.shape[0] % 128 == 0
        and (root_inverse.size + level_inverse.size) * 2 <= 40 * 1024 * 1024
        and root_inverse.shape[1] % (4 * rhs_root.shape[0] * NC) == 0
    )
    chosen = two_level_body if fits else general_body
    return chosen(rhs_root, rhs_level, root_inverse, level_inverse, coupling_t, coupling_rows)


def solution(mesh):
    return jax.shard_map(
        body,
        mesh=mesh,
        in_specs=(
            P(("sub", "front"), None),
            P(("sub", "front"), None),
            P("front", "sub"),
            P("front", "sub"),
            P("front", "sub"),
            P("front", "sub"),
        ),
        out_specs=(P(("sub", "front"), None), P(("sub", "front"), None)),
        check_vma=False,
    )
```

```python
import functools

import jax
import jax.numpy as jnp
import numpy as np
from jax import lax
from jax.experimental import pallas as pl
from jax.experimental.pallas import tpu as pltpu
from jax.sharding import PartitionSpec as P

RB = 128
NX = 2
NC = 2
F32 = jnp.float32
BF16 = jnp.bfloat16
HIGHEST_PRECISION = lax.Precision.HIGHEST
VMEM = pl.BlockSpec(memory_space=pltpu.VMEM)
SMEM = pl.BlockSpec(memory_space=pltpu.SMEM)
HBM = pl.BlockSpec(memory_space=pltpu.HBM)
ANY = pl.BlockSpec(memory_space=pl.ANY)
VMEM_LIMIT = 16 * 1024 * 1024


def transposed_product(matrix, vector):
    return lax.dot_general(
        matrix, vector, (((0,), (0,)), ((), ())), preferred_element_type=jnp.float32
    )


def gather_columns(pieces):
    return lax.all_gather(pieces, "front", axis=0, tiled=True)


def gather_rows(pieces):
    return lax.all_gather(pieces, "sub", axis=0, tiled=True)


def share_sub(summand):
    return lax.psum_scatter(
        summand.astype(jnp.bfloat16), "sub", scatter_dimension=0, tiled=True
    ).astype(jnp.float32)


def share_front(summand):
    return lax.psum_scatter(summand, "front", scatter_dimension=0, tiled=True)


def general_body(rhs_root, rhs_level, root_inverse, level_inverse, coupling_t, coupling_rows):
    rhs_count = rhs_root.shape[1]
    block_count = root_inverse.shape[1] // RB
    slot_count = coupling_t.shape[1] // RB
    level_cols = gather_columns(rhs_level.astype(jnp.bfloat16))
    forward_level = share_sub(
        jnp.dot(level_inverse, level_cols, preferred_element_type=jnp.float32)
    )
    level_rows = gather_rows(forward_level.astype(jnp.bfloat16))
    local_block = coupling_rows[0] % block_count
    selector = (
        lax.broadcasted_iota(jnp.int32, (block_count, slot_count), 0) == local_block[None, :]
    ).astype(jnp.float32)
    pushed = transposed_product(coupling_t, level_rows).reshape(slot_count, RB, rhs_count)
    update = jnp.einsum("bk,kin->bin", selector, pushed, precision=HIGHEST_PRECISION).reshape(
        block_count * RB, rhs_count
    )
    shifted = rhs_root - share_front(update)
    root_cols = gather_columns(shifted.astype(jnp.bfloat16))
    forward_root = share_sub(jnp.dot(root_inverse, root_cols, preferred_element_type=jnp.float32))
    root_rows = gather_rows(forward_root.astype(jnp.bfloat16))
    root_potential = share_front(transposed_product(root_inverse, root_rows))
    potential_cols = gather_columns(root_potential.astype(jnp.bfloat16))
    picked = potential_cols.reshape(block_count, RB, rhs_count)[local_block]
    pulled = jnp.dot(
        coupling_t, picked.reshape(slot_count * RB, rhs_count), preferred_element_type=jnp.float32
    )
    corrected = forward_level - share_sub(pulled)
    corrected_rows = gather_rows(corrected.astype(jnp.bfloat16))
    level_potential = share_front(transposed_product(level_inverse, corrected_rows))
    return (root_potential, level_potential)


def z_shift(value, shift, nz):
    width = NX * NC
    count = nz * width
    return lax.ppermute(
        value, "front", [(i, (i + shift * width) % count) for i in range(count)]
    )


def x_swap(value, nz):
    return lax.ppermute(value, "front", [(i, i ^ NC) for i in range(nz * NX * NC)])


def c_swap(value, nz):
    return lax.ppermute(value, "front", [(i, i ^ 1) for i in range(nz * NX * NC)])


def sub_swap(value):
    return lax.ppermute(value, "sub", [(0, 1), (1, 0)])


def gather_pieces(own, mark, nz):
    group = NX * NC
    order = near_first(nz)
    held = {0: own}
    for k in order[1:]:
        held[k] = z_shift(own, -k, nz)
    mark, *arrived = ahead_of(mark, *[held[k] for k in order[1:-1]])
    held.update(zip(order[1:-1], arrived))
    across = {}
    for k in order:
        across[k] = x_swap(held[k], nz)
    lanes = [(k * group, held[k]) for k in order], [(k * group + NC, across[k]) for k in order]
    pieces = lanes[0] + lanes[1]
    out = [(piece, [spot]) for spot, piece in pieces]
    batches = [list(pair) for pair in zip(*lanes)]
    for batch in batches[:-1] + [batches[-1][:1], batches[-1][1:]]:
        sent = [piece for _, piece in batch]
        sent = jnp.concatenate(sent) if len(sent) > 1 else sent[0]
        out.append((c_swap(sent, nz), [spot + 1 for spot, _ in batch]))
    return out, mark


def near_first(nz):
    return sorted(range(nz), key=lambda k: min(k, nz - k))


def ring_step(value, way, nz):
    count = NX * nz
    chip = lambda p: (p * NX if p < nz else (count - 1 - p) * NX + 1)
    pairs = [
        (chip(p) * NC + c, chip((p + way) % count) * NC + c)
        for p in range(count)
        for c in range(NC)
    ]
    return lax.ppermute(value, "front", pairs)


def ring_product(place, own, matrix, mark, nz):
    count = NX * nz
    at = Spots(nz)
    acc = None
    held = {0: own}
    for step in range(nz + 1):
        if step:
            acc, *arrived = ahead_of(acc, *held.values())
            held = dict(zip(held, arrived))
        following = {}
        if step < nz:
            following[(-step - 1) % count] = ring_step(held[(-step) % count], 1, nz)
            if step < nz - 1:
                following[step + 1] = ring_step(held[step], -1, nz)
        units = [[piece, c_swap(piece, nz)] for piece in held.values()]
        blocks = [at.ring + j for j in held]
        acc, *acc_b = unit_product(
            place, blocks, at.core, units, matrix, mark, acc, step == nz
        )
        held = following
    return acc, acc_b[0]


def far_first(nz):
    return near_first(nz)[::-1]


def scatter_sum(keep, send, load, nz):
    order = far_first(nz)
    moved = {k: c_swap(send[k], nz) for k in order}
    across, partial = {}, {}
    for k in order:
        far = (keep[k][1].astype(F32) + moved[k][1].astype(F32)).astype(BF16)
        across[k] = x_swap(far, nz)
    for k in order:
        partial[k] = keep[k][0].astype(F32) + moved[k][0].astype(F32) + across[k].astype(F32)
    total = partial[0]
    leaving = {k: partial[k].astype(BF16) for k in order[:-1]}
    mark = load(leaving[order[-2]])
    arrived = [z_shift(leaving[k], k, nz) for k in order[:-1]]
    mark, *arrived = ahead_of(mark, *arrived)
    for value in arrived:
        total = total + value.astype(F32)
    return total, mark


def places(nz):
    count = NX * nz
    table = []
    for me in range(count * NC):
        z, x, c = me // (NX * NC), (me // NC) % NX, me % NC
        near = [(x ^ xr) * NC + (c ^ cr) for xr in range(NX) for cr in range(NC)]
        blocks = [(z + k) % nz for k in range(nz)]
        row = [b * NX * NC + i for b in blocks for i in near]
        spot = z if x == 0 else count - 1 - z
        for j in range(count):
            p = (spot + j) % count
            row.append(p * NX if p < nz else (count - 1 - p) * NX + 1)
        table.append(row + blocks + near + [c, 1 - c])
    return lax.dynamic_index_in_dim(
        jnp.asarray(np.array(table, np.int32)), lax.axis_index("front"), 0, keepdims=False
    )


class Spots:
    def __init__(self, nz):
        self.nz = nz
        group = NX * NC
        self.ring = nz * group
        self.blocks = self.ring + NX * nz
        self.near = self.blocks + nz
        self.core = self.near + group


def assemble(place, pieces, spots, whole):
    for piece, parts in zip(pieces, spots):
        rows = piece.shape[0] // len(parts)
        for i, spot in enumerate(parts):
            start = pl.multiple_of(place[spot] * rows, rows)
            whole[pl.ds(start, rows), :] = piece[i * rows : (i + 1) * rows, :]


def distribute(place, whole, keep, send):
    nz = len(keep)
    rows = keep[0].shape[1]
    for k in range(nz):
        for xr in range(NX):
            for cr, out in ((0, keep[k]), (1, send[k])):
                i = (k * NX + xr) * NC + cr
                out[xr] = whole[
                    pl.ds(pl.multiple_of(place[i] * rows, rows), rows), :
                ].astype(out.dtype)


def load_kernel(start, count, matrix, *refs):
    out, mark, arrived = refs[-3:]
    rows, width = out.shape
    height = rows // count
    copies = []
    for i in range(count):
        here = pl.ds(i * height, height)
        copies.append(
            pltpu.make_async_copy(
                matrix.at[here, pl.ds(start, width)], out.at[here, :], arrived.at[i]
            )
        )
    for copy in copies:
        copy.start()
    for copy in copies:
        copy.wait()
    mark[...] = jnp.zeros_like(mark)


def load_columns(matrix, part, parts, *others):
    rows, width = matrix.shape
    width //= parts
    count = max(p for p in range(1, 13) if rows % (16 * p) == 0)
    return pl.pallas_call(
        functools.partial(load_kernel, part * width, count),
        out_shape=(
            pltpu.VMEM((rows, width), matrix.dtype),
            jax.ShapeDtypeStruct((8, 128), F32),
        ),
        in_specs=[HBM] + [ANY] * len(others),
        out_specs=(VMEM, VMEM),
        scratch_shapes=[pltpu.SemaphoreType.DMA((count,))],
        compiler_params=pltpu.CompilerParams(vmem_limit_bytes=VMEM_LIMIT),
        cost_estimate=pl.CostEstimate(
            flops=0, bytes_accessed=4 * rows * width, transcendentals=0
        ),
        name="load_columns",
    )(in_hbm(matrix), *others)


def ahead_of(mark, *values):
    return lax.optimization_barrier((mark, *values))


def whole_kernel(spots, step, place, *refs):
    pieces, (matrix, _, out, out_b, cols) = refs[: len(spots)], refs[len(spots) :]
    assemble(place, pieces, spots, cols)
    total = None
    for start in range(0, cols.shape[0], step):
        here = slice(start, start + step)
        product = jnp.dot(matrix[:, here], cols[here, :], preferred_element_type=F32)
        total = product if total is None else total + product
    out[...] = total
    out_b[...] = total.astype(BF16)


def whole_product(place, pieces, matrix, mark, step):
    rows, width = matrix.shape
    n = pieces[0][0].shape[1]
    return pl.pallas_call(
        functools.partial(whole_kernel, [spots for _, spots in pieces], step),
        out_shape=(jax.ShapeDtypeStruct((rows, n), F32), jax.ShapeDtypeStruct((rows, n), BF16)),
        in_specs=[SMEM] + [VMEM] * (len(pieces) + 1) + [ANY],
        out_specs=(VMEM, VMEM),
        scratch_shapes=[pltpu.VMEM((width, n), BF16)],
        compiler_params=pltpu.CompilerParams(vmem_limit_bytes=VMEM_LIMIT),
        cost_estimate=pl.CostEstimate(
            flops=2 * rows * width * n, bytes_accessed=2 * rows * width, transcendentals=0
        ),
        name="whole_product",
    )(place, *[piece for piece, _ in pieces], in_vmem(matrix), mark)


def unit_kernel(blocks, spots, count, fresh, last, parts, place, *refs):
    units = len(blocks)
    pieces, refs = refs[: units * count], refs[units * count :]
    if not fresh:
        acc, refs = refs[0], refs[1:]
    matrix, refs = refs[:parts], refs[parts + 1 :]
    out, cols = refs[0], refs[-1]
    rows = pieces[0].shape[0]
    depth = cols.shape[1]
    for i, piece in enumerate(pieces):
        at = place[spots + i % count]
        cols[i // count, pl.ds(pl.multiple_of(at * rows, rows), rows), :] = piece[...]
    if not fresh:
        out[...] = acc[...]
    each = matrix[0].shape[1] // depth
    for u in range(units):
        index = place[blocks[u]]
        for part in range(parts):

            @pl.when(index // each == part)
            def _(u=u, part=part, index=index):
                here = pl.ds(pl.multiple_of(index % each * depth, 128), depth)
                product = jnp.dot(matrix[part][:, here], cols[u], preferred_element_type=F32)
                if fresh and u == 0:
                    out[...] = product
                else:
                    out[...] += product

    if last:
        refs[1][...] = out[...].astype(BF16)


def unit_product(place, blocks, spots, units, matrix, mark, acc, last):
    rows = matrix[0].shape[0]
    part, n = units[0][0].shape
    count = len(units[0])
    depth = count * part
    pieces = [piece for unit in units for piece in unit]
    start = [] if acc is None else [acc]
    return pl.pallas_call(
        functools.partial(
            unit_kernel, blocks, spots, count, acc is None, last, len(matrix)
        ),
        out_shape=[jax.ShapeDtypeStruct((rows, n), F32)]
        + [jax.ShapeDtypeStruct((rows, n), BF16)] * last,
        in_specs=[SMEM] + [VMEM] * (len(pieces) + len(start) + len(matrix)) + [ANY],
        out_specs=[VMEM] * (1 + last),
        scratch_shapes=[pltpu.VMEM((len(units), depth, n), BF16)],
        compiler_params=pltpu.CompilerParams(vmem_limit_bytes=VMEM_LIMIT),
        cost_estimate=pl.CostEstimate(
            flops=2 * rows * depth * n * len(units),
            bytes_accessed=2 * rows * depth * len(units),
            transcendentals=0,
        ),
        name="unit_product",
    )(place, *pieces, *start, *[in_vmem(m) for m in matrix], mark)


def backward_kernel(ks, at, count, parts, others, place, *refs):
    inputs, matrix = refs[:count], refs[count : count + parts]
    refs = refs[count + parts + others :]
    outs = refs[: 2 * len(ks)]
    whole = refs[-1]
    if count == 1:
        vector = inputs[0]
    else:
        vector = refs[2 * len(ks)]
        total = inputs[0][...] + inputs[1][...].astype(F32)
        if count == 3:
            total = inputs[2][...] - total
        vector[...] = total.T.astype(BF16)
    depth = whole.shape[0]
    half = depth // 2 if depth // 2 % 128 == 0 else depth
    each = matrix[0].shape[1] // depth
    for u, k in enumerate(ks):
        index = place[at.blocks + k]
        for part in range(parts):

            @pl.when(index // each == part)
            def _(part=part, index=index):
                for start in range(0, depth, half):
                    here = pl.ds(pl.multiple_of(index % each * depth + start, 128), half)
                    product = jnp.dot(
                        vector[...], matrix[part][:, here], preferred_element_type=F32
                    )
                    whole[start : start + half, :] = product.T

        part = outs[2 * u].shape[1]
        for xr in range(NX):
            for cr in range(NC):
                out = outs[2 * u + cr]
                spot = place[at.near + xr * NC + cr]
                out[xr] = whole[pl.ds(pl.multiple_of(spot * part, part), part), :].astype(out.dtype)


def backward_blocks(place, ks, inputs, others, matrix, nz):
    rows, width = matrix[0].shape
    width *= len(matrix)
    n = inputs[0].shape[0] if len(inputs) == 1 else inputs[0].shape[1]
    depth = width // nz
    part = depth // (NX * NC)
    fresh = len(inputs) > 1
    outs = pl.pallas_call(
        functools.partial(
            backward_kernel, ks, Spots(nz), len(inputs), len(matrix), len(others)
        ),
        out_shape=[
            jax.ShapeDtypeStruct((NX, part, n), F32),
            jax.ShapeDtypeStruct((NX, part, n), BF16),
        ]
        * len(ks)
        + [jax.ShapeDtypeStruct((n, rows), BF16)] * fresh,
        in_specs=[SMEM] + [VMEM] * (len(inputs) + len(matrix)) + [ANY] * len(others),
        out_specs=[VMEM] * (2 * len(ks) + fresh),
        scratch_shapes=[pltpu.VMEM((depth, n), F32)],
        compiler_params=pltpu.CompilerParams(vmem_limit_bytes=VMEM_LIMIT),
        cost_estimate=pl.CostEstimate(
            flops=2 * rows * depth * n * len(ks),
            bytes_accessed=2 * rows * depth * len(ks),
            transcendentals=0,
        ),
        name="backward_blocks",
    )(place, *inputs, *[in_vmem(m) for m in matrix], *others)
    pairs = {k: (outs[2 * u], outs[2 * u + 1]) for u, k in enumerate(ks)}
    return pairs, outs[-1] if fresh else inputs[0]


def product_scatter(place, inputs, matrix, groups, nz):
    keep, moved, across, left = {}, {}, {}, {}

    def cross(group):
        for k in group:
            far = (keep[k][1] + moved[k][1].astype(F32)).astype(BF16)
            started.append(far)
            across[k] = x_swap(far, nz)

    def leave(group):
        for k in group:
            partial = keep[k][0] + moved[k][0].astype(F32) + across[k].astype(F32)
            if k:
                partial = partial.astype(BF16)
                started.append(partial)
                partial = z_shift(partial, k, nz).astype(F32)
            left[k] = partial

    count = len(groups)
    for g, group in enumerate(groups):
        started = []
        if g == count - 1:
            for later in groups[max(g - 2, 0) : g]:
                cross(later)
        elif g >= 2:
            cross(groups[g - 2])
        if g >= 3:
            leave(groups[g - 3])
        pairs, vector = backward_blocks(place, group, inputs, started, matrix, nz)
        inputs = [vector]
        for k, (mine, sent) in pairs.items():
            keep[k] = mine
            moved[k] = c_swap(sent, nz)
    started = []
    for later in groups[max(count - 4, 0) if count < 4 else count - 3 : count - 1]:
        leave(later)
    cross(groups[-1])
    leave(groups[-1])
    total = left[0]
    for k in far_first(nz)[:-1]:
        total = total + left[k]
    return total


def push_kernel(nz, place, block, own, arrived, coupling, mark, *refs):
    total_out, keep, send, (whole,) = refs[0], refs[1 : nz + 1], refs[nz + 1 : 2 * nz + 1], refs[2 * nz + 1 :]
    total = own[...] + arrived[...].astype(F32)
    total_out[...] = total
    pushed = jnp.dot(total.T.astype(BF16), coupling[...], preferred_element_type=F32).T
    whole[...] = jnp.zeros_like(whole)
    for j in range(coupling.shape[1] // RB):
        start = pl.multiple_of(block[j] * RB, RB)
        whole[pl.ds(start, RB), :] = pushed[j * RB : (j + 1) * RB, :]
    distribute(place, whole, keep, send)


def push_product(place, block, own, arrived, coupling, mark, width, nz):
    n = own.shape[1]
    part = width // (nz * NX * NC)
    outs = pl.pallas_call(
        functools.partial(push_kernel, nz),
        out_shape=[jax.ShapeDtypeStruct(own.shape, F32)]
        + [jax.ShapeDtypeStruct((NX, part, n), F32)] * nz
        + [jax.ShapeDtypeStruct((NX, part, n), BF16)] * nz,
        in_specs=[SMEM, SMEM, VMEM, VMEM, VMEM, ANY],
        out_specs=[VMEM] * (2 * nz + 1),
        scratch_shapes=[pltpu.VMEM((width, n), F32)],
        compiler_params=pltpu.CompilerParams(vmem_limit_bytes=VMEM_LIMIT),
        name="push_product",
    )(place, block, own, arrived, coupling, mark)
    return outs[0], outs[1 : nz + 1], outs[nz + 1 :]


def pull_kernel(spots, place, block, *refs):
    pieces, (coupling, _, out, out_b, whole, picked) = refs[: len(spots)], refs[len(spots) :]
    assemble(place, pieces, spots, whole)
    for j in range(coupling.shape[1] // RB):
        start = pl.multiple_of(block[j] * RB, RB)
        picked[j * RB : (j + 1) * RB, :] = whole[pl.ds(start, RB), :]
    out[...] = jnp.dot(coupling[...], picked[...], preferred_element_type=F32)
    out_b[...] = out[...].astype(BF16)


def pull_product(place, block, pieces, coupling, mark, height):
    rows, width = coupling.shape
    n = pieces[0][0].shape[1]
    return pl.pallas_call(
        functools.partial(pull_kernel, [spots for _, spots in pieces]),
        out_shape=(
            jax.ShapeDtypeStruct((rows, n), F32),
            jax.ShapeDtypeStruct((rows, n), BF16),
        ),
        in_specs=[SMEM, SMEM] + [VMEM] * (len(pieces) + 1) + [ANY],
        out_specs=(VMEM, VMEM),
        scratch_shapes=[pltpu.VMEM((height, n), BF16), pltpu.VMEM((width, n), BF16)],
        compiler_params=pltpu.CompilerParams(vmem_limit_bytes=VMEM_LIMIT),
        name="pull_product",
    )(place, block, *[piece for piece, _ in pieces], coupling, mark)


def in_hbm(matrix):
    return pltpu.with_memory_space_constraint(matrix, pltpu.HBM)


def in_vmem(matrix):
    return pltpu.with_memory_space_constraint(matrix, pltpu.VMEM)


def two_level_body(rhs_root, rhs_level, root_inverse, level_inverse, coupling_t, coupling_rows):
    nz = lax.axis_size("front") // (NX * NC)
    width = root_inverse.shape[1]
    place = places(nz)
    block = coupling_rows[0] % (width // RB)

    level_vmem, mark = load_columns(level_inverse, 0, 1, place, block)
    pieces, mark = gather_pieces(rhs_level.astype(BF16), mark, nz)
    own, own_b = whole_product(place, pieces, level_vmem, mark, level_inverse.shape[1] // nz)
    arrived = sub_swap(own_b)
    left, mark = load_columns(root_inverse, 0, 2, own_b)
    forward_level, keep, send = push_product(
        place, block, own, arrived, coupling_t, mark, width, nz
    )
    halves = [left]

    def load(value):
        right, mark = load_columns(root_inverse, 1, 2, value)
        halves.append(right)
        return mark

    update, mark = scatter_sum(keep, send, load, nz)
    shifted = rhs_root - update

    own, own_b = ring_product(place, shifted.astype(BF16), halves, mark, nz)
    root_potential = product_scatter(
        place, [own, sub_swap(own_b)], halves, [[k] for k in far_first(nz)], nz
    )

    level_vmem, mark = load_columns(level_inverse, 0, 1, root_potential)
    pieces, mark = gather_pieces(root_potential.astype(BF16), mark, nz)
    own, own_b = pull_product(place, block, pieces, coupling_t, mark, width)
    far = far_first(nz)
    level_potential = product_scatter(
        place,
        [own, sub_swap(own_b), forward_level],
        [level_vmem],
        [far[: nz // 2], far[nz // 2 : -1], far[-1:]],
        nz,
    )
    return (root_potential, level_potential)


def body(rhs_root, rhs_level, root_inverse, level_inverse, coupling_t, coupling_rows):
    fits = (
        lax.axis_size("sub") == 2
        and lax.axis_size("front") % (2 * NX * NC) == 0
        and all(a.shape[0] % 16 == 0 for a in (rhs_root, rhs_level, root_inverse, level_inverse))
        and all(a.shape[1] % 128 == 0 for a in (rhs_root, root_inverse, level_inverse, coupling_t))
        and NC * rhs_root.shape[0] % 128 == 0
        and NX * NC * rhs_level.shape[0] % 128 == 0
        and (root_inverse.size + level_inverse.size) * 2 <= 40 * 1024 * 1024
        and root_inverse.shape[1] % (4 * rhs_root.shape[0] * NC) == 0
    )
    chosen = two_level_body if fits else general_body
    return chosen(rhs_root, rhs_level, root_inverse, level_inverse, coupling_t, coupling_rows)


def solution(mesh):
    return jax.shard_map(
        body,
        mesh=mesh,
        in_specs=(
            P(("sub", "front"), None),
            P(("sub", "front"), None),
            P("front", "sub"),
            P("front", "sub"),
            P("front", "sub"),
            P("front", "sub"),
        ),
        out_specs=(P(("sub", "front"), None), P(("sub", "front"), None)),
        check_vma=False,
    )
```

```python
import functools

import jax
import jax.numpy as jnp
import numpy as np
from jax import lax
from jax.experimental import pallas as pl
from jax.experimental.pallas import tpu as pltpu
from jax.sharding import PartitionSpec as P

RB = 128
NX = 2
NC = 2
F32 = jnp.float32
BF16 = jnp.bfloat16
HIGHEST_PRECISION = lax.Precision.HIGHEST
VMEM = pl.BlockSpec(memory_space=pltpu.VMEM)
SMEM = pl.BlockSpec(memory_space=pltpu.SMEM)
HBM = pl.BlockSpec(memory_space=pltpu.HBM)
ANY = pl.BlockSpec(memory_space=pl.ANY)
VMEM_LIMIT = 16 * 1024 * 1024


def transposed_product(matrix, vector):
    return lax.dot_general(
        matrix, vector, (((0,), (0,)), ((), ())), preferred_element_type=jnp.float32
    )


def gather_columns(pieces):
    return lax.all_gather(pieces, "front", axis=0, tiled=True)


def gather_rows(pieces):
    return lax.all_gather(pieces, "sub", axis=0, tiled=True)


def share_sub(summand):
    return lax.psum_scatter(
        summand.astype(jnp.bfloat16), "sub", scatter_dimension=0, tiled=True
    ).astype(jnp.float32)


def share_front(summand):
    return lax.psum_scatter(summand, "front", scatter_dimension=0, tiled=True)


def general_body(rhs_root, rhs_level, root_inverse, level_inverse, coupling_t, coupling_rows):
    rhs_count = rhs_root.shape[1]
    block_count = root_inverse.shape[1] // RB
    slot_count = coupling_t.shape[1] // RB
    level_cols = gather_columns(rhs_level.astype(jnp.bfloat16))
    forward_level = share_sub(
        jnp.dot(level_inverse, level_cols, preferred_element_type=jnp.float32)
    )
    level_rows = gather_rows(forward_level.astype(jnp.bfloat16))
    local_block = coupling_rows[0] % block_count
    selector = (
        lax.broadcasted_iota(jnp.int32, (block_count, slot_count), 0) == local_block[None, :]
    ).astype(jnp.float32)
    pushed = transposed_product(coupling_t, level_rows).reshape(slot_count, RB, rhs_count)
    update = jnp.einsum("bk,kin->bin", selector, pushed, precision=HIGHEST_PRECISION).reshape(
        block_count * RB, rhs_count
    )
    shifted = rhs_root - share_front(update)
    root_cols = gather_columns(shifted.astype(jnp.bfloat16))
    forward_root = share_sub(jnp.dot(root_inverse, root_cols, preferred_element_type=jnp.float32))
    root_rows = gather_rows(forward_root.astype(jnp.bfloat16))
    root_potential = share_front(transposed_product(root_inverse, root_rows))
    potential_cols = gather_columns(root_potential.astype(jnp.bfloat16))
    picked = potential_cols.reshape(block_count, RB, rhs_count)[local_block]
    pulled = jnp.dot(
        coupling_t, picked.reshape(slot_count * RB, rhs_count), preferred_element_type=jnp.float32
    )
    corrected = forward_level - share_sub(pulled)
    corrected_rows = gather_rows(corrected.astype(jnp.bfloat16))
    level_potential = share_front(transposed_product(level_inverse, corrected_rows))
    return (root_potential, level_potential)


def z_shift(value, shift, nz):
    width = NX * NC
    count = nz * width
    return lax.ppermute(
        value, "front", [(i, (i + shift * width) % count) for i in range(count)]
    )


def x_swap(value, nz):
    return lax.ppermute(value, "front", [(i, i ^ NC) for i in range(nz * NX * NC)])


def c_swap(value, nz):
    return lax.ppermute(value, "front", [(i, i ^ 1) for i in range(nz * NX * NC)])


def sub_swap(value):
    return lax.ppermute(value, "sub", [(0, 1), (1, 0)])


def gather_pieces(own, mark, nz, ready=None):
    group = NX * NC
    order = near_first(nz)
    held = {0: own}
    for k in order[1:]:
        held[k] = z_shift(own, -k, nz)
    out = [(own, [0])]
    if ready:
        out.append((c_swap(own, nz), [1]))
        arrived = ready(0, out, *[held[k] for k in order[1:-1]])
    else:
        mark, *arrived = ahead_of(mark, *[held[k] for k in order[1:-1]])
    held.update(zip(order[1:-1], arrived))
    for k in order:
        spot = k * group
        across = x_swap(held[k], nz)
        out.append((across, [spot + NC]))
        if k == order[-1]:
            out += [(held[k], [spot]), (c_swap(held[k], nz), [spot + 1])]
            if ready:
                across, = ready(1, out, across)
            out.append((c_swap(across, nz), [spot + NC + 1]))
        elif ready and k == 0:
            out.append((c_swap(across, nz), [spot + NC + 1]))
        else:
            both = c_swap(jnp.concatenate([held[k], across]), nz)
            out.append((both, [spot + 1, spot + NC + 1]))
            if k:
                out.append((held[k], [spot]))
    return out, mark


def near_first(nz):
    return sorted(range(nz), key=lambda k: min(k, nz - k))


def gather_product(place, own, matrix, mark, calls, size, between, nz):
    acc, acc_b, token = None, [], mark
    left = list(calls)

    def multiply(pieces):
        nonlocal acc, acc_b
        units = left.pop(0)
        used = [(piece, spots) for piece, spots in pieces if spots[0] // size in units]
        acc, *acc_b = unit_product(
            place, units, used, size, matrix, token, acc, not left, nz
        )

    def ready(stage, pieces, *values):
        nonlocal acc
        for _ in range(between[stage]):
            multiply(pieces)
        acc, *values = ahead_of(acc, *values)
        return values

    pieces, token = gather_pieces(own, mark, nz, ready if between else None)
    while left:
        multiply(pieces)
    return acc, acc_b[0]


def far_first(nz):
    return near_first(nz)[::-1]


def scatter_sum(keep, send, load, nz):
    order = far_first(nz)
    moved = {k: c_swap(send[k], nz) for k in order}
    across, partial = {}, {}
    for k in order:
        far = (keep[k][1].astype(F32) + moved[k][1].astype(F32)).astype(BF16)
        across[k] = x_swap(far, nz)
    for k in order:
        partial[k] = keep[k][0].astype(F32) + moved[k][0].astype(F32) + across[k].astype(F32)
    total = partial[0]
    leaving = {k: partial[k].astype(BF16) for k in order[:-1]}
    mark = load(leaving[order[-2]])
    arrived = [z_shift(leaving[k], k, nz) for k in order[:-1]]
    mark, *arrived = ahead_of(mark, *arrived)
    for value in arrived:
        total = total + value.astype(F32)
    return total, mark


def places(nz):
    table = []
    for me in range(nz * NX * NC):
        z, x, c = me // (NX * NC), (me // NC) % NX, me % NC
        near = [(x ^ xr) * NC + (c ^ cr) for xr in range(NX) for cr in range(NC)]
        blocks = [(z + k) % nz for k in range(nz)]
        row = [b * NX * NC + i for b in blocks for i in near]
        pairs = [b * NX + (x ^ xr) for b in blocks for xr in range(NX)]
        table.append(row + blocks + near + [c, 1 - c] + pairs)
    return lax.dynamic_index_in_dim(
        jnp.asarray(np.array(table, np.int32)), lax.axis_index("front"), 0, keepdims=False
    )


class Spots:
    def __init__(self, nz):
        self.nz = nz
        group = NX * NC
        self.blocks = nz * group
        self.near = self.blocks + nz
        self.core = self.near + group
        self.pairs = self.core + NC


def assemble(place, pieces, spots, whole):
    for piece, parts in zip(pieces, spots):
        rows = piece.shape[0] // len(parts)
        for i, spot in enumerate(parts):
            start = pl.multiple_of(place[spot] * rows, rows)
            whole[pl.ds(start, rows), :] = piece[i * rows : (i + 1) * rows, :]


def distribute(place, whole, keep, send):
    nz = len(keep)
    rows = keep[0].shape[1]
    for k in range(nz):
        for xr in range(NX):
            for cr, out in ((0, keep[k]), (1, send[k])):
                i = (k * NX + xr) * NC + cr
                out[xr] = whole[
                    pl.ds(pl.multiple_of(place[i] * rows, rows), rows), :
                ].astype(out.dtype)


def load_kernel(start, count, matrix, *refs):
    out, mark, arrived = refs[-3:]
    rows, width = out.shape
    height = rows // count
    copies = []
    for i in range(count):
        here = pl.ds(i * height, height)
        copies.append(
            pltpu.make_async_copy(
                matrix.at[here, pl.ds(start, width)], out.at[here, :], arrived.at[i]
            )
        )
    for copy in copies:
        copy.start()
    for copy in copies:
        copy.wait()
    mark[...] = jnp.zeros_like(mark)


def load_columns(matrix, part, parts, *others):
    rows, width = matrix.shape
    width //= parts
    count = max(p for p in range(1, 13) if rows % (16 * p) == 0)
    return pl.pallas_call(
        functools.partial(load_kernel, part * width, count),
        out_shape=(
            pltpu.VMEM((rows, width), matrix.dtype),
            jax.ShapeDtypeStruct((8, 128), F32),
        ),
        in_specs=[HBM] + [ANY] * len(others),
        out_specs=(VMEM, VMEM),
        scratch_shapes=[pltpu.SemaphoreType.DMA((count,))],
        compiler_params=pltpu.CompilerParams(vmem_limit_bytes=VMEM_LIMIT),
        cost_estimate=pl.CostEstimate(
            flops=0, bytes_accessed=4 * rows * width, transcendentals=0
        ),
        name="load_columns",
    )(in_hbm(matrix), *others)


def ahead_of(mark, *values):
    return lax.optimization_barrier((mark, *values))


def unit_kernel(units, spots, size, at, fresh, last, parts, place, *refs):
    pieces, refs = refs[: len(spots)], refs[len(spots) :]
    if not fresh:
        acc, refs = refs[0], refs[1:]
    matrix, refs = refs[:parts], refs[parts + 1 :]
    out, cols = refs[0], refs[-1]
    depth = cols.shape[1]
    rows = depth // size
    first, inside = (at.pairs, at.core) if size == NC else (at.blocks, at.near)
    for piece, places_of in zip(pieces, spots):
        for i, spot in enumerate(places_of):
            start = pl.multiple_of(place[inside + spot % size] * rows, rows)
            cols[units.index(spot // size), pl.ds(start, rows), :] = piece[
                i * rows : (i + 1) * rows, :
            ]
    if not fresh:
        out[...] = acc[...]
    each = matrix[0].shape[1] // depth
    for u, unit in enumerate(units):
        index = place[first + unit]
        for part in range(parts):

            @pl.when(index // each == part)
            def _(u=u, part=part, index=index):
                here = pl.ds(pl.multiple_of(index % each * depth, 128), depth)
                product = jnp.dot(matrix[part][:, here], cols[u], preferred_element_type=F32)
                if fresh and u == 0:
                    out[...] = product
                else:
                    out[...] += product

    if last:
        refs[1][...] = out[...].astype(BF16)


def unit_product(place, units, pieces, size, matrix, mark, acc, last, nz):
    rows = matrix[0].shape[0]
    n = pieces[0][0].shape[1]
    depth = size * pieces[0][0].shape[0] // len(pieces[0][1])
    start = [] if acc is None else [acc]
    return pl.pallas_call(
        functools.partial(
            unit_kernel,
            units,
            [spots for _, spots in pieces],
            size,
            Spots(nz),
            acc is None,
            last,
            len(matrix),
        ),
        out_shape=[
            jax.ShapeDtypeStruct((rows, n), F32),
        ]
        + [jax.ShapeDtypeStruct((rows, n), BF16)] * last,
        in_specs=[SMEM] + [VMEM] * (len(pieces) + len(start) + len(matrix)) + [ANY],
        out_specs=[VMEM] * (1 + last),
        scratch_shapes=[pltpu.VMEM((len(units), depth, n), BF16)],
        compiler_params=pltpu.CompilerParams(vmem_limit_bytes=VMEM_LIMIT),
        cost_estimate=pl.CostEstimate(flops=0, bytes_accessed=0, transcendentals=0),
        name="unit_product",
    )(place, *[piece for piece, _ in pieces], *start, *[in_vmem(m) for m in matrix], mark)


def backward_kernel(ks, at, count, parts, others, place, *refs):
    inputs, matrix = refs[:count], refs[count : count + parts]
    refs = refs[count + parts + others :]
    outs = refs[: 2 * len(ks)]
    whole = refs[-1]
    if count == 1:
        vector = inputs[0]
    else:
        vector = refs[2 * len(ks)]
        total = inputs[0][...] + inputs[1][...].astype(F32)
        if count == 3:
            total = inputs[2][...] - total
        vector[...] = total.T.astype(BF16)
    depth = whole.shape[0]
    half = depth // 2 if depth // 2 % 128 == 0 else depth
    each = matrix[0].shape[1] // depth
    for u, k in enumerate(ks):
        index = place[at.blocks + k]
        for part in range(parts):

            @pl.when(index // each == part)
            def _(part=part, index=index):
                for start in range(0, depth, half):
                    here = pl.ds(pl.multiple_of(index % each * depth + start, 128), half)
                    product = jnp.dot(
                        vector[...], matrix[part][:, here], preferred_element_type=F32
                    )
                    whole[start : start + half, :] = product.T

        part = outs[2 * u].shape[1]
        for xr in range(NX):
            for cr in range(NC):
                out = outs[2 * u + cr]
                spot = place[at.near + xr * NC + cr]
                out[xr] = whole[pl.ds(pl.multiple_of(spot * part, part), part), :].astype(out.dtype)


def backward_blocks(place, ks, inputs, others, matrix, nz):
    rows, width = matrix[0].shape
    width *= len(matrix)
    n = inputs[0].shape[0] if len(inputs) == 1 else inputs[0].shape[1]
    depth = width // nz
    part = depth // (NX * NC)
    fresh = len(inputs) > 1
    outs = pl.pallas_call(
        functools.partial(
            backward_kernel, ks, Spots(nz), len(inputs), len(matrix), len(others)
        ),
        out_shape=[
            jax.ShapeDtypeStruct((NX, part, n), F32),
            jax.ShapeDtypeStruct((NX, part, n), BF16),
        ]
        * len(ks)
        + [jax.ShapeDtypeStruct((n, rows), BF16)] * fresh,
        in_specs=[SMEM] + [VMEM] * (len(inputs) + len(matrix)) + [ANY] * len(others),
        out_specs=[VMEM] * (2 * len(ks) + fresh),
        scratch_shapes=[pltpu.VMEM((depth, n), F32)],
        compiler_params=pltpu.CompilerParams(vmem_limit_bytes=VMEM_LIMIT),
        cost_estimate=pl.CostEstimate(
            flops=2 * rows * depth * n * len(ks),
            bytes_accessed=2 * rows * depth * len(ks),
            transcendentals=0,
        ),
        name="backward_blocks",
    )(place, *inputs, *[in_vmem(m) for m in matrix], *others)
    pairs = {k: (outs[2 * u], outs[2 * u + 1]) for u, k in enumerate(ks)}
    return pairs, outs[-1] if fresh else inputs[0]


def product_scatter(place, inputs, matrix, groups, nz):
    keep, moved, across, left = {}, {}, {}, {}

    def cross(group):
        for k in group:
            far = (keep[k][1] + moved[k][1].astype(F32)).astype(BF16)
            started.append(far)
            across[k] = x_swap(far, nz)

    def leave(group):
        for k in group:
            partial = keep[k][0] + moved[k][0].astype(F32) + across[k].astype(F32)
            if k:
                partial = partial.astype(BF16)
                started.append(partial)
                partial = z_shift(partial, k, nz).astype(F32)
            left[k] = partial

    count = len(groups)
    for g, group in enumerate(groups):
        started = []
        if g == count - 1:
            for later in groups[max(g - 2, 0) : g]:
                cross(later)
        elif g >= 2:
            cross(groups[g - 2])
        if g >= 3:
            leave(groups[g - 3])
        pairs, vector = backward_blocks(place, group, inputs, started, matrix, nz)
        inputs = [vector]
        for k, (mine, sent) in pairs.items():
            keep[k] = mine
            moved[k] = c_swap(sent, nz)
    started = []
    for later in groups[max(count - 4, 0) if count < 4 else count - 3 : count - 1]:
        leave(later)
    cross(groups[-1])
    leave(groups[-1])
    total = left[0]
    for k in far_first(nz)[:-1]:
        total = total + left[k]
    return total


def push_kernel(nz, place, block, own, arrived, coupling, mark, *refs):
    total_out, keep, send, (whole,) = refs[0], refs[1 : nz + 1], refs[nz + 1 : 2 * nz + 1], refs[2 * nz + 1 :]
    total = own[...] + arrived[...].astype(F32)
    total_out[...] = total
    pushed = jnp.dot(total.T.astype(BF16), coupling[...], preferred_element_type=F32).T
    whole[...] = jnp.zeros_like(whole)
    for j in range(coupling.shape[1] // RB):
        start = pl.multiple_of(block[j] * RB, RB)
        whole[pl.ds(start, RB), :] = pushed[j * RB : (j + 1) * RB, :]
    distribute(place, whole, keep, send)


def push_product(place, block, own, arrived, coupling, mark, width, nz):
    n = own.shape[1]
    part = width // (nz * NX * NC)
    outs = pl.pallas_call(
        functools.partial(push_kernel, nz),
        out_shape=[jax.ShapeDtypeStruct(own.shape, F32)]
        + [jax.ShapeDtypeStruct((NX, part, n), F32)] * nz
        + [jax.ShapeDtypeStruct((NX, part, n), BF16)] * nz,
        in_specs=[SMEM, SMEM, VMEM, VMEM, VMEM, ANY],
        out_specs=[VMEM] * (2 * nz + 1),
        scratch_shapes=[pltpu.VMEM((width, n), F32)],
        compiler_params=pltpu.CompilerParams(vmem_limit_bytes=VMEM_LIMIT),
        name="push_product",
    )(place, block, own, arrived, coupling, mark)
    return outs[0], outs[1 : nz + 1], outs[nz + 1 :]


def pull_kernel(spots, place, block, *refs):
    pieces, (coupling, _, out, out_b, whole, picked) = refs[: len(spots)], refs[len(spots) :]
    assemble(place, pieces, spots, whole)
    for j in range(coupling.shape[1] // RB):
        start = pl.multiple_of(block[j] * RB, RB)
        picked[j * RB : (j + 1) * RB, :] = whole[pl.ds(start, RB), :]
    out[...] = jnp.dot(coupling[...], picked[...], preferred_element_type=F32)
    out_b[...] = out[...].astype(BF16)


def pull_product(place, block, pieces, coupling, mark, height):
    rows, width = coupling.shape
    n = pieces[0][0].shape[1]
    return pl.pallas_call(
        functools.partial(pull_kernel, [spots for _, spots in pieces]),
        out_shape=(
            jax.ShapeDtypeStruct((rows, n), F32),
            jax.ShapeDtypeStruct((rows, n), BF16),
        ),
        in_specs=[SMEM, SMEM] + [VMEM] * (len(pieces) + 1) + [ANY],
        out_specs=(VMEM, VMEM),
        scratch_shapes=[pltpu.VMEM((height, n), BF16), pltpu.VMEM((width, n), BF16)],
        compiler_params=pltpu.CompilerParams(vmem_limit_bytes=VMEM_LIMIT),
        name="pull_product",
    )(place, block, *[piece for piece, _ in pieces], coupling, mark)


def in_hbm(matrix):
    return pltpu.with_memory_space_constraint(matrix, pltpu.HBM)


def in_vmem(matrix):
    return pltpu.with_memory_space_constraint(matrix, pltpu.VMEM)


def two_level_body(rhs_root, rhs_level, root_inverse, level_inverse, coupling_t, coupling_rows):
    nz = lax.axis_size("front") // (NX * NC)
    width = root_inverse.shape[1]
    place = places(nz)
    block = coupling_rows[0] % (width // RB)

    level_vmem, mark = load_columns(level_inverse, 0, 1, place, block)
    order = near_first(nz)
    calls = [order[:-1], order[-1:]]
    own, own_b = gather_product(
        place, rhs_level.astype(BF16), [level_vmem], mark, calls, NX * NC, (), nz
    )
    arrived = sub_swap(own_b)
    left, mark = load_columns(root_inverse, 0, 2, own_b)
    forward_level, keep, send = push_product(
        place, block, own, arrived, coupling_t, mark, width, nz
    )
    halves = [left]

    def load(value):
        right, mark = load_columns(root_inverse, 1, 2, value)
        halves.append(right)
        return mark

    update, mark = scatter_sum(keep, send, load, nz)
    shifted = rhs_root - update

    units = [k * NX + xr for k in order for xr in range(NX)]
    calls = [units[:1], units[1 : NX * 2], units[-2:-1], units[NX * 2 : -2], units[-1:]]
    own, own_b = gather_product(
        place, shifted.astype(BF16), halves, mark, calls, NC, (1, 2), nz
    )
    root_potential = product_scatter(
        place, [own, sub_swap(own_b)], halves, [[k] for k in far_first(nz)], nz
    )

    level_vmem, mark = load_columns(level_inverse, 0, 1, root_potential)
    pieces, mark = gather_pieces(root_potential.astype(BF16), mark, nz)
    own, own_b = pull_product(place, block, pieces, coupling_t, mark, width)
    far = far_first(nz)
    level_potential = product_scatter(
        place,
        [own, sub_swap(own_b), forward_level],
        [level_vmem],
        [far[: nz // 2], far[nz // 2 : -1], far[-1:]],
        nz,
    )
    return (root_potential, level_potential)


def body(rhs_root, rhs_level, root_inverse, level_inverse, coupling_t, coupling_rows):
    fits = (
        lax.axis_size("sub") == 2
        and lax.axis_size("front") % (NX * NC) == 0
        and lax.axis_size("front") >= 3 * NX * NC
        and all(a.shape[0] % 16 == 0 for a in (rhs_root, rhs_level, root_inverse, level_inverse))
        and all(a.shape[1] % 128 == 0 for a in (rhs_root, root_inverse, level_inverse, coupling_t))
        and NC * rhs_root.shape[0] % 128 == 0
        and NX * NC * rhs_level.shape[0] % 128 == 0
        and (root_inverse.size + level_inverse.size) * 2 <= 40 * 1024 * 1024
        and root_inverse.shape[1] % (4 * rhs_root.shape[0] * NC) == 0
    )
    chosen = two_level_body if fits else general_body
    return chosen(rhs_root, rhs_level, root_inverse, level_inverse, coupling_t, coupling_rows)


def solution(mesh):
    return jax.shard_map(
        body,
        mesh=mesh,
        in_specs=(
            P(("sub", "front"), None),
            P(("sub", "front"), None),
            P("front", "sub"),
            P("front", "sub"),
            P("front", "sub"),
            P("front", "sub"),
        ),
        out_specs=(P(("sub", "front"), None), P(("sub", "front"), None)),
        check_vma=False,
    )
```

```python
import functools

import jax
import jax.numpy as jnp
import numpy as np
from jax import lax
from jax.experimental import pallas as pl
from jax.experimental.pallas import tpu as pltpu
from jax.sharding import PartitionSpec as P

RB = 128
NX = 2
NC = 2
F32 = jnp.float32
BF16 = jnp.bfloat16
HIGHEST_PRECISION = lax.Precision.HIGHEST
VMEM = pl.BlockSpec(memory_space=pltpu.VMEM)
SMEM = pl.BlockSpec(memory_space=pltpu.SMEM)
HBM = pl.BlockSpec(memory_space=pltpu.HBM)
ANY = pl.BlockSpec(memory_space=pl.ANY)
VMEM_LIMIT = 16 * 1024 * 1024


def transposed_product(matrix, vector):
    return lax.dot_general(
        matrix, vector, (((0,), (0,)), ((), ())), preferred_element_type=jnp.float32
    )


def gather_columns(pieces):
    return lax.all_gather(pieces, "front", axis=0, tiled=True)


def gather_rows(pieces):
    return lax.all_gather(pieces, "sub", axis=0, tiled=True)


def share_sub(summand):
    return lax.psum_scatter(
        summand.astype(jnp.bfloat16), "sub", scatter_dimension=0, tiled=True
    ).astype(jnp.float32)


def share_front(summand):
    return lax.psum_scatter(summand, "front", scatter_dimension=0, tiled=True)


def general_body(rhs_root, rhs_level, root_inverse, level_inverse, coupling_t, coupling_rows):
    rhs_count = rhs_root.shape[1]
    block_count = root_inverse.shape[1] // RB
    slot_count = coupling_t.shape[1] // RB
    level_cols = gather_columns(rhs_level.astype(jnp.bfloat16))
    forward_level = share_sub(
        jnp.dot(level_inverse, level_cols, preferred_element_type=jnp.float32)
    )
    level_rows = gather_rows(forward_level.astype(jnp.bfloat16))
    local_block = coupling_rows[0] % block_count
    selector = (
        lax.broadcasted_iota(jnp.int32, (block_count, slot_count), 0) == local_block[None, :]
    ).astype(jnp.float32)
    pushed = transposed_product(coupling_t, level_rows).reshape(slot_count, RB, rhs_count)
    update = jnp.einsum("bk,kin->bin", selector, pushed, precision=HIGHEST_PRECISION).reshape(
        block_count * RB, rhs_count
    )
    shifted = rhs_root - share_front(update)
    root_cols = gather_columns(shifted.astype(jnp.bfloat16))
    forward_root = share_sub(jnp.dot(root_inverse, root_cols, preferred_element_type=jnp.float32))
    root_rows = gather_rows(forward_root.astype(jnp.bfloat16))
    root_potential = share_front(transposed_product(root_inverse, root_rows))
    potential_cols = gather_columns(root_potential.astype(jnp.bfloat16))
    picked = potential_cols.reshape(block_count, RB, rhs_count)[local_block]
    pulled = jnp.dot(
        coupling_t, picked.reshape(slot_count * RB, rhs_count), preferred_element_type=jnp.float32
    )
    corrected = forward_level - share_sub(pulled)
    corrected_rows = gather_rows(corrected.astype(jnp.bfloat16))
    level_potential = share_front(transposed_product(level_inverse, corrected_rows))
    return (root_potential, level_potential)


def z_shift(value, shift, nz):
    width = NX * NC
    count = nz * width
    return lax.ppermute(
        value, "front", [(i, (i + shift * width) % count) for i in range(count)]
    )


def x_swap(value, nz):
    return lax.ppermute(value, "front", [(i, i ^ NC) for i in range(nz * NX * NC)])


def c_swap(value, nz):
    return lax.ppermute(value, "front", [(i, i ^ 1) for i in range(nz * NX * NC)])


def sub_swap(value):
    return lax.ppermute(value, "sub", [(0, 1), (1, 0)])


def gather_pieces(own, mark, nz):
    group = NX * NC
    order = near_first(nz)
    held = {0: own}
    for k in order[1:]:
        held[k] = z_shift(own, -k, nz)
    mark, *arrived = ahead_of(mark, *[held[k] for k in order[1:-1]])
    held.update(zip(order[1:-1], arrived))
    across = {}
    for k in order:
        across[k] = x_swap(held[k], nz)
    lanes = [(k * group, held[k]) for k in order], [(k * group + NC, across[k]) for k in order]
    pieces = lanes[0] + lanes[1]
    out = [(piece, [spot]) for spot, piece in pieces]
    batches = [list(pair) for pair in zip(*lanes)]
    for batch in batches[:-1] + [batches[-1][:1], batches[-1][1:]]:
        sent = [piece for _, piece in batch]
        sent = jnp.concatenate(sent) if len(sent) > 1 else sent[0]
        out.append((c_swap(sent, nz), [spot + 1 for spot, _ in batch]))
    return out, mark


def near_first(nz):
    return sorted(range(nz), key=lambda k: min(k, nz - k))


def ring_step(value, way, nz):
    count = NX * nz
    chip = lambda p: (p * NX if p < nz else (count - 1 - p) * NX + 1)
    pairs = [
        (chip(p) * NC + c, chip((p + way) % count) * NC + c)
        for p in range(count)
        for c in range(NC)
    ]
    return lax.ppermute(value, "front", pairs)


def ring_product(place, own, matrix, mark, nz):
    count = NX * nz
    at = Spots(nz)
    acc, acc_b, waiting = None, [], None
    held = {0: own}

    def multiply(units, last=False):
        nonlocal acc, acc_b
        blocks = [at.ring + j for j in units]
        pieces = list(units.values())
        acc, *acc_b = unit_product(place, blocks, at.core, pieces, matrix, mark, acc, last)

    for step in range(nz + 1):
        if step > 1:
            acc, *arrived = ahead_of(acc, *held.values())
            held = dict(zip(held, arrived))
        following = {}
        if step < nz:
            following[(-step - 1) % count] = ring_step(held[(-step) % count], 1, nz)
            if step < nz - 1:
                following[step + 1] = ring_step(held[step], -1, nz)
        units = {j: [piece, c_swap(piece, nz)] for j, piece in held.items()}
        if waiting:
            multiply(waiting)
        waiting, held = units, following
    multiply(waiting, True)
    return acc, acc_b[0]


def far_first(nz):
    return near_first(nz)[::-1]


def scatter_sum(keep, send, load, nz):
    order = far_first(nz)
    moved = {k: c_swap(send[k], nz) for k in order}
    across, partial = {}, {}
    for k in order:
        far = (keep[k][1].astype(F32) + moved[k][1].astype(F32)).astype(BF16)
        across[k] = x_swap(far, nz)
    for k in order:
        partial[k] = keep[k][0].astype(F32) + moved[k][0].astype(F32) + across[k].astype(F32)
    total = partial[0]
    leaving = {k: partial[k].astype(BF16) for k in order[:-1]}
    mark = load(leaving[order[-2]])
    arrived = [z_shift(leaving[k], k, nz) for k in order[:-1]]
    mark, *arrived = ahead_of(mark, *arrived)
    for value in arrived:
        total = total + value.astype(F32)
    return total, mark


def places(nz):
    count = NX * nz
    table = []
    for me in range(count * NC):
        z, x, c = me // (NX * NC), (me // NC) % NX, me % NC
        near = [(x ^ xr) * NC + (c ^ cr) for xr in range(NX) for cr in range(NC)]
        blocks = [(z + k) % nz for k in range(nz)]
        row = [b * NX * NC + i for b in blocks for i in near]
        spot = z if x == 0 else count - 1 - z
        for j in range(count):
            p = (spot + j) % count
            row.append(p * NX if p < nz else (count - 1 - p) * NX + 1)
        pairs = [b * NX + (x ^ xr) for b in blocks for xr in range(NX)]
        table.append(row + blocks + near + [c, 1 - c] + pairs)
    return lax.dynamic_index_in_dim(
        jnp.asarray(np.array(table, np.int32)), lax.axis_index("front"), 0, keepdims=False
    )


class Spots:
    def __init__(self, nz):
        self.nz = nz
        group = NX * NC
        self.ring = nz * group
        self.blocks = self.ring + NX * nz
        self.near = self.blocks + nz
        self.core = self.near + group
        self.pairs = self.core + NC


def assemble(place, pieces, spots, whole):
    for piece, parts in zip(pieces, spots):
        rows = piece.shape[0] // len(parts)
        for i, spot in enumerate(parts):
            start = pl.multiple_of(place[spot] * rows, rows)
            whole[pl.ds(start, rows), :] = piece[i * rows : (i + 1) * rows, :]


def distribute(place, whole, keep, send):
    nz = len(keep)
    rows = keep[0].shape[1]
    for k in range(nz):
        for xr in range(NX):
            for cr, out in ((0, keep[k]), (1, send[k])):
                i = (k * NX + xr) * NC + cr
                out[xr] = whole[
                    pl.ds(pl.multiple_of(place[i] * rows, rows), rows), :
                ].astype(out.dtype)


def load_kernel(start, count, matrix, *refs):
    out, mark, arrived = refs[-3:]
    rows, width = out.shape
    height = rows // count
    copies = []
    for i in range(count):
        here = pl.ds(i * height, height)
        copies.append(
            pltpu.make_async_copy(
                matrix.at[here, pl.ds(start, width)], out.at[here, :], arrived.at[i]
            )
        )
    for copy in copies:
        copy.start()
    for copy in copies:
        copy.wait()
    mark[...] = jnp.zeros_like(mark)


def load_columns(matrix, part, parts, *others):
    rows, width = matrix.shape
    width //= parts
    count = max(p for p in range(1, 13) if rows % (16 * p) == 0)
    return pl.pallas_call(
        functools.partial(load_kernel, part * width, count),
        out_shape=(
            pltpu.VMEM((rows, width), matrix.dtype),
            jax.ShapeDtypeStruct((8, 128), F32),
        ),
        in_specs=[HBM] + [ANY] * len(others),
        out_specs=(VMEM, VMEM),
        scratch_shapes=[pltpu.SemaphoreType.DMA((count,))],
        compiler_params=pltpu.CompilerParams(vmem_limit_bytes=VMEM_LIMIT),
        cost_estimate=pl.CostEstimate(
            flops=0, bytes_accessed=4 * rows * width, transcendentals=0
        ),
        name="load_columns",
    )(in_hbm(matrix), *others)


def ahead_of(mark, *values):
    return lax.optimization_barrier((mark, *values))


def whole_kernel(spots, step, place, *refs):
    pieces, (matrix, _, out, out_b, cols) = refs[: len(spots)], refs[len(spots) :]
    assemble(place, pieces, spots, cols)
    total = None
    for start in range(0, cols.shape[0], step):
        here = slice(start, start + step)
        product = jnp.dot(matrix[:, here], cols[here, :], preferred_element_type=F32)
        total = product if total is None else total + product
    out[...] = total
    out_b[...] = total.astype(BF16)


def whole_product(place, pieces, matrix, mark, step):
    rows, width = matrix.shape
    n = pieces[0][0].shape[1]
    return pl.pallas_call(
        functools.partial(whole_kernel, [spots for _, spots in pieces], step),
        out_shape=(jax.ShapeDtypeStruct((rows, n), F32), jax.ShapeDtypeStruct((rows, n), BF16)),
        in_specs=[SMEM] + [VMEM] * (len(pieces) + 1) + [ANY],
        out_specs=(VMEM, VMEM),
        scratch_shapes=[pltpu.VMEM((width, n), BF16)],
        compiler_params=pltpu.CompilerParams(vmem_limit_bytes=VMEM_LIMIT),
        cost_estimate=pl.CostEstimate(
            flops=2 * rows * width * n, bytes_accessed=2 * rows * width, transcendentals=0
        ),
        name="whole_product",
    )(place, *[piece for piece, _ in pieces], in_vmem(matrix), mark)


def unit_kernel(blocks, spots, count, fresh, last, parts, place, *refs):
    units = len(blocks)
    pieces, refs = refs[: units * count], refs[units * count :]
    if not fresh:
        acc, refs = refs[0], refs[1:]
    matrix, refs = refs[:parts], refs[parts + 1 :]
    out, cols = refs[0], refs[-1]
    rows = pieces[0].shape[0]
    depth = cols.shape[1]
    for i, piece in enumerate(pieces):
        at = place[spots + i % count]
        cols[i // count, pl.ds(pl.multiple_of(at * rows, rows), rows), :] = piece[...]
    if not fresh:
        out[...] = acc[...]
    each = matrix[0].shape[1] // depth
    for u in range(units):
        index = place[blocks[u]]
        for part in range(parts):

            @pl.when(index // each == part)
            def _(u=u, part=part, index=index):
                here = pl.ds(pl.multiple_of(index % each * depth, 128), depth)
                product = jnp.dot(matrix[part][:, here], cols[u], preferred_element_type=F32)
                if fresh and u == 0:
                    out[...] = product
                else:
                    out[...] += product

    if last:
        refs[1][...] = out[...].astype(BF16)


def unit_product(place, blocks, spots, units, matrix, mark, acc, last):
    rows = matrix[0].shape[0]
    part, n = units[0][0].shape
    count = len(units[0])
    depth = count * part
    pieces = [piece for unit in units for piece in unit]
    start = [] if acc is None else [acc]
    return pl.pallas_call(
        functools.partial(
            unit_kernel, blocks, spots, count, acc is None, last, len(matrix)
        ),
        out_shape=[jax.ShapeDtypeStruct((rows, n), F32)]
        + [jax.ShapeDtypeStruct((rows, n), BF16)] * last,
        in_specs=[SMEM] + [VMEM] * (len(pieces) + len(start) + len(matrix)) + [ANY],
        out_specs=[VMEM] * (1 + last),
        scratch_shapes=[pltpu.VMEM((len(units), depth, n), BF16)],
        compiler_params=pltpu.CompilerParams(vmem_limit_bytes=VMEM_LIMIT),
        cost_estimate=pl.CostEstimate(
            flops=2 * rows * depth * n * len(units),
            bytes_accessed=2 * rows * depth * len(units),
            transcendentals=0,
        ),
        name="unit_product",
    )(place, *pieces, *start, *[in_vmem(m) for m in matrix], mark)


def backward_kernel(units, size, at, count, parts, others, place, *refs):
    inputs, matrix = refs[:count], refs[count : count + parts]
    refs = refs[count + parts + others :]
    width = size // NC + 1
    outs = refs[: width * len(units)]
    whole = refs[-1]
    if count == 1:
        vector = inputs[0]
    else:
        vector = refs[width * len(units)]
        total = inputs[0][...] + inputs[1][...].astype(F32)
        if count == 3:
            total = inputs[2][...] - total
        vector[...] = total.T.astype(BF16)
    depth = whole.shape[0]
    rows = depth // size
    each = matrix[0].shape[1] // depth
    first, inside = (at.pairs, at.core) if size == NC else (at.blocks, at.near)
    for u, unit in enumerate(units):
        index = place[first + unit]
        for part in range(parts):

            @pl.when(index // each == part)
            def _(part=part, index=index):
                here = pl.ds(pl.multiple_of(index % each * depth, 128), depth)
                product = jnp.dot(
                    vector[...], matrix[part][:, here], preferred_element_type=F32
                )
                whole[...] = product.T

        *keep, send = outs[width * u : width * (u + 1)]
        for i in range(size):
            start = pl.multiple_of(place[inside + i] * rows, rows)
            piece = whole[pl.ds(start, rows), :]
            if i % NC:
                send[i // NC * rows : (i // NC + 1) * rows, :] = piece.astype(BF16)
            else:
                keep[i // NC][...] = piece


def backward_blocks(place, units, size, inputs, others, matrix, nz):
    rows, width = matrix[0].shape
    n = inputs[0].shape[0] if len(inputs) == 1 else inputs[0].shape[1]
    part = width * len(matrix) // (nz * NX * NC)
    fresh = len(inputs) > 1
    outs = pl.pallas_call(
        functools.partial(
            backward_kernel, units, size, Spots(nz), len(inputs), len(matrix), len(others)
        ),
        out_shape=(
            [jax.ShapeDtypeStruct((part, n), F32)] * (size // NC)
            + [jax.ShapeDtypeStruct((size // NC * part, n), BF16)]
        )
        * len(units)
        + [jax.ShapeDtypeStruct((n, rows), BF16)] * fresh,
        in_specs=[SMEM] + [VMEM] * (len(inputs) + len(matrix)) + [ANY] * len(others),
        out_specs=[VMEM] * ((size // NC + 1) * len(units) + fresh),
        scratch_shapes=[pltpu.VMEM((size * part, n), F32)],
        compiler_params=pltpu.CompilerParams(vmem_limit_bytes=VMEM_LIMIT),
        cost_estimate=pl.CostEstimate(
            flops=2 * rows * size * part * n * len(units),
            bytes_accessed=2 * rows * size * part * len(units),
            transcendentals=0,
        ),
        name="backward_blocks",
    )(place, *inputs, *[in_vmem(m) for m in matrix], *others)
    each = size // NC + 1
    made = {unit: outs[each * u : each * (u + 1)] for u, unit in enumerate(units)}
    return made, outs[-1] if fresh else inputs[0]


def product_scatter(place, inputs, matrix, groups, size, nz):
    group = NX * NC
    pieces, moved, across, left = {}, {}, {}, {}

    def cross(k):
        spot = k * group + NC
        far = (pieces[spot] + moved[spot].astype(F32)).astype(BF16)
        started.append(far)
        across[k] = x_swap(far, nz)

    def leave(k):
        spot = k * group
        partial = pieces[spot] + moved[spot].astype(F32) + across[k].astype(F32)
        if k:
            partial = partial.astype(BF16)
            started.append(partial)
            partial = z_shift(partial, k, nz).astype(F32)
        left[k] = partial

    for units, crossing, leaving in groups:
        started = []
        for k in crossing:
            cross(k)
        for k in leaving:
            leave(k)
        made, vector = backward_blocks(place, units, size, inputs, started, matrix, nz)
        inputs = [vector]
        for unit, (*kept, send) in made.items():
            arrived = c_swap(send, nz)
            part = kept[0].shape[0]
            for i, piece in enumerate(kept):
                pieces[unit * size + i * NC] = piece
                moved[unit * size + i * NC] = arrived[i * part : (i + 1) * part]
    started = []
    for k in far_first(nz):
        if k not in across:
            cross(k)
    for k in far_first(nz):
        if k not in left:
            leave(k)
    total = left[0]
    for k in far_first(nz)[:-1]:
        total = total + left[k]
    return total


def push_kernel(nz, place, block, own, arrived, coupling, mark, *refs):
    total_out, keep, send, (whole,) = refs[0], refs[1 : nz + 1], refs[nz + 1 : 2 * nz + 1], refs[2 * nz + 1 :]
    total = own[...] + arrived[...].astype(F32)
    total_out[...] = total
    pushed = jnp.dot(total.T.astype(BF16), coupling[...], preferred_element_type=F32).T
    whole[...] = jnp.zeros_like(whole)
    for j in range(coupling.shape[1] // RB):
        start = pl.multiple_of(block[j] * RB, RB)
        whole[pl.ds(start, RB), :] = pushed[j * RB : (j + 1) * RB, :]
    distribute(place, whole, keep, send)


def push_product(place, block, own, arrived, coupling, mark, width, nz):
    n = own.shape[1]
    part = width // (nz * NX * NC)
    outs = pl.pallas_call(
        functools.partial(push_kernel, nz),
        out_shape=[jax.ShapeDtypeStruct(own.shape, F32)]
        + [jax.ShapeDtypeStruct((NX, part, n), F32)] * nz
        + [jax.ShapeDtypeStruct((NX, part, n), BF16)] * nz,
        in_specs=[SMEM, SMEM, VMEM, VMEM, VMEM, ANY],
        out_specs=[VMEM] * (2 * nz + 1),
        scratch_shapes=[pltpu.VMEM((width, n), F32)],
        compiler_params=pltpu.CompilerParams(vmem_limit_bytes=VMEM_LIMIT),
        name="push_product",
    )(place, block, own, arrived, coupling, mark)
    return outs[0], outs[1 : nz + 1], outs[nz + 1 :]


def pull_kernel(spots, place, block, *refs):
    pieces, (coupling, _, out, out_b, whole, picked) = refs[: len(spots)], refs[len(spots) :]
    assemble(place, pieces, spots, whole)
    for j in range(coupling.shape[1] // RB):
        start = pl.multiple_of(block[j] * RB, RB)
        picked[j * RB : (j + 1) * RB, :] = whole[pl.ds(start, RB), :]
    out[...] = jnp.dot(coupling[...], picked[...], preferred_element_type=F32)
    out_b[...] = out[...].astype(BF16)


def pull_product(place, block, pieces, coupling, mark, height):
    rows, width = coupling.shape
    n = pieces[0][0].shape[1]
    return pl.pallas_call(
        functools.partial(pull_kernel, [spots for _, spots in pieces]),
        out_shape=(
            jax.ShapeDtypeStruct((rows, n), F32),
            jax.ShapeDtypeStruct((rows, n), BF16),
        ),
        in_specs=[SMEM, SMEM] + [VMEM] * (len(pieces) + 1) + [ANY],
        out_specs=(VMEM, VMEM),
        scratch_shapes=[pltpu.VMEM((height, n), BF16), pltpu.VMEM((width, n), BF16)],
        compiler_params=pltpu.CompilerParams(vmem_limit_bytes=VMEM_LIMIT),
        name="pull_product",
    )(place, block, *[piece for piece, _ in pieces], coupling, mark)


def in_hbm(matrix):
    return pltpu.with_memory_space_constraint(matrix, pltpu.HBM)


def in_vmem(matrix):
    return pltpu.with_memory_space_constraint(matrix, pltpu.VMEM)


def two_level_body(rhs_root, rhs_level, root_inverse, level_inverse, coupling_t, coupling_rows):
    nz = lax.axis_size("front") // (NX * NC)
    width = root_inverse.shape[1]
    place = places(nz)
    block = coupling_rows[0] % (width // RB)

    level_vmem, mark = load_columns(level_inverse, 0, 1, place, block)
    pieces, mark = gather_pieces(rhs_level.astype(BF16), mark, nz)
    own, own_b = whole_product(place, pieces, level_vmem, mark, level_inverse.shape[1] // nz)
    arrived = sub_swap(own_b)
    left, mark = load_columns(root_inverse, 0, 2, own_b)
    forward_level, keep, send = push_product(
        place, block, own, arrived, coupling_t, mark, width, nz
    )
    halves = [left]

    def load(value):
        right, mark = load_columns(root_inverse, 1, 2, value)
        halves.append(right)
        return mark

    update, mark = scatter_sum(keep, send, load, nz)
    shifted = rhs_root - update

    own, own_b = ring_product(place, shifted.astype(BF16), halves, mark, nz)
    far = far_first(nz)
    most, mid, mine = far[0], far[1:-1], far[-1]
    pair = lambda k, xr: k * NX + xr
    groups = [([pair(most, 1)], [], []), ([pair(most, 0), pair(mid[0], 1)], [], [])]
    groups += [([pair(k, 1) for k in mid[1:]] + [pair(mid[0], 0)], [most], [])]
    groups += [([pair(k, 0) for k in mid[1:]], mid[:1], [])]
    groups += [([pair(mine, 1), pair(mine, 0)], mid[1:], [most])]
    root_potential = product_scatter(
        place, [own, sub_swap(own_b)], halves, groups, NC, nz
    )

    level_vmem, mark = load_columns(level_inverse, 0, 1, root_potential)
    pieces, mark = gather_pieces(root_potential.astype(BF16), mark, nz)
    own, own_b = pull_product(place, block, pieces, coupling_t, mark, width)
    groups = [([most], [], []), (mid, [], []), ([mine], far[:-1], [])]
    level_potential = product_scatter(
        place, [own, sub_swap(own_b), forward_level], [level_vmem], groups, NX * NC, nz
    )
    return (root_potential, level_potential)


def body(rhs_root, rhs_level, root_inverse, level_inverse, coupling_t, coupling_rows):
    fits = (
        lax.axis_size("sub") == 2
        and lax.axis_size("front") % (NX * NC) == 0
        and lax.axis_size("front") >= 3 * NX * NC
        and all(a.shape[0] % 16 == 0 for a in (rhs_root, rhs_level, root_inverse, level_inverse))
        and all(a.shape[1] % 128 == 0 for a in (rhs_root, root_inverse, level_inverse, coupling_t))
        and NC * rhs_root.shape[0] % 128 == 0
        and NX * NC * rhs_level.shape[0] % 128 == 0
        and (root_inverse.size + level_inverse.size) * 2 <= 40 * 1024 * 1024
        and root_inverse.shape[1] % (4 * rhs_root.shape[0] * NC) == 0
    )
    chosen = two_level_body if fits else general_body
    return chosen(rhs_root, rhs_level, root_inverse, level_inverse, coupling_t, coupling_rows)


def solution(mesh):
    return jax.shard_map(
        body,
        mesh=mesh,
        in_specs=(
            P(("sub", "front"), None),
            P(("sub", "front"), None),
            P("front", "sub"),
            P("front", "sub"),
            P("front", "sub"),
            P("front", "sub"),
        ),
        out_specs=(P(("sub", "front"), None), P(("sub", "front"), None)),
        check_vma=False,
    )
```

```python
import functools

import jax
import jax.numpy as jnp
import numpy as np
from jax import lax
from jax.experimental import pallas as pl
from jax.experimental.pallas import tpu as pltpu
from jax.sharding import PartitionSpec as P

RB = 128
NX = 2
NC = 2
F32 = jnp.float32
BF16 = jnp.bfloat16
HIGHEST_PRECISION = lax.Precision.HIGHEST
VMEM = pl.BlockSpec(memory_space=pltpu.VMEM)
SMEM = pl.BlockSpec(memory_space=pltpu.SMEM)
HBM = pl.BlockSpec(memory_space=pltpu.HBM)
ANY = pl.BlockSpec(memory_space=pl.ANY)
VMEM_LIMIT = 15 * 1024 * 1024
LESS_VMEM = 8 * 1024 * 1024


def transposed_product(matrix, vector):
    return lax.dot_general(
        matrix, vector, (((0,), (0,)), ((), ())), preferred_element_type=jnp.float32
    )


def gather_columns(pieces):
    return lax.all_gather(pieces, "front", axis=0, tiled=True)


def gather_rows(pieces):
    return lax.all_gather(pieces, "sub", axis=0, tiled=True)


def share_sub(summand):
    return lax.psum_scatter(
        summand.astype(jnp.bfloat16), "sub", scatter_dimension=0, tiled=True
    ).astype(jnp.float32)


def share_front(summand):
    return lax.psum_scatter(summand, "front", scatter_dimension=0, tiled=True)


def general_body(rhs_root, rhs_level, root_inverse, level_inverse, coupling_t, coupling_rows):
    rhs_count = rhs_root.shape[1]
    block_count = root_inverse.shape[1] // RB
    slot_count = coupling_t.shape[1] // RB
    level_cols = gather_columns(rhs_level.astype(jnp.bfloat16))
    forward_level = share_sub(
        jnp.dot(level_inverse, level_cols, preferred_element_type=jnp.float32)
    )
    level_rows = gather_rows(forward_level.astype(jnp.bfloat16))
    local_block = coupling_rows[0] % block_count
    selector = (
        lax.broadcasted_iota(jnp.int32, (block_count, slot_count), 0) == local_block[None, :]
    ).astype(jnp.float32)
    pushed = transposed_product(coupling_t, level_rows).reshape(slot_count, RB, rhs_count)
    update = jnp.einsum("bk,kin->bin", selector, pushed, precision=HIGHEST_PRECISION).reshape(
        block_count * RB, rhs_count
    )
    shifted = rhs_root - share_front(update)
    root_cols = gather_columns(shifted.astype(jnp.bfloat16))
    forward_root = share_sub(jnp.dot(root_inverse, root_cols, preferred_element_type=jnp.float32))
    root_rows = gather_rows(forward_root.astype(jnp.bfloat16))
    root_potential = share_front(transposed_product(root_inverse, root_rows))
    potential_cols = gather_columns(root_potential.astype(jnp.bfloat16))
    picked = potential_cols.reshape(block_count, RB, rhs_count)[local_block]
    pulled = jnp.dot(
        coupling_t, picked.reshape(slot_count * RB, rhs_count), preferred_element_type=jnp.float32
    )
    corrected = forward_level - share_sub(pulled)
    corrected_rows = gather_rows(corrected.astype(jnp.bfloat16))
    level_potential = share_front(transposed_product(level_inverse, corrected_rows))
    return (root_potential, level_potential)


def z_shift(value, shift, nz):
    width = NX * NC
    count = nz * width
    return lax.ppermute(
        value, "front", [(i, (i + shift * width) % count) for i in range(count)]
    )


def x_swap(value, nz):
    return lax.ppermute(value, "front", [(i, i ^ NC) for i in range(nz * NX * NC)])


def c_swap(value, nz):
    return lax.ppermute(value, "front", [(i, i ^ 1) for i in range(nz * NX * NC)])


def sub_swap(value):
    return lax.ppermute(value, "sub", [(0, 1), (1, 0)])


def gather_pieces(own, mark, nz):
    group = NX * NC
    order = near_first(nz)
    held = {0: own}
    for k in order[1:]:
        held[k] = z_shift(own, -k, nz)
    mark, *arrived = ahead_of(mark, *[held[k] for k in order[1:-1]])
    held.update(zip(order[1:-1], arrived))
    across = {}
    for k in order:
        across[k] = x_swap(held[k], nz)
    lanes = [(k * group, held[k]) for k in order], [(k * group + NC, across[k]) for k in order]
    pieces = lanes[0] + lanes[1]
    out = [(piece, [spot]) for spot, piece in pieces]
    batches = [list(pair) for pair in zip(*lanes)]
    for batch in batches[:-1] + [batches[-1][:1], batches[-1][1:]]:
        sent = [piece for _, piece in batch]
        sent = jnp.concatenate(sent) if len(sent) > 1 else sent[0]
        out.append((c_swap(sent, nz), [spot + 1 for spot, _ in batch]))
    return out, mark


def near_first(nz):
    return sorted(range(nz), key=lambda k: min(k, nz - k))


def ring_step(value, way, nz):
    count = NX * nz
    chip = lambda p: (p * NX if p < nz else (count - 1 - p) * NX + 1)
    pairs = [
        (chip(p) * NC + c, chip((p + way) % count) * NC + c)
        for p in range(count)
        for c in range(NC)
    ]
    return lax.ppermute(value, "front", pairs)


def ring_product(place, own, matrix, ranges, mark, nz):
    count = NX * nz
    at = Spots(nz)
    accs, waiting = [], None
    held = {0: own}

    def multiply(units, accs, ranges, last=False):
        blocks = [at.ring + j for j in units]
        pieces = list(units.values())
        return unit_product(place, blocks, at.core, pieces, matrix, mark, accs, ranges, last)

    for step in range(nz + 1):
        if step > 1:
            first, *arrived = ahead_of(accs[0], *held.values())
            accs = [first, *accs[1:]]
            held = dict(zip(held, arrived))
        following = {}
        if step < nz:
            following[(-step - 1) % count] = ring_step(held[(-step) % count], 1, nz)
            if step < nz - 1:
                following[step + 1] = ring_step(held[step], -1, nz)
        units = {j: [piece, c_swap(piece, nz)] for j, piece in held.items()}
        if waiting:
            accs, _ = multiply(waiting, accs, ranges)
        waiting, held = units, following
    outs = [
        multiply(waiting, [acc], [rows], True) for acc, rows in zip(accs, ranges)
    ]
    return [own for (own,), _ in outs], [own_b for _, (own_b,) in outs]


def far_first(nz):
    return near_first(nz)[::-1]


def scatter_sum(keep, send, load, nz):
    order = far_first(nz)
    moved = {k: c_swap(send[k], nz) for k in order}
    across, partial = {}, {}
    for k in order:
        far = (keep[k][1].astype(F32) + moved[k][1].astype(F32)).astype(BF16)
        across[k] = x_swap(far, nz)
    for k in order:
        partial[k] = keep[k][0].astype(F32) + moved[k][0].astype(F32) + across[k].astype(F32)
    total = partial[0]
    leaving = {k: partial[k].astype(BF16) for k in order[:-1]}
    mark = load(leaving[order[-2]])
    arrived = [z_shift(leaving[k], k, nz) for k in order[:-1]]
    mark, *arrived = ahead_of(mark, *arrived)
    for value in arrived:
        total = total + value.astype(F32)
    return total, mark


def places(nz):
    count = NX * nz
    table = []
    for me in range(count * NC):
        z, x, c = me // (NX * NC), (me // NC) % NX, me % NC
        near = [(x ^ xr) * NC + (c ^ cr) for xr in range(NX) for cr in range(NC)]
        blocks = [(z + k) % nz for k in range(nz)]
        row = [b * NX * NC + i for b in blocks for i in near]
        spot = z if x == 0 else count - 1 - z
        for j in range(count):
            p = (spot + j) % count
            row.append(p * NX if p < nz else (count - 1 - p) * NX + 1)
        pairs = [b * NX + (x ^ xr) for b in blocks for xr in range(NX)]
        table.append(row + blocks + near + [c, 1 - c] + pairs)
    return lax.dynamic_index_in_dim(
        jnp.asarray(np.array(table, np.int32)), lax.axis_index("front"), 0, keepdims=False
    )


class Spots:
    def __init__(self, nz):
        self.nz = nz
        group = NX * NC
        self.ring = nz * group
        self.blocks = self.ring + NX * nz
        self.near = self.blocks + nz
        self.core = self.near + group
        self.pairs = self.core + NC


def assemble(place, pieces, spots, whole):
    for piece, parts in zip(pieces, spots):
        rows = piece.shape[0] // len(parts)
        for i, spot in enumerate(parts):
            start = pl.multiple_of(place[spot] * rows, rows)
            whole[pl.ds(start, rows), :] = piece[i * rows : (i + 1) * rows, :]


def distribute(place, whole, keep, send):
    nz = len(keep)
    rows = keep[0].shape[1]
    for k in range(nz):
        for xr in range(NX):
            for cr, out in ((0, keep[k]), (1, send[k])):
                i = (k * NX + xr) * NC + cr
                out[xr] = whole[
                    pl.ds(pl.multiple_of(place[i] * rows, rows), rows), :
                ].astype(out.dtype)


def load_kernel(start, count, matrix, *refs):
    out, mark, arrived = refs[-3:]
    rows, width = out.shape
    height = rows // count
    copies = []
    for i in range(count):
        here = pl.ds(i * height, height)
        copies.append(
            pltpu.make_async_copy(
                matrix.at[here, pl.ds(start, width)], out.at[here, :], arrived.at[i]
            )
        )
    for copy in copies:
        copy.start()
    for copy in copies:
        copy.wait()
    mark[...] = jnp.zeros_like(mark)


def load_columns(matrix, part, parts, *others):
    rows, width = matrix.shape
    width //= parts
    count = max(p for p in range(1, 13) if rows % (16 * p) == 0)
    return pl.pallas_call(
        functools.partial(load_kernel, part * width, count),
        out_shape=(
            pltpu.VMEM((rows, width), matrix.dtype),
            jax.ShapeDtypeStruct((8, 128), F32),
        ),
        in_specs=[HBM] + [ANY] * len(others),
        out_specs=(VMEM, VMEM),
        scratch_shapes=[pltpu.SemaphoreType.DMA((count,))],
        compiler_params=pltpu.CompilerParams(vmem_limit_bytes=VMEM_LIMIT),
        cost_estimate=pl.CostEstimate(
            flops=0, bytes_accessed=4 * rows * width, transcendentals=0
        ),
        name="load_columns",
    )(in_hbm(matrix), *others)


def ahead_of(mark, *values):
    return lax.optimization_barrier((mark, *values))


def whole_kernel(spots, step, place, *refs):
    pieces, (matrix, _, out, out_b, cols) = refs[: len(spots)], refs[len(spots) :]
    assemble(place, pieces, spots, cols)
    total = None
    for start in range(0, cols.shape[0], step):
        here = slice(start, start + step)
        product = jnp.dot(matrix[:, here], cols[here, :], preferred_element_type=F32)
        total = product if total is None else total + product
    out[...] = total
    out_b[...] = total.astype(BF16)


def whole_product(place, pieces, matrix, mark, step):
    rows, width = matrix.shape
    n = pieces[0][0].shape[1]
    return pl.pallas_call(
        functools.partial(whole_kernel, [spots for _, spots in pieces], step),
        out_shape=(jax.ShapeDtypeStruct((rows, n), F32), jax.ShapeDtypeStruct((rows, n), BF16)),
        in_specs=[SMEM] + [VMEM] * (len(pieces) + 1) + [ANY],
        out_specs=(VMEM, VMEM),
        scratch_shapes=[pltpu.VMEM((width, n), BF16)],
        compiler_params=pltpu.CompilerParams(vmem_limit_bytes=VMEM_LIMIT),
        cost_estimate=pl.CostEstimate(
            flops=2 * rows * width * n, bytes_accessed=2 * rows * width, transcendentals=0
        ),
        name="whole_product",
    )(place, *[piece for piece, _ in pieces], in_vmem(matrix), mark)


def unit_kernel(blocks, spots, count, fresh, last, parts, ranges, place, *refs):
    units = len(blocks)
    pieces, refs = refs[: units * count], refs[units * count :]
    accs, refs = ([], refs) if fresh else (refs[: len(ranges)], refs[len(ranges) :])
    matrix, refs = refs[:parts], refs[parts + 1 :]
    outs, cols = refs[: len(ranges)], refs[-1]
    rows = pieces[0].shape[0]
    depth = cols.shape[1]
    for i, piece in enumerate(pieces):
        at = place[spots + i % count]
        cols[i // count, pl.ds(pl.multiple_of(at * rows, rows), rows), :] = piece[...]
    each = matrix[0].shape[1] // depth
    for u in range(units):
        index = place[blocks[u]]
        for part in range(parts):

            @pl.when(index // each == part)
            def _(u=u, part=part, index=index):
                here = pl.ds(pl.multiple_of(index % each * depth, 128), depth)
                for p, (start, height) in enumerate(ranges):
                    product = jnp.dot(
                        matrix[part][start : start + height, here],
                        cols[u],
                        preferred_element_type=F32,
                    )
                    if u:
                        outs[p][...] += product
                    elif fresh:
                        outs[p][...] = product
                    else:
                        outs[p][...] = accs[p][...] + product

    if last:
        for p in range(len(ranges)):
            refs[len(ranges) + p][...] = outs[p][...].astype(BF16)


def unit_product(place, blocks, spots, units, matrix, mark, accs, ranges, last):
    part, n = units[0][0].shape
    count = len(units[0])
    depth = count * part
    pieces = [piece for unit in units for piece in unit]
    rows = sum(height for _, height in ranges)
    parts = len(matrix)
    outs = pl.pallas_call(
        functools.partial(unit_kernel, blocks, spots, count, not accs, last, parts, ranges),
        out_shape=[jax.ShapeDtypeStruct((height, n), F32) for _, height in ranges]
        + [jax.ShapeDtypeStruct((height, n), BF16) for _, height in ranges] * last,
        in_specs=[SMEM] + [VMEM] * (len(pieces) + len(accs) + parts) + [ANY],
        out_specs=[VMEM] * (len(ranges) * (1 + last)),
        scratch_shapes=[pltpu.VMEM((len(units), depth, n), BF16)],
        compiler_params=pltpu.CompilerParams(vmem_limit_bytes=VMEM_LIMIT),
        cost_estimate=pl.CostEstimate(
            flops=2 * rows * depth * n * len(units),
            bytes_accessed=2 * rows * depth * len(units),
            transcendentals=0,
        ),
        name="unit_product",
    )(place, *pieces, *accs, *[in_vmem(m) for m in matrix], mark)
    return outs[: len(ranges)], outs[len(ranges) :]


def backward_kernel(ks, at, raw, given, ranges, parts, mode, others, place, *refs):
    raws, refs = refs[:raw], refs[raw:]
    vectors, refs = list(refs[:given]), refs[given:]
    matrix, refs = refs[:parts], refs[parts:]
    accs, refs = (refs[: len(ks)], refs[len(ks) :]) if mode == "added" else ([], refs)
    refs = refs[others:]
    if raw:
        vector = refs[-2 if mode else -1]
        total = raws[0][...] + raws[1][...].astype(F32)
        if raw == 3:
            total = raws[2][...] - total
        vector[...] = total.T.astype(BF16)
        vectors.append(vector)
    each = at.nz // parts
    depth = matrix[0].shape[1] // each
    half = depth // 2 if depth // 2 % 128 == 0 else depth
    for u, k in enumerate(ks):
        index = place[at.blocks + k]
        for part in range(parts):

            @pl.when(index // each == part)
            def _(u=u, part=part, index=index):
                for start in range(0, depth, half):
                    here = pl.ds(pl.multiple_of(index % each * depth + start, 128), half)
                    total = accs[u][:, start : start + half] if accs else None
                    for vector, (first, height) in zip(vectors, ranges):
                        product = jnp.dot(
                            vector[...],
                            matrix[part][first : first + height, here],
                            preferred_element_type=F32,
                        )
                        total = product if total is None else total + product
                    if mode:
                        refs[-1][start : start + half, :] = total.T
                    else:
                        refs[u][:, start : start + half] = total

        if mode:
            whole, (keep, send) = refs[-1], refs[2 * u : 2 * u + 2]
            rows = keep.shape[1]
            for xr in range(NX):
                for cr, out in ((0, keep), (1, send)):
                    spot = pl.multiple_of(place[at.near + xr * NC + cr] * rows, rows)
                    out[xr] = whole[pl.ds(spot, rows), :].astype(out.dtype)


def backward_blocks(place, ks, raws, vectors, ranges, matrix, accs, final, others, nz):
    n = raws[0].shape[1] if raws else vectors[0].shape[0]
    depth = matrix[0].shape[1] * len(matrix) // nz
    part = depth // (NX * NC)
    rows = sum(height for _, height in ranges)
    mode = ("added" if accs else "alone") if final else ""
    if final:
        shapes = [
            jax.ShapeDtypeStruct((NX, part, n), F32),
            jax.ShapeDtypeStruct((NX, part, n), BF16),
        ]
    else:
        shapes = [jax.ShapeDtypeStruct((n, depth), F32)]
    fresh = [jax.ShapeDtypeStruct((n, ranges[-1][1]), BF16)] if raws else []
    outs = pl.pallas_call(
        functools.partial(
            backward_kernel,
            ks,
            Spots(nz),
            len(raws),
            len(vectors),
            ranges,
            len(matrix),
            mode,
            len(others),
        ),
        out_shape=shapes * len(ks) + fresh,
        in_specs=[SMEM]
        + [VMEM] * (len(raws) + len(vectors) + len(matrix) + len(accs))
        + [ANY] * len(others),
        out_specs=[VMEM] * (len(shapes) * len(ks) + len(fresh)),
        scratch_shapes=[pltpu.VMEM((depth, n), F32)] * final,
        compiler_params=pltpu.CompilerParams(vmem_limit_bytes=LESS_VMEM),
        cost_estimate=pl.CostEstimate(
            flops=2 * rows * depth * n * len(ks),
            bytes_accessed=2 * rows * depth * len(ks),
            transcendentals=0,
        ),
        name="backward_blocks",
    )(place, *raws, *vectors, *[in_vmem(m) for m in matrix], *accs, *others)
    each = len(shapes)
    made = {k: outs[each * u : each * (u + 1)] for u, k in enumerate(ks)}
    return made, outs[-1] if raws else None


def product_scatter(multiply, groups, nz):
    keep, moved, across, left = {}, {}, {}, {}

    def cross(k):
        far = (keep[k][1] + moved[k][1].astype(F32)).astype(BF16)
        started.append(far)
        across[k] = x_swap(far, nz)

    def leave(k):
        partial = keep[k][0] + moved[k][0].astype(F32) + across[k].astype(F32)
        if k:
            partial = partial.astype(BF16)
            started.append(partial)
            partial = z_shift(partial, k, nz).astype(F32)
        left[k] = partial

    for ks, crossing, leaving in groups:
        started = []
        for k in crossing:
            cross(k)
        for k in leaving:
            leave(k)
        for k, (mine, send) in multiply(ks, started).items():
            keep[k] = mine
            moved[k] = c_swap(send, nz)
    started = []
    for k in far_first(nz):
        if k not in across:
            cross(k)
    for k in far_first(nz):
        if k not in left:
            leave(k)
    total = left[0]
    for k in far_first(nz)[:-1]:
        total = total + left[k]
    return total


def push_kernel(nz, place, block, own, arrived, coupling, mark, *refs):
    total_out, keep, send, (whole,) = refs[0], refs[1 : nz + 1], refs[nz + 1 : 2 * nz + 1], refs[2 * nz + 1 :]
    total = own[...] + arrived[...].astype(F32)
    total_out[...] = total
    pushed = jnp.dot(total.T.astype(BF16), coupling[...], preferred_element_type=F32).T
    whole[...] = jnp.zeros_like(whole)
    for j in range(coupling.shape[1] // RB):
        start = pl.multiple_of(block[j] * RB, RB)
        whole[pl.ds(start, RB), :] = pushed[j * RB : (j + 1) * RB, :]
    distribute(place, whole, keep, send)


def push_product(place, block, own, arrived, coupling, mark, width, nz):
    n = own.shape[1]
    part = width // (nz * NX * NC)
    outs = pl.pallas_call(
        functools.partial(push_kernel, nz),
        out_shape=[jax.ShapeDtypeStruct(own.shape, F32)]
        + [jax.ShapeDtypeStruct((NX, part, n), F32)] * nz
        + [jax.ShapeDtypeStruct((NX, part, n), BF16)] * nz,
        in_specs=[SMEM, SMEM, VMEM, VMEM, VMEM, ANY],
        out_specs=[VMEM] * (2 * nz + 1),
        scratch_shapes=[pltpu.VMEM((width, n), F32)],
        compiler_params=pltpu.CompilerParams(vmem_limit_bytes=VMEM_LIMIT),
        name="push_product",
    )(place, block, own, arrived, coupling, mark)
    return outs[0], outs[1 : nz + 1], outs[nz + 1 :]


def pull_kernel(spots, place, block, *refs):
    pieces, (coupling, _, out, out_b, whole, picked) = refs[: len(spots)], refs[len(spots) :]
    assemble(place, pieces, spots, whole)
    for j in range(coupling.shape[1] // RB):
        start = pl.multiple_of(block[j] * RB, RB)
        picked[j * RB : (j + 1) * RB, :] = whole[pl.ds(start, RB), :]
    out[...] = jnp.dot(coupling[...], picked[...], preferred_element_type=F32)
    out_b[...] = out[...].astype(BF16)


def pull_product(place, block, pieces, coupling, mark, height):
    rows, width = coupling.shape
    n = pieces[0][0].shape[1]
    return pl.pallas_call(
        functools.partial(pull_kernel, [spots for _, spots in pieces]),
        out_shape=(
            jax.ShapeDtypeStruct((rows, n), F32),
            jax.ShapeDtypeStruct((rows, n), BF16),
        ),
        in_specs=[SMEM, SMEM] + [VMEM] * (len(pieces) + 1) + [ANY],
        out_specs=(VMEM, VMEM),
        scratch_shapes=[pltpu.VMEM((height, n), BF16), pltpu.VMEM((width, n), BF16)],
        compiler_params=pltpu.CompilerParams(vmem_limit_bytes=VMEM_LIMIT),
        name="pull_product",
    )(place, block, *[piece for piece, _ in pieces], coupling, mark)


def in_hbm(matrix):
    return pltpu.with_memory_space_constraint(matrix, pltpu.HBM)


def in_vmem(matrix):
    return pltpu.with_memory_space_constraint(matrix, pltpu.VMEM)


def two_level_body(rhs_root, rhs_level, root_inverse, level_inverse, coupling_t, coupling_rows):
    nz = lax.axis_size("front") // (NX * NC)
    width = root_inverse.shape[1]
    place = places(nz)
    block = coupling_rows[0] % (width // RB)

    level_vmem, mark = load_columns(level_inverse, 0, 1, place, block)
    pieces, mark = gather_pieces(rhs_level.astype(BF16), mark, nz)
    own, own_b = whole_product(place, pieces, level_vmem, mark, level_inverse.shape[1] // nz)
    arrived = sub_swap(own_b)
    top, mark = load_columns(root_inverse, 0, 2, own_b)
    forward_level, keep, send = push_product(
        place, block, own, arrived, coupling_t, mark, width, nz
    )
    halves = [top]

    def load(value):
        bottom, mark = load_columns(root_inverse, 1, 2, value)
        halves.append(bottom)
        return mark

    update, mark = scatter_sum(keep, send, load, nz)
    shifted = rhs_root - update

    middle = root_inverse.shape[0] // 2
    upper, lower = (0, middle), (middle, middle)
    own, own_b = ring_product(
        place, shifted.astype(BF16), halves, [upper, lower], mark, nz
    )
    arrived = [sub_swap(value) for value in own_b]
    far = far_first(nz)
    others, mine = far[:-1], far[-1]
    accs, vector = backward_blocks(
        place, others, [own[0], arrived[0]], [], [upper], halves, [], False, [], nz
    )
    vectors = [vector]

    def multiply_root(ks, started):
        raws = [own[1], arrived[1]] if len(vectors) == 1 else []
        if ks == [mine]:
            made, _ = backward_blocks(
                place, ks, [], vectors, [upper, lower], halves, [], True, started, nz
            )
            return made
        added = [accs[k][0] for k in ks]
        made, vector = backward_blocks(
            place, ks, raws, vectors[1:], [lower], halves, added, True, started, nz
        )
        if raws:
            vectors.append(vector)
        return made

    groups = [([far[0]], [], []), ([far[1]], [], []), (far[2:-1], far[:1], [])]
    groups += [([mine], far[1:-1], far[:1])]
    root_potential = product_scatter(multiply_root, groups, nz)

    level_vmem, mark = load_columns(level_inverse, 0, 1, root_potential)
    pieces, mark = gather_pieces(root_potential.astype(BF16), mark, nz)
    own, own_b = pull_product(place, block, pieces, coupling_t, mark, width)
    raws = [own, sub_swap(own_b), forward_level]
    level_rows = [(0, level_inverse.shape[0])]
    vector = None

    def multiply_level(ks, started):
        nonlocal vector
        given = ([], [vector]) if vector is not None else (raws, [])
        made, new = backward_blocks(
            place, ks, *given, level_rows, [level_vmem], [], True, started, nz
        )
        vector = new if vector is None else vector
        return made

    groups = [(far[:1], [], []), (far[1:-1], [], []), ([mine], far[:-1], [])]
    level_potential = product_scatter(multiply_level, groups, nz)
    return (root_potential, level_potential)


def body(rhs_root, rhs_level, root_inverse, level_inverse, coupling_t, coupling_rows):
    fits = (
        lax.axis_size("sub") == 2
        and lax.axis_size("front") % (NX * NC) == 0
        and lax.axis_size("front") >= 3 * NX * NC
        and all(a.shape[0] % 16 == 0 for a in (rhs_root, rhs_level, root_inverse, level_inverse))
        and all(a.shape[1] % 128 == 0 for a in (rhs_root, root_inverse, level_inverse, coupling_t))
        and NC * rhs_root.shape[0] % 128 == 0
        and NX * NC * rhs_level.shape[0] % 128 == 0
        and (root_inverse.size + level_inverse.size) * 2 <= 40 * 1024 * 1024
        and root_inverse.shape[0] % 32 == 0
        and root_inverse.shape[1] % (4 * rhs_root.shape[0] * NC) == 0
    )
    chosen = two_level_body if fits else general_body
    return chosen(rhs_root, rhs_level, root_inverse, level_inverse, coupling_t, coupling_rows)


def solution(mesh):
    return jax.shard_map(
        body,
        mesh=mesh,
        in_specs=(
            P(("sub", "front"), None),
            P(("sub", "front"), None),
            P("front", "sub"),
            P("front", "sub"),
            P("front", "sub"),
            P("front", "sub"),
        ),
        out_specs=(P(("sub", "front"), None), P(("sub", "front"), None)),
        check_vma=False,
    )
```

```python
import functools

import jax
import jax.numpy as jnp
import numpy as np
from jax import lax
from jax.experimental import pallas as pl
from jax.experimental.pallas import tpu as pltpu
from jax.sharding import PartitionSpec as P

RB = 128
NX = 2
NC = 2
F32 = jnp.float32
BF16 = jnp.bfloat16
HIGHEST_PRECISION = lax.Precision.HIGHEST
VMEM = pl.BlockSpec(memory_space=pltpu.VMEM)
SMEM = pl.BlockSpec(memory_space=pltpu.SMEM)
HBM = pl.BlockSpec(memory_space=pltpu.HBM)
ANY = pl.BlockSpec(memory_space=pl.ANY)
VMEM_LIMIT = 15 * 1024 * 1024
LESS_VMEM = 8 * 1024 * 1024


def transposed_product(matrix, vector):
    return lax.dot_general(
        matrix, vector, (((0,), (0,)), ((), ())), preferred_element_type=jnp.float32
    )


def gather_columns(pieces):
    return lax.all_gather(pieces, "front", axis=0, tiled=True)


def gather_rows(pieces):
    return lax.all_gather(pieces, "sub", axis=0, tiled=True)


def share_sub(summand):
    return lax.psum_scatter(
        summand.astype(jnp.bfloat16), "sub", scatter_dimension=0, tiled=True
    ).astype(jnp.float32)


def share_front(summand):
    return lax.psum_scatter(summand, "front", scatter_dimension=0, tiled=True)


def general_body(rhs_root, rhs_level, root_inverse, level_inverse, coupling_t, coupling_rows):
    rhs_count = rhs_root.shape[1]
    block_count = root_inverse.shape[1] // RB
    slot_count = coupling_t.shape[1] // RB
    level_cols = gather_columns(rhs_level.astype(jnp.bfloat16))
    forward_level = share_sub(
        jnp.dot(level_inverse, level_cols, preferred_element_type=jnp.float32)
    )
    level_rows = gather_rows(forward_level.astype(jnp.bfloat16))
    local_block = coupling_rows[0] % block_count
    selector = (
        lax.broadcasted_iota(jnp.int32, (block_count, slot_count), 0) == local_block[None, :]
    ).astype(jnp.float32)
    pushed = transposed_product(coupling_t, level_rows).reshape(slot_count, RB, rhs_count)
    update = jnp.einsum("bk,kin->bin", selector, pushed, precision=HIGHEST_PRECISION).reshape(
        block_count * RB, rhs_count
    )
    shifted = rhs_root - share_front(update)
    root_cols = gather_columns(shifted.astype(jnp.bfloat16))
    forward_root = share_sub(jnp.dot(root_inverse, root_cols, preferred_element_type=jnp.float32))
    root_rows = gather_rows(forward_root.astype(jnp.bfloat16))
    root_potential = share_front(transposed_product(root_inverse, root_rows))
    potential_cols = gather_columns(root_potential.astype(jnp.bfloat16))
    picked = potential_cols.reshape(block_count, RB, rhs_count)[local_block]
    pulled = jnp.dot(
        coupling_t, picked.reshape(slot_count * RB, rhs_count), preferred_element_type=jnp.float32
    )
    corrected = forward_level - share_sub(pulled)
    corrected_rows = gather_rows(corrected.astype(jnp.bfloat16))
    level_potential = share_front(transposed_product(level_inverse, corrected_rows))
    return (root_potential, level_potential)


def z_shift(value, shift, nz):
    width = NX * NC
    count = nz * width
    return lax.ppermute(
        value, "front", [(i, (i + shift * width) % count) for i in range(count)]
    )


def x_swap(value, nz):
    return lax.ppermute(value, "front", [(i, i ^ NC) for i in range(nz * NX * NC)])


def c_swap(value, nz):
    return lax.ppermute(value, "front", [(i, i ^ 1) for i in range(nz * NX * NC)])


def sub_swap(value):
    return lax.ppermute(value, "sub", [(0, 1), (1, 0)])


def gather_pieces(own, mark, nz):
    group = NX * NC
    order = near_first(nz)
    held = {0: own}
    for k in order[1:]:
        held[k] = z_shift(own, -k, nz)
    mark, *arrived = ahead_of(mark, *[held[k] for k in order[1:-1]])
    held.update(zip(order[1:-1], arrived))
    across = {}
    for k in order:
        across[k] = x_swap(held[k], nz)
    lanes = [(k * group, held[k]) for k in order], [(k * group + NC, across[k]) for k in order]
    pieces = lanes[0] + lanes[1]
    out = [(piece, [spot]) for spot, piece in pieces]
    batches = [list(pair) for pair in zip(*lanes)]
    for batch in batches[:-1] + [batches[-1][:1], batches[-1][1:]]:
        sent = [piece for _, piece in batch]
        sent = jnp.concatenate(sent) if len(sent) > 1 else sent[0]
        out.append((c_swap(sent, nz), [spot + 1 for spot, _ in batch]))
    return out, mark


def near_first(nz):
    return sorted(range(nz), key=lambda k: min(k, nz - k))


def ring_step(value, way, nz):
    count = NX * nz
    chip = lambda p: (p * NX if p < nz else (count - 1 - p) * NX + 1)
    pairs = [
        (chip(p) * NC + c, chip((p + way) % count) * NC + c)
        for p in range(count)
        for c in range(NC)
    ]
    return lax.ppermute(value, "front", pairs)


def ring_product(place, own, matrix, ranges, mark, nz):
    count = NX * nz
    at = Spots(nz)
    accs, waiting = [], None
    held = {0: own}

    def multiply(units, accs, ranges, last=False):
        steps, pieces, others = units
        blocks = [at.ring + j for j in steps]
        return unit_product(
            place, blocks, at.core, pieces, others, matrix, mark, accs, ranges, last
        )

    for step in range(nz + 1):
        if step > 1:
            first, *arrived = ahead_of(accs[0], *held.values())
            accs = [first, *accs[1:]]
            held = dict(zip(held, arrived))
        following = {}
        if step < nz:
            following[(-step - 1) % count] = ring_step(held[(-step) % count], 1, nz)
            if step < nz - 1:
                following[step + 1] = ring_step(held[step], -1, nz)
        pieces = list(held.values())
        others = c_swap(jnp.concatenate(pieces) if len(pieces) > 1 else pieces[0], nz)
        units = (list(held), pieces, others)
        if waiting:
            accs, _ = multiply(waiting, accs, ranges)
        waiting, held = units, following
    outs = [
        multiply(waiting, [acc], [rows], True) for acc, rows in zip(accs, ranges)
    ]
    return [own for (own,), _ in outs], [own_b for _, (own_b,) in outs]


def far_first(nz):
    return near_first(nz)[::-1]


def scatter_sum(keep, send, load, nz):
    order = far_first(nz)
    moved = {k: c_swap(send[k], nz) for k in order}
    across, partial = {}, {}
    for k in order:
        far = (keep[k][1].astype(F32) + moved[k][1].astype(F32)).astype(BF16)
        across[k] = x_swap(far, nz)
    for k in order:
        partial[k] = keep[k][0].astype(F32) + moved[k][0].astype(F32) + across[k].astype(F32)
    total = partial[0]
    leaving = {k: partial[k].astype(BF16) for k in order[:-1]}
    mark = load(leaving[order[-2]])
    arrived = [z_shift(leaving[k], k, nz) for k in order[:-1]]
    mark, *arrived = ahead_of(mark, *arrived)
    for value in arrived:
        total = total + value.astype(F32)
    return total, mark


def places(nz):
    count = NX * nz
    table = []
    for me in range(count * NC):
        z, x, c = me // (NX * NC), (me // NC) % NX, me % NC
        near = [(x ^ xr) * NC + (c ^ cr) for xr in range(NX) for cr in range(NC)]
        blocks = [(z + k) % nz for k in range(nz)]
        row = [b * NX * NC + i for b in blocks for i in near]
        spot = z if x == 0 else count - 1 - z
        for j in range(count):
            p = (spot + j) % count
            row.append(p * NX if p < nz else (count - 1 - p) * NX + 1)
        pairs = [b * NX + (x ^ xr) for b in blocks for xr in range(NX)]
        table.append(row + blocks + near + [c, 1 - c] + pairs)
    return lax.dynamic_index_in_dim(
        jnp.asarray(np.array(table, np.int32)), lax.axis_index("front"), 0, keepdims=False
    )


class Spots:
    def __init__(self, nz):
        self.nz = nz
        group = NX * NC
        self.ring = nz * group
        self.blocks = self.ring + NX * nz
        self.near = self.blocks + nz
        self.core = self.near + group
        self.pairs = self.core + NC


def assemble(place, pieces, spots, whole):
    for piece, parts in zip(pieces, spots):
        rows = piece.shape[0] // len(parts)
        for i, spot in enumerate(parts):
            start = pl.multiple_of(place[spot] * rows, rows)
            whole[pl.ds(start, rows), :] = piece[i * rows : (i + 1) * rows, :]


def distribute(place, whole, keep, send):
    nz = len(keep)
    rows = keep[0].shape[1]
    for k in range(nz):
        for xr in range(NX):
            for cr, out in ((0, keep[k]), (1, send[k])):
                i = (k * NX + xr) * NC + cr
                out[xr] = whole[
                    pl.ds(pl.multiple_of(place[i] * rows, rows), rows), :
                ].astype(out.dtype)


def load_kernel(start, count, matrix, *refs):
    out, mark, arrived = refs[-3:]
    rows, width = out.shape
    height = rows // count
    copies = []
    for i in range(count):
        here = pl.ds(i * height, height)
        copies.append(
            pltpu.make_async_copy(
                matrix.at[here, pl.ds(start, width)], out.at[here, :], arrived.at[i]
            )
        )
    for copy in copies:
        copy.start()
    for copy in copies:
        copy.wait()
    mark[...] = jnp.zeros_like(mark)


def load_columns(matrix, part, parts, *others):
    rows, width = matrix.shape
    width //= parts
    count = max(p for p in range(1, 13) if rows % (16 * p) == 0)
    return pl.pallas_call(
        functools.partial(load_kernel, part * width, count),
        out_shape=(
            pltpu.VMEM((rows, width), matrix.dtype),
            jax.ShapeDtypeStruct((8, 128), F32),
        ),
        in_specs=[HBM] + [ANY] * len(others),
        out_specs=(VMEM, VMEM),
        scratch_shapes=[pltpu.SemaphoreType.DMA((count,))],
        compiler_params=pltpu.CompilerParams(vmem_limit_bytes=VMEM_LIMIT),
        cost_estimate=pl.CostEstimate(
            flops=0, bytes_accessed=4 * rows * width, transcendentals=0
        ),
        name="load_columns",
    )(in_hbm(matrix), *others)


def ahead_of(mark, *values):
    return lax.optimization_barrier((mark, *values))


def whole_kernel(spots, step, place, *refs):
    pieces, (matrix, _, out, out_b, cols) = refs[: len(spots)], refs[len(spots) :]
    assemble(place, pieces, spots, cols)
    total = None
    for start in range(0, cols.shape[0], step):
        here = slice(start, start + step)
        product = jnp.dot(matrix[:, here], cols[here, :], preferred_element_type=F32)
        total = product if total is None else total + product
    out[...] = total
    out_b[...] = total.astype(BF16)


def whole_product(place, pieces, matrix, mark, step):
    rows, width = matrix.shape
    n = pieces[0][0].shape[1]
    return pl.pallas_call(
        functools.partial(whole_kernel, [spots for _, spots in pieces], step),
        out_shape=(jax.ShapeDtypeStruct((rows, n), F32), jax.ShapeDtypeStruct((rows, n), BF16)),
        in_specs=[SMEM] + [VMEM] * (len(pieces) + 1) + [ANY],
        out_specs=(VMEM, VMEM),
        scratch_shapes=[pltpu.VMEM((width, n), BF16)],
        compiler_params=pltpu.CompilerParams(vmem_limit_bytes=VMEM_LIMIT),
        cost_estimate=pl.CostEstimate(
            flops=2 * rows * width * n, bytes_accessed=2 * rows * width, transcendentals=0
        ),
        name="whole_product",
    )(place, *[piece for piece, _ in pieces], in_vmem(matrix), mark)


def unit_kernel(blocks, core, fresh, last, parts, ranges, place, *refs):
    units = len(blocks)
    pieces, others, refs = refs[:units], refs[units], refs[units + 1 :]
    accs, refs = ([], refs) if fresh else (refs[: len(ranges)], refs[len(ranges) :])
    matrix, refs = refs[:parts], refs[parts + 1 :]
    outs, cols = refs[: len(ranges)], refs[-1]
    rows = pieces[0].shape[0]
    depth = cols.shape[1]
    mine = pl.ds(pl.multiple_of(place[core] * rows, rows), rows)
    theirs = pl.ds(pl.multiple_of(place[core + 1] * rows, rows), rows)
    for u, piece in enumerate(pieces):
        cols[u, mine, :] = piece[...]
        cols[u, theirs, :] = others[u * rows : (u + 1) * rows, :]
    each = matrix[0].shape[1] // depth
    for u in range(units):
        index = place[blocks[u]]
        for part in range(parts):

            @pl.when(index // each == part)
            def _(u=u, part=part, index=index):
                here = pl.ds(pl.multiple_of(index % each * depth, 128), depth)
                for p, (start, height) in enumerate(ranges):
                    product = jnp.dot(
                        matrix[part][start : start + height, here],
                        cols[u],
                        preferred_element_type=F32,
                    )
                    if u:
                        outs[p][...] += product
                    elif fresh:
                        outs[p][...] = product
                    else:
                        outs[p][...] = accs[p][...] + product

    if last:
        for p in range(len(ranges)):
            refs[len(ranges) + p][...] = outs[p][...].astype(BF16)


def unit_product(place, blocks, core, pieces, others, matrix, mark, accs, ranges, last):
    part, n = pieces[0].shape
    units = len(pieces)
    depth = NC * part
    rows = sum(height for _, height in ranges)
    parts = len(matrix)
    outs = pl.pallas_call(
        functools.partial(unit_kernel, blocks, core, not accs, last, parts, ranges),
        out_shape=[jax.ShapeDtypeStruct((height, n), F32) for _, height in ranges]
        + [jax.ShapeDtypeStruct((height, n), BF16) for _, height in ranges] * last,
        in_specs=[SMEM] + [VMEM] * (units + 1 + len(accs) + parts) + [ANY],
        out_specs=[VMEM] * (len(ranges) * (1 + last)),
        scratch_shapes=[pltpu.VMEM((units, depth, n), BF16)],
        compiler_params=pltpu.CompilerParams(vmem_limit_bytes=VMEM_LIMIT),
        cost_estimate=pl.CostEstimate(
            flops=2 * rows * depth * n * units,
            bytes_accessed=2 * rows * depth * units,
            transcendentals=0,
        ),
        name="unit_product",
    )(place, *pieces, others, *accs, *[in_vmem(m) for m in matrix], mark)
    return outs[: len(ranges)], outs[len(ranges) :]


def backward_kernel(ks, at, raw, given, ranges, parts, mode, others, place, *refs):
    raws, refs = refs[:raw], refs[raw:]
    vectors, refs = list(refs[:given]), refs[given:]
    matrix, refs = refs[:parts], refs[parts:]
    accs, refs = (refs[: len(ks)], refs[len(ks) :]) if mode == "added" else ([], refs)
    refs = refs[others:]
    if raw:
        vector = refs[-2 if mode else -1]
        total = raws[0][...] + raws[1][...].astype(F32)
        if raw == 3:
            total = raws[2][...] - total
        vector[...] = total.T.astype(BF16)
        vectors.append(vector)
    each = at.nz // parts
    depth = matrix[0].shape[1] // each
    half = depth // 2 if depth // 2 % 128 == 0 else depth
    for u, k in enumerate(ks):
        index = place[at.blocks + k]
        for part in range(parts):

            @pl.when(index // each == part)
            def _(u=u, part=part, index=index):
                for start in range(0, depth, half):
                    here = pl.ds(pl.multiple_of(index % each * depth + start, 128), half)
                    total = accs[u][:, start : start + half] if accs else None
                    for vector, (first, height) in zip(vectors, ranges):
                        product = jnp.dot(
                            vector[...],
                            matrix[part][first : first + height, here],
                            preferred_element_type=F32,
                        )
                        total = product if total is None else total + product
                    if mode:
                        refs[-1][start : start + half, :] = total.T
                    else:
                        refs[u][:, start : start + half] = total

        if mode:
            whole, (keep, send) = refs[-1], refs[2 * u : 2 * u + 2]
            rows = keep.shape[1]
            for xr in range(NX):
                for cr, out in ((0, keep), (1, send)):
                    spot = pl.multiple_of(place[at.near + xr * NC + cr] * rows, rows)
                    out[xr] = whole[pl.ds(spot, rows), :].astype(out.dtype)


def backward_blocks(place, ks, raws, vectors, ranges, matrix, accs, final, others, nz):
    n = raws[0].shape[1] if raws else vectors[0].shape[0]
    depth = matrix[0].shape[1] * len(matrix) // nz
    part = depth // (NX * NC)
    rows = sum(height for _, height in ranges)
    mode = ("added" if accs else "alone") if final else ""
    if final:
        shapes = [
            jax.ShapeDtypeStruct((NX, part, n), F32),
            jax.ShapeDtypeStruct((NX, part, n), BF16),
        ]
    else:
        shapes = [jax.ShapeDtypeStruct((n, depth), F32)]
    fresh = [jax.ShapeDtypeStruct((n, ranges[-1][1]), BF16)] if raws else []
    outs = pl.pallas_call(
        functools.partial(
            backward_kernel,
            ks,
            Spots(nz),
            len(raws),
            len(vectors),
            ranges,
            len(matrix),
            mode,
            len(others),
        ),
        out_shape=shapes * len(ks) + fresh,
        in_specs=[SMEM]
        + [VMEM] * (len(raws) + len(vectors) + len(matrix) + len(accs))
        + [ANY] * len(others),
        out_specs=[VMEM] * (len(shapes) * len(ks) + len(fresh)),
        scratch_shapes=[pltpu.VMEM((depth, n), F32)] * final,
        compiler_params=pltpu.CompilerParams(vmem_limit_bytes=LESS_VMEM),
        cost_estimate=pl.CostEstimate(
            flops=2 * rows * depth * n * len(ks),
            bytes_accessed=2 * rows * depth * len(ks),
            transcendentals=0,
        ),
        name="backward_blocks",
    )(place, *raws, *vectors, *[in_vmem(m) for m in matrix], *accs, *others)
    each = len(shapes)
    made = {k: outs[each * u : each * (u + 1)] for u, k in enumerate(ks)}
    return made, outs[-1] if raws else None


def product_scatter(multiply, groups, nz):
    keep, moved, across, left = {}, {}, {}, {}

    def cross(k):
        far = (keep[k][1] + moved[k][1].astype(F32)).astype(BF16)
        started.append(far)
        across[k] = x_swap(far, nz)

    def leave(k):
        partial = keep[k][0] + moved[k][0].astype(F32) + across[k].astype(F32)
        if k:
            partial = partial.astype(BF16)
            started.append(partial)
            partial = z_shift(partial, k, nz).astype(F32)
        left[k] = partial

    for ks, crossing, leaving in groups:
        started = []
        for k in crossing:
            cross(k)
        for k in leaving:
            leave(k)
        for k, (mine, send) in multiply(ks, started).items():
            keep[k] = mine
            moved[k] = c_swap(send, nz)
    started = []
    for k in far_first(nz):
        if k not in across:
            cross(k)
    for k in far_first(nz):
        if k not in left:
            leave(k)
    total = left[0]
    for k in far_first(nz)[:-1]:
        total = total + left[k]
    return total


def push_kernel(nz, place, block, own, arrived, coupling, mark, *refs):
    total_out, keep, send, (whole,) = refs[0], refs[1 : nz + 1], refs[nz + 1 : 2 * nz + 1], refs[2 * nz + 1 :]
    total = own[...] + arrived[...].astype(F32)
    total_out[...] = total
    pushed = jnp.dot(total.T.astype(BF16), coupling[...], preferred_element_type=F32).T
    whole[...] = jnp.zeros_like(whole)
    for j in range(coupling.shape[1] // RB):
        start = pl.multiple_of(block[j] * RB, RB)
        whole[pl.ds(start, RB), :] = pushed[j * RB : (j + 1) * RB, :]
    distribute(place, whole, keep, send)


def push_product(place, block, own, arrived, coupling, mark, width, nz):
    n = own.shape[1]
    part = width // (nz * NX * NC)
    outs = pl.pallas_call(
        functools.partial(push_kernel, nz),
        out_shape=[jax.ShapeDtypeStruct(own.shape, F32)]
        + [jax.ShapeDtypeStruct((NX, part, n), F32)] * nz
        + [jax.ShapeDtypeStruct((NX, part, n), BF16)] * nz,
        in_specs=[SMEM, SMEM, VMEM, VMEM, VMEM, ANY],
        out_specs=[VMEM] * (2 * nz + 1),
        scratch_shapes=[pltpu.VMEM((width, n), F32)],
        compiler_params=pltpu.CompilerParams(vmem_limit_bytes=VMEM_LIMIT),
        name="push_product",
    )(place, block, own, arrived, coupling, mark)
    return outs[0], outs[1 : nz + 1], outs[nz + 1 :]


def pull_kernel(spots, place, block, *refs):
    pieces, (coupling, _, out, out_b, whole, picked) = refs[: len(spots)], refs[len(spots) :]
    assemble(place, pieces, spots, whole)
    for j in range(coupling.shape[1] // RB):
        start = pl.multiple_of(block[j] * RB, RB)
        picked[j * RB : (j + 1) * RB, :] = whole[pl.ds(start, RB), :]
    out[...] = jnp.dot(coupling[...], picked[...], preferred_element_type=F32)
    out_b[...] = out[...].astype(BF16)


def pull_product(place, block, pieces, coupling, mark, height):
    rows, width = coupling.shape
    n = pieces[0][0].shape[1]
    return pl.pallas_call(
        functools.partial(pull_kernel, [spots for _, spots in pieces]),
        out_shape=(
            jax.ShapeDtypeStruct((rows, n), F32),
            jax.ShapeDtypeStruct((rows, n), BF16),
        ),
        in_specs=[SMEM, SMEM] + [VMEM] * (len(pieces) + 1) + [ANY],
        out_specs=(VMEM, VMEM),
        scratch_shapes=[pltpu.VMEM((height, n), BF16), pltpu.VMEM((width, n), BF16)],
        compiler_params=pltpu.CompilerParams(vmem_limit_bytes=VMEM_LIMIT),
        name="pull_product",
    )(place, block, *[piece for piece, _ in pieces], coupling, mark)


def in_hbm(matrix):
    return pltpu.with_memory_space_constraint(matrix, pltpu.HBM)


def in_vmem(matrix):
    return pltpu.with_memory_space_constraint(matrix, pltpu.VMEM)


def two_level_body(rhs_root, rhs_level, root_inverse, level_inverse, coupling_t, coupling_rows):
    nz = lax.axis_size("front") // (NX * NC)
    width = root_inverse.shape[1]
    place = places(nz)
    block = coupling_rows[0] % (width // RB)

    level_vmem, mark = load_columns(level_inverse, 0, 1, place, block)
    pieces, mark = gather_pieces(rhs_level.astype(BF16), mark, nz)
    own, own_b = whole_product(place, pieces, level_vmem, mark, level_inverse.shape[1] // nz)
    arrived = sub_swap(own_b)
    top, mark = load_columns(root_inverse, 0, 2, own_b)
    forward_level, keep, send = push_product(
        place, block, own, arrived, coupling_t, mark, width, nz
    )
    halves = [top]

    def load(value):
        bottom, mark = load_columns(root_inverse, 1, 2, value)
        halves.append(bottom)
        return mark

    update, mark = scatter_sum(keep, send, load, nz)
    shifted = rhs_root - update

    middle = root_inverse.shape[0] // 2
    upper, lower = (0, middle), (middle, middle)
    own, own_b = ring_product(
        place, shifted.astype(BF16), halves, [upper, lower], mark, nz
    )
    arrived = [sub_swap(value) for value in own_b]
    far = far_first(nz)
    others, mine = far[:-1], far[-1]
    accs, vector = backward_blocks(
        place, others, [own[0], arrived[0]], [], [upper], halves, [], False, [], nz
    )
    vectors = [vector]

    def multiply_root(ks, started):
        raws = [own[1], arrived[1]] if len(vectors) == 1 else []
        if ks == [mine]:
            made, _ = backward_blocks(
                place, ks, [], vectors, [upper, lower], halves, [], True, started, nz
            )
            return made
        added = [accs[k][0] for k in ks]
        made, vector = backward_blocks(
            place, ks, raws, vectors[1:], [lower], halves, added, True, started, nz
        )
        if raws:
            vectors.append(vector)
        return made

    groups = [([far[0]], [], []), ([far[1]], [], []), (far[2:-1], far[:1], [])]
    groups += [([mine], far[1:-1], far[:1])]
    root_potential = product_scatter(multiply_root, groups, nz)

    level_vmem, mark = load_columns(level_inverse, 0, 1, root_potential)
    pieces, mark = gather_pieces(root_potential.astype(BF16), mark, nz)
    own, own_b = pull_product(place, block, pieces, coupling_t, mark, width)
    raws = [own, sub_swap(own_b), forward_level]
    level_rows = [(0, level_inverse.shape[0])]
    vector = None

    def multiply_level(ks, started):
        nonlocal vector
        given = ([], [vector]) if vector is not None else (raws, [])
        made, new = backward_blocks(
            place, ks, *given, level_rows, [level_vmem], [], True, started, nz
        )
        vector = new if vector is None else vector
        return made

    groups = [(far[:1], [], []), (far[1:-1], [], []), ([mine], far[:-1], [])]
    level_potential = product_scatter(multiply_level, groups, nz)
    return (root_potential, level_potential)


def body(rhs_root, rhs_level, root_inverse, level_inverse, coupling_t, coupling_rows):
    fits = (
        lax.axis_size("sub") == 2
        and lax.axis_size("front") % (NX * NC) == 0
        and lax.axis_size("front") >= 3 * NX * NC
        and all(a.shape[0] % 16 == 0 for a in (rhs_root, rhs_level, root_inverse, level_inverse))
        and all(a.shape[1] % 128 == 0 for a in (rhs_root, root_inverse, level_inverse, coupling_t))
        and NC * rhs_root.shape[0] % 128 == 0
        and NX * NC * rhs_level.shape[0] % 128 == 0
        and (root_inverse.size + level_inverse.size) * 2 <= 40 * 1024 * 1024
        and root_inverse.shape[0] % 32 == 0
        and root_inverse.shape[1] % (4 * rhs_root.shape[0] * NC) == 0
    )
    chosen = two_level_body if fits else general_body
    return chosen(rhs_root, rhs_level, root_inverse, level_inverse, coupling_t, coupling_rows)


def solution(mesh):
    return jax.shard_map(
        body,
        mesh=mesh,
        in_specs=(
            P(("sub", "front"), None),
            P(("sub", "front"), None),
            P("front", "sub"),
            P("front", "sub"),
            P("front", "sub"),
            P("front", "sub"),
        ),
        out_specs=(P(("sub", "front"), None), P(("sub", "front"), None)),
        check_vma=False,
    )
```

```python
import functools

import jax
import jax.numpy as jnp
import numpy as np
from jax import lax
from jax.experimental import pallas as pl
from jax.experimental.pallas import tpu as pltpu
from jax.sharding import PartitionSpec as P

RB = 128
NX = 2
NC = 2
F32 = jnp.float32
BF16 = jnp.bfloat16
HIGHEST_PRECISION = lax.Precision.HIGHEST
VMEM = pl.BlockSpec(memory_space=pltpu.VMEM)
SMEM = pl.BlockSpec(memory_space=pltpu.SMEM)
HBM = pl.BlockSpec(memory_space=pltpu.HBM)
ANY = pl.BlockSpec(memory_space=pl.ANY)
VMEM_LIMIT = 15 * 1024 * 1024
LESS_VMEM = 8 * 1024 * 1024


def transposed_product(matrix, vector):
    return lax.dot_general(
        matrix, vector, (((0,), (0,)), ((), ())), preferred_element_type=jnp.float32
    )


def gather_columns(pieces):
    return lax.all_gather(pieces, "front", axis=0, tiled=True)


def gather_rows(pieces):
    return lax.all_gather(pieces, "sub", axis=0, tiled=True)


def share_sub(summand):
    return lax.psum_scatter(
        summand.astype(jnp.bfloat16), "sub", scatter_dimension=0, tiled=True
    ).astype(jnp.float32)


def share_front(summand):
    return lax.psum_scatter(summand, "front", scatter_dimension=0, tiled=True)


def general_body(rhs_root, rhs_level, root_inverse, level_inverse, coupling_t, coupling_rows):
    rhs_count = rhs_root.shape[1]
    block_count = root_inverse.shape[1] // RB
    slot_count = coupling_t.shape[1] // RB
    level_cols = gather_columns(rhs_level.astype(jnp.bfloat16))
    forward_level = share_sub(
        jnp.dot(level_inverse, level_cols, preferred_element_type=jnp.float32)
    )
    level_rows = gather_rows(forward_level.astype(jnp.bfloat16))
    local_block = coupling_rows[0] % block_count
    selector = (
        lax.broadcasted_iota(jnp.int32, (block_count, slot_count), 0) == local_block[None, :]
    ).astype(jnp.float32)
    pushed = transposed_product(coupling_t, level_rows).reshape(slot_count, RB, rhs_count)
    update = jnp.einsum("bk,kin->bin", selector, pushed, precision=HIGHEST_PRECISION).reshape(
        block_count * RB, rhs_count
    )
    shifted = rhs_root - share_front(update)
    root_cols = gather_columns(shifted.astype(jnp.bfloat16))
    forward_root = share_sub(jnp.dot(root_inverse, root_cols, preferred_element_type=jnp.float32))
    root_rows = gather_rows(forward_root.astype(jnp.bfloat16))
    root_potential = share_front(transposed_product(root_inverse, root_rows))
    potential_cols = gather_columns(root_potential.astype(jnp.bfloat16))
    picked = potential_cols.reshape(block_count, RB, rhs_count)[local_block]
    pulled = jnp.dot(
        coupling_t, picked.reshape(slot_count * RB, rhs_count), preferred_element_type=jnp.float32
    )
    corrected = forward_level - share_sub(pulled)
    corrected_rows = gather_rows(corrected.astype(jnp.bfloat16))
    level_potential = share_front(transposed_product(level_inverse, corrected_rows))
    return (root_potential, level_potential)


def z_shift(value, shift, nz):
    width = NX * NC
    count = nz * width
    return lax.ppermute(
        value, "front", [(i, (i + shift * width) % count) for i in range(count)]
    )


def x_swap(value, nz):
    return lax.ppermute(value, "front", [(i, i ^ NC) for i in range(nz * NX * NC)])


def c_swap(value, nz):
    return lax.ppermute(value, "front", [(i, i ^ 1) for i in range(nz * NX * NC)])


def sub_swap(value):
    return lax.ppermute(value, "sub", [(0, 1), (1, 0)])


def gather_pieces(own, mark, nz):
    group = NX * NC
    order = near_first(nz)
    held = {0: own}
    for k in order[1:]:
        held[k] = z_shift(own, -k, nz)
    mark, *arrived = ahead_of(mark, *[held[k] for k in order[1:-1]])
    held.update(zip(order[1:-1], arrived))
    across = {}
    for k in order:
        across[k] = x_swap(held[k], nz)
    lanes = [(k * group, held[k]) for k in order], [(k * group + NC, across[k]) for k in order]
    pieces = lanes[0] + lanes[1]
    out = [(piece, [spot]) for spot, piece in pieces]
    batches = [list(pair) for pair in zip(*lanes)]
    for batch in batches[:-1] + [batches[-1][:1], batches[-1][1:]]:
        sent = [piece for _, piece in batch]
        sent = jnp.concatenate(sent) if len(sent) > 1 else sent[0]
        out.append((c_swap(sent, nz), [spot + 1 for spot, _ in batch]))
    return out, mark


def near_first(nz):
    return sorted(range(nz), key=lambda k: min(k, nz - k))


def ring_step(value, nz):
    count = NX * nz
    chip = lambda p: (p * NX if p < nz else (count - 1 - p) * NX + 1)
    pairs = [
        (chip(p) * NC + c, chip((p + (-1 if c else 1)) % count) * NC + c)
        for p in range(count)
        for c in range(NC)
    ]
    return lax.ppermute(value, "front", pairs)


def ring_product(place, own, matrix, ranges, mark, nz):
    at = Spots(nz)
    accs, waiting = [], None
    rows = own.shape[0]
    held = jnp.concatenate([own, c_swap(own, nz)])

    def multiply(units, accs, ranges, last=False):
        blocks, arrays, parts = units
        return unit_product(
            place, blocks, arrays, parts, at.core, matrix, mark, accs, ranges, last
        )

    for step in range(nz + 1):
        if step > 1:
            first, held = ahead_of(accs[0], held)
            accs = [first, *accs[1:]]
        following = None
        if step < nz - 1:
            following = ring_step(held, nz)
        elif step < nz:
            following = ring_step(held[:rows], nz)
        if step == 0:
            accs, _ = multiply(([at.mine], [held], [((0, 0), (0, 1))]), accs, ranges)
            units = None
        elif step < nz:
            units = (
                [at.mine + step, at.theirs + step],
                [held, c_swap(held, nz)],
                [((0, 0), (0, 1)), ((1, 1), (1, 0))],
            )
        else:
            units = [at.mine + step], [held, c_swap(held, nz)], [((0, 0), (1, 0))]
        if waiting:
            accs, _ = multiply(waiting, accs, ranges)
        waiting, held = units, following
    outs = [
        multiply(waiting, [acc], [rows], True) for acc, rows in zip(accs, ranges)
    ]
    return [own for (own,), _ in outs], [own_b for _, (own_b,) in outs]


def far_first(nz):
    return near_first(nz)[::-1]


def scatter_sum(keep, send, load, nz):
    order = far_first(nz)
    moved = {k: c_swap(send[k], nz) for k in order}
    across, partial = {}, {}
    for k in order:
        far = (keep[k][1].astype(F32) + moved[k][1].astype(F32)).astype(BF16)
        across[k] = x_swap(far, nz)
    for k in order:
        partial[k] = keep[k][0].astype(F32) + moved[k][0].astype(F32) + across[k].astype(F32)
    total = partial[0]
    leaving = {k: partial[k].astype(BF16) for k in order[:-1]}
    mark = load(leaving[order[-2]])
    arrived = [z_shift(leaving[k], k, nz) for k in order[:-1]]
    mark, *arrived = ahead_of(mark, *arrived)
    for value in arrived:
        total = total + value.astype(F32)
    return total, mark


def places(nz):
    count = NX * nz
    table = []
    for me in range(count * NC):
        z, x, c = me // (NX * NC), (me // NC) % NX, me % NC
        near = [(x ^ xr) * NC + (c ^ cr) for xr in range(NX) for cr in range(NC)]
        blocks = [(z + k) % nz for k in range(nz)]
        row = [b * NX * NC + i for b in blocks for i in near]
        spot = z if x == 0 else count - 1 - z
        for j in range(count):
            p = (spot + j) % count
            row.append(p * NX if p < nz else (count - 1 - p) * NX + 1)
        pairs = [b * NX + (x ^ xr) for b in blocks for xr in range(NX)]
        ring = row[nz * NX * NC :]
        sides = [[ring[way * j % count] for j in range(nz + 1)] for way in (-1, 1)]
        if c:
            sides.reverse()
        table.append(row + blocks + near + [c, 1 - c] + pairs + sides[0] + sides[1])
    return lax.dynamic_index_in_dim(
        jnp.asarray(np.array(table, np.int32)), lax.axis_index("front"), 0, keepdims=False
    )


class Spots:
    def __init__(self, nz):
        self.nz = nz
        group = NX * NC
        self.ring = nz * group
        self.blocks = self.ring + NX * nz
        self.near = self.blocks + nz
        self.core = self.near + group
        self.pairs = self.core + NC
        self.mine = self.pairs + nz * NX
        self.theirs = self.mine + nz + 1


def assemble(place, pieces, spots, whole):
    for piece, parts in zip(pieces, spots):
        rows = piece.shape[0] // len(parts)
        for i, spot in enumerate(parts):
            start = pl.multiple_of(place[spot] * rows, rows)
            whole[pl.ds(start, rows), :] = piece[i * rows : (i + 1) * rows, :]


def distribute(place, whole, keep, send):
    nz = len(keep)
    rows = keep[0].shape[1]
    for k in range(nz):
        for xr in range(NX):
            for cr, out in ((0, keep[k]), (1, send[k])):
                i = (k * NX + xr) * NC + cr
                out[xr] = whole[
                    pl.ds(pl.multiple_of(place[i] * rows, rows), rows), :
                ].astype(out.dtype)


def load_kernel(start, count, matrix, *refs):
    out, mark, arrived = refs[-3:]
    rows, width = out.shape
    height = rows // count
    copies = []
    for i in range(count):
        here = pl.ds(i * height, height)
        copies.append(
            pltpu.make_async_copy(
                matrix.at[here, pl.ds(start, width)], out.at[here, :], arrived.at[i]
            )
        )
    for copy in copies:
        copy.start()
    for copy in copies:
        copy.wait()
    mark[...] = jnp.zeros_like(mark)


def load_columns(matrix, part, parts, *others):
    rows, width = matrix.shape
    width //= parts
    count = max(p for p in range(1, 13) if rows % (16 * p) == 0)
    return pl.pallas_call(
        functools.partial(load_kernel, part * width, count),
        out_shape=(
            pltpu.VMEM((rows, width), matrix.dtype),
            jax.ShapeDtypeStruct((8, 128), F32),
        ),
        in_specs=[HBM] + [ANY] * len(others),
        out_specs=(VMEM, VMEM),
        scratch_shapes=[pltpu.SemaphoreType.DMA((count,))],
        compiler_params=pltpu.CompilerParams(vmem_limit_bytes=VMEM_LIMIT),
        cost_estimate=pl.CostEstimate(
            flops=0, bytes_accessed=4 * rows * width, transcendentals=0
        ),
        name="load_columns",
    )(in_hbm(matrix), *others)


def ahead_of(mark, *values):
    return lax.optimization_barrier((mark, *values))


def whole_kernel(spots, step, place, *refs):
    pieces, (matrix, _, out, out_b, cols) = refs[: len(spots)], refs[len(spots) :]
    assemble(place, pieces, spots, cols)
    total = None
    for start in range(0, cols.shape[0], step):
        here = slice(start, start + step)
        product = jnp.dot(matrix[:, here], cols[here, :], preferred_element_type=F32)
        total = product if total is None else total + product
    out[...] = total
    out_b[...] = total.astype(BF16)


def whole_product(place, pieces, matrix, mark, step):
    rows, width = matrix.shape
    n = pieces[0][0].shape[1]
    return pl.pallas_call(
        functools.partial(whole_kernel, [spots for _, spots in pieces], step),
        out_shape=(jax.ShapeDtypeStruct((rows, n), F32), jax.ShapeDtypeStruct((rows, n), BF16)),
        in_specs=[SMEM] + [VMEM] * (len(pieces) + 1) + [ANY],
        out_specs=(VMEM, VMEM),
        scratch_shapes=[pltpu.VMEM((width, n), BF16)],
        compiler_params=pltpu.CompilerParams(vmem_limit_bytes=VMEM_LIMIT),
        cost_estimate=pl.CostEstimate(
            flops=2 * rows * width * n, bytes_accessed=2 * rows * width, transcendentals=0
        ),
        name="whole_product",
    )(place, *[piece for piece, _ in pieces], in_vmem(matrix), mark)


def unit_kernel(blocks, count, where, core, fresh, last, parts, ranges, place, *refs):
    units = len(blocks)
    arrays, refs = refs[:count], refs[count:]
    accs, refs = ([], refs) if fresh else (refs[: len(ranges)], refs[len(ranges) :])
    matrix, refs = refs[:parts], refs[parts + 1 :]
    outs, cols = refs[: len(ranges)], refs[-1]
    depth = cols.shape[1]
    rows = depth // NC
    for u in range(units):
        for i, (array, part) in enumerate(where[u]):
            here = pl.ds(pl.multiple_of(place[core + i] * rows, rows), rows)
            cols[u, here, :] = arrays[array][part * rows : (part + 1) * rows, :]
    each = matrix[0].shape[1] // depth
    for u in range(units):
        index = place[blocks[u]]
        for part in range(parts):

            @pl.when(index // each == part)
            def _(u=u, part=part, index=index):
                here = pl.ds(pl.multiple_of(index % each * depth, 128), depth)
                for p, (start, height) in enumerate(ranges):
                    product = jnp.dot(
                        matrix[part][start : start + height, here],
                        cols[u],
                        preferred_element_type=F32,
                    )
                    if u:
                        outs[p][...] += product
                    elif fresh:
                        outs[p][...] = product
                    else:
                        outs[p][...] = accs[p][...] + product

    if last:
        for p in range(len(ranges)):
            refs[len(ranges) + p][...] = outs[p][...].astype(BF16)


def unit_product(
    place, blocks, arrays, parts, core, matrix, mark, accs, ranges, last
):
    n = arrays[0].shape[1]
    units = len(blocks)
    depth = matrix[0].shape[1] * len(matrix) // (lax.axis_size("front") // NC)
    rows = sum(height for _, height in ranges)
    outs = pl.pallas_call(
        functools.partial(
            unit_kernel,
            blocks,
            len(arrays),
            parts,
            core,
            not accs,
            last,
            len(matrix),
            ranges,
        ),
        out_shape=[jax.ShapeDtypeStruct((height, n), F32) for _, height in ranges]
        + [jax.ShapeDtypeStruct((height, n), BF16) for _, height in ranges] * last,
        in_specs=[SMEM] + [VMEM] * (len(arrays) + len(accs) + len(matrix)) + [ANY],
        out_specs=[VMEM] * (len(ranges) * (1 + last)),
        scratch_shapes=[pltpu.VMEM((units, depth, n), BF16)],
        compiler_params=pltpu.CompilerParams(vmem_limit_bytes=VMEM_LIMIT),
        cost_estimate=pl.CostEstimate(
            flops=2 * rows * depth * n * units,
            bytes_accessed=2 * rows * depth * units,
            transcendentals=0,
        ),
        name="unit_product",
    )(place, *arrays, *accs, *[in_vmem(m) for m in matrix], mark)
    return outs[: len(ranges)], outs[len(ranges) :]


def backward_kernel(ks, at, raw, given, ranges, parts, mode, others, place, *refs):
    raws, refs = refs[:raw], refs[raw:]
    vectors, refs = list(refs[:given]), refs[given:]
    matrix, refs = refs[:parts], refs[parts:]
    accs, refs = (refs[: len(ks)], refs[len(ks) :]) if mode == "added" else ([], refs)
    refs = refs[others:]
    if raw:
        vector = refs[-2 if mode else -1]
        total = raws[0][...] + raws[1][...].astype(F32)
        if raw == 3:
            total = raws[2][...] - total
        vector[...] = total.T.astype(BF16)
        vectors.append(vector)
    each = at.nz // parts
    depth = matrix[0].shape[1] // each
    half = depth // 2 if depth // 2 % 128 == 0 else depth
    for u, k in enumerate(ks):
        index = place[at.blocks + k]
        for part in range(parts):

            @pl.when(index // each == part)
            def _(u=u, part=part, index=index):
                for start in range(0, depth, half):
                    here = pl.ds(pl.multiple_of(index % each * depth + start, 128), half)
                    total = accs[u][:, start : start + half] if accs else None
                    for vector, (first, height) in zip(vectors, ranges):
                        product = jnp.dot(
                            vector[...],
                            matrix[part][first : first + height, here],
                            preferred_element_type=F32,
                        )
                        total = product if total is None else total + product
                    if mode:
                        refs[-1][start : start + half, :] = total.T
                    else:
                        refs[u][:, start : start + half] = total

        if mode:
            whole, (keep, send) = refs[-1], refs[2 * u : 2 * u + 2]
            rows = keep.shape[1]
            for xr in range(NX):
                for cr, out in ((0, keep), (1, send)):
                    spot = pl.multiple_of(place[at.near + xr * NC + cr] * rows, rows)
                    out[xr] = whole[pl.ds(spot, rows), :].astype(out.dtype)


def backward_blocks(place, ks, raws, vectors, ranges, matrix, accs, final, others, nz):
    n = raws[0].shape[1] if raws else vectors[0].shape[0]
    depth = matrix[0].shape[1] * len(matrix) // nz
    part = depth // (NX * NC)
    rows = sum(height for _, height in ranges)
    mode = ("added" if accs else "alone") if final else ""
    if final:
        shapes = [
            jax.ShapeDtypeStruct((NX, part, n), F32),
            jax.ShapeDtypeStruct((NX, part, n), BF16),
        ]
    else:
        shapes = [jax.ShapeDtypeStruct((n, depth), F32)]
    fresh = [jax.ShapeDtypeStruct((n, ranges[-1][1]), BF16)] if raws else []
    outs = pl.pallas_call(
        functools.partial(
            backward_kernel,
            ks,
            Spots(nz),
            len(raws),
            len(vectors),
            ranges,
            len(matrix),
            mode,
            len(others),
        ),
        out_shape=shapes * len(ks) + fresh,
        in_specs=[SMEM]
        + [VMEM] * (len(raws) + len(vectors) + len(matrix) + len(accs))
        + [ANY] * len(others),
        out_specs=[VMEM] * (len(shapes) * len(ks) + len(fresh)),
        scratch_shapes=[pltpu.VMEM((depth, n), F32)] * final,
        compiler_params=pltpu.CompilerParams(vmem_limit_bytes=LESS_VMEM),
        cost_estimate=pl.CostEstimate(
            flops=2 * rows * depth * n * len(ks),
            bytes_accessed=2 * rows * depth * len(ks),
            transcendentals=0,
        ),
        name="backward_blocks",
    )(place, *raws, *vectors, *[in_vmem(m) for m in matrix], *accs, *others)
    each = len(shapes)
    made = {k: outs[each * u : each * (u + 1)] for u, k in enumerate(ks)}
    return made, outs[-1] if raws else None


def product_scatter(multiply, groups, nz):
    keep, moved, across, left = {}, {}, {}, {}

    def cross(k):
        far = (keep[k][1] + moved[k][1].astype(F32)).astype(BF16)
        started.append(far)
        across[k] = x_swap(far, nz)

    def leave(k):
        partial = keep[k][0] + moved[k][0].astype(F32) + across[k].astype(F32)
        if k:
            partial = partial.astype(BF16)
            started.append(partial)
            partial = z_shift(partial, k, nz).astype(F32)
        left[k] = partial

    for ks, crossing, leaving in groups:
        started = []
        for k in crossing:
            cross(k)
        for k in leaving:
            leave(k)
        for k, (mine, send) in multiply(ks, started).items():
            keep[k] = mine
            moved[k] = c_swap(send, nz)
    started = []
    for k in far_first(nz):
        if k not in across:
            cross(k)
    for k in far_first(nz):
        if k not in left:
            leave(k)
    total = left[0]
    for k in far_first(nz)[:-1]:
        total = total + left[k]
    return total


def push_kernel(nz, place, block, own, arrived, coupling, mark, *refs):
    total_out, keep, send, (whole,) = refs[0], refs[1 : nz + 1], refs[nz + 1 : 2 * nz + 1], refs[2 * nz + 1 :]
    total = own[...] + arrived[...].astype(F32)
    total_out[...] = total
    pushed = jnp.dot(total.T.astype(BF16), coupling[...], preferred_element_type=F32).T
    whole[...] = jnp.zeros_like(whole)
    for j in range(coupling.shape[1] // RB):
        start = pl.multiple_of(block[j] * RB, RB)
        whole[pl.ds(start, RB), :] = pushed[j * RB : (j + 1) * RB, :]
    distribute(place, whole, keep, send)


def push_product(place, block, own, arrived, coupling, mark, width, nz):
    n = own.shape[1]
    part = width // (nz * NX * NC)
    outs = pl.pallas_call(
        functools.partial(push_kernel, nz),
        out_shape=[jax.ShapeDtypeStruct(own.shape, F32)]
        + [jax.ShapeDtypeStruct((NX, part, n), F32)] * nz
        + [jax.ShapeDtypeStruct((NX, part, n), BF16)] * nz,
        in_specs=[SMEM, SMEM, VMEM, VMEM, VMEM, ANY],
        out_specs=[VMEM] * (2 * nz + 1),
        scratch_shapes=[pltpu.VMEM((width, n), F32)],
        compiler_params=pltpu.CompilerParams(vmem_limit_bytes=VMEM_LIMIT),
        name="push_product",
    )(place, block, own, arrived, coupling, mark)
    return outs[0], outs[1 : nz + 1], outs[nz + 1 :]


def pull_kernel(spots, place, block, *refs):
    pieces, (coupling, _, out, out_b, whole, picked) = refs[: len(spots)], refs[len(spots) :]
    assemble(place, pieces, spots, whole)
    for j in range(coupling.shape[1] // RB):
        start = pl.multiple_of(block[j] * RB, RB)
        picked[j * RB : (j + 1) * RB, :] = whole[pl.ds(start, RB), :]
    out[...] = jnp.dot(coupling[...], picked[...], preferred_element_type=F32)
    out_b[...] = out[...].astype(BF16)


def pull_product(place, block, pieces, coupling, mark, height):
    rows, width = coupling.shape
    n = pieces[0][0].shape[1]
    return pl.pallas_call(
        functools.partial(pull_kernel, [spots for _, spots in pieces]),
        out_shape=(
            jax.ShapeDtypeStruct((rows, n), F32),
            jax.ShapeDtypeStruct((rows, n), BF16),
        ),
        in_specs=[SMEM, SMEM] + [VMEM] * (len(pieces) + 1) + [ANY],
        out_specs=(VMEM, VMEM),
        scratch_shapes=[pltpu.VMEM((height, n), BF16), pltpu.VMEM((width, n), BF16)],
        compiler_params=pltpu.CompilerParams(vmem_limit_bytes=VMEM_LIMIT),
        name="pull_product",
    )(place, block, *[piece for piece, _ in pieces], coupling, mark)


def in_hbm(matrix):
    return pltpu.with_memory_space_constraint(matrix, pltpu.HBM)


def in_vmem(matrix):
    return pltpu.with_memory_space_constraint(matrix, pltpu.VMEM)


def two_level_body(rhs_root, rhs_level, root_inverse, level_inverse, coupling_t, coupling_rows):
    nz = lax.axis_size("front") // (NX * NC)
    width = root_inverse.shape[1]
    place = places(nz)
    block = coupling_rows[0] % (width // RB)

    level_vmem, mark = load_columns(level_inverse, 0, 1, place, block)
    pieces, mark = gather_pieces(rhs_level.astype(BF16), mark, nz)
    own, own_b = whole_product(place, pieces, level_vmem, mark, level_inverse.shape[1] // nz)
    arrived = sub_swap(own_b)
    top, mark = load_columns(root_inverse, 0, 2, own_b)
    forward_level, keep, send = push_product(
        place, block, own, arrived, coupling_t, mark, width, nz
    )
    halves = [top]

    def load(value):
        bottom, mark = load_columns(root_inverse, 1, 2, value)
        halves.append(bottom)
        return mark

    update, mark = scatter_sum(keep, send, load, nz)
    shifted = rhs_root - update

    middle = root_inverse.shape[0] // 2
    upper, lower = (0, middle), (middle, middle)
    own, own_b = ring_product(
        place, shifted.astype(BF16), halves, [upper, lower], mark, nz
    )
    arrived = [sub_swap(value) for value in own_b]
    far = far_first(nz)
    others, mine = far[:-1], far[-1]
    accs, vector = backward_blocks(
        place, others, [own[0], arrived[0]], [], [upper], halves, [], False, [], nz
    )
    vectors = [vector]

    def multiply_root(ks, started):
        raws = [own[1], arrived[1]] if len(vectors) == 1 else []
        if ks == [mine]:
            made, _ = backward_blocks(
                place, ks, [], vectors, [upper, lower], halves, [], True, started, nz
            )
            return made
        added = [accs[k][0] for k in ks]
        made, vector = backward_blocks(
            place, ks, raws, vectors[1:], [lower], halves, added, True, started, nz
        )
        if raws:
            vectors.append(vector)
        return made

    groups = [([far[0]], [], []), ([far[1]], [], []), (far[2:-1], far[:1], [])]
    groups += [([mine], far[1:-1], far[:1])]
    root_potential = product_scatter(multiply_root, groups, nz)

    level_vmem, mark = load_columns(level_inverse, 0, 1, root_potential)
    pieces, mark = gather_pieces(root_potential.astype(BF16), mark, nz)
    own, own_b = pull_product(place, block, pieces, coupling_t, mark, width)
    raws = [own, sub_swap(own_b), forward_level]
    level_rows = [(0, level_inverse.shape[0])]
    vector = None

    def multiply_level(ks, started):
        nonlocal vector
        given = ([], [vector]) if vector is not None else (raws, [])
        made, new = backward_blocks(
            place, ks, *given, level_rows, [level_vmem], [], True, started, nz
        )
        vector = new if vector is None else vector
        return made

    groups = [(far[:1], [], []), (far[1:-1], [], []), ([mine], far[:-1], [])]
    level_potential = product_scatter(multiply_level, groups, nz)
    return (root_potential, level_potential)


def body(rhs_root, rhs_level, root_inverse, level_inverse, coupling_t, coupling_rows):
    fits = (
        lax.axis_size("sub") == 2
        and lax.axis_size("front") % (NX * NC) == 0
        and lax.axis_size("front") >= 3 * NX * NC
        and all(a.shape[0] % 16 == 0 for a in (rhs_root, rhs_level, root_inverse, level_inverse))
        and all(a.shape[1] % 128 == 0 for a in (rhs_root, root_inverse, level_inverse, coupling_t))
        and NC * rhs_root.shape[0] % 128 == 0
        and NX * NC * rhs_level.shape[0] % 128 == 0
        and (root_inverse.size + level_inverse.size) * 2 <= 40 * 1024 * 1024
        and root_inverse.shape[0] % 32 == 0
        and root_inverse.shape[1] % (4 * rhs_root.shape[0] * NC) == 0
    )
    chosen = two_level_body if fits else general_body
    return chosen(rhs_root, rhs_level, root_inverse, level_inverse, coupling_t, coupling_rows)


def solution(mesh):
    return jax.shard_map(
        body,
        mesh=mesh,
        in_specs=(
            P(("sub", "front"), None),
            P(("sub", "front"), None),
            P("front", "sub"),
            P("front", "sub"),
            P("front", "sub"),
            P("front", "sub"),
        ),
        out_specs=(P(("sub", "front"), None), P(("sub", "front"), None)),
        check_vma=False,
    )
```

```python
import functools

import jax
import jax.numpy as jnp
import numpy as np
from jax import lax
from jax.experimental import pallas as pl
from jax.experimental.pallas import tpu as pltpu
from jax.sharding import PartitionSpec as P

RB = 128
NX = 2
NC = 2
F32 = jnp.float32
BF16 = jnp.bfloat16
HIGHEST_PRECISION = lax.Precision.HIGHEST
VMEM = pl.BlockSpec(memory_space=pltpu.VMEM)
SMEM = pl.BlockSpec(memory_space=pltpu.SMEM)
HBM = pl.BlockSpec(memory_space=pltpu.HBM)
ANY = pl.BlockSpec(memory_space=pl.ANY)
VMEM_LIMIT = 15 * 1024 * 1024
LESS_VMEM = 8 * 1024 * 1024


def transposed_product(matrix, vector):
    return lax.dot_general(
        matrix, vector, (((0,), (0,)), ((), ())), preferred_element_type=jnp.float32
    )


def gather_columns(pieces):
    return lax.all_gather(pieces, "front", axis=0, tiled=True)


def gather_rows(pieces):
    return lax.all_gather(pieces, "sub", axis=0, tiled=True)


def share_sub(summand):
    return lax.psum_scatter(
        summand.astype(jnp.bfloat16), "sub", scatter_dimension=0, tiled=True
    ).astype(jnp.float32)


def share_front(summand):
    return lax.psum_scatter(summand, "front", scatter_dimension=0, tiled=True)


def general_body(rhs_root, rhs_level, root_inverse, level_inverse, coupling_t, coupling_rows):
    rhs_count = rhs_root.shape[1]
    block_count = root_inverse.shape[1] // RB
    slot_count = coupling_t.shape[1] // RB
    level_cols = gather_columns(rhs_level.astype(jnp.bfloat16))
    forward_level = share_sub(
        jnp.dot(level_inverse, level_cols, preferred_element_type=jnp.float32)
    )
    level_rows = gather_rows(forward_level.astype(jnp.bfloat16))
    local_block = coupling_rows[0] % block_count
    selector = (
        lax.broadcasted_iota(jnp.int32, (block_count, slot_count), 0) == local_block[None, :]
    ).astype(jnp.float32)
    pushed = transposed_product(coupling_t, level_rows).reshape(slot_count, RB, rhs_count)
    update = jnp.einsum("bk,kin->bin", selector, pushed, precision=HIGHEST_PRECISION).reshape(
        block_count * RB, rhs_count
    )
    shifted = rhs_root - share_front(update)
    root_cols = gather_columns(shifted.astype(jnp.bfloat16))
    forward_root = share_sub(jnp.dot(root_inverse, root_cols, preferred_element_type=jnp.float32))
    root_rows = gather_rows(forward_root.astype(jnp.bfloat16))
    root_potential = share_front(transposed_product(root_inverse, root_rows))
    potential_cols = gather_columns(root_potential.astype(jnp.bfloat16))
    picked = potential_cols.reshape(block_count, RB, rhs_count)[local_block]
    pulled = jnp.dot(
        coupling_t, picked.reshape(slot_count * RB, rhs_count), preferred_element_type=jnp.float32
    )
    corrected = forward_level - share_sub(pulled)
    corrected_rows = gather_rows(corrected.astype(jnp.bfloat16))
    level_potential = share_front(transposed_product(level_inverse, corrected_rows))
    return (root_potential, level_potential)


def z_shift(value, shift, nz):
    width = NX * NC
    count = nz * width
    return lax.ppermute(
        value, "front", [(i, (i + shift * width) % count) for i in range(count)]
    )


def x_swap(value, nz):
    return lax.ppermute(value, "front", [(i, i ^ NC) for i in range(nz * NX * NC)])


def c_swap(value, nz):
    return lax.ppermute(value, "front", [(i, i ^ 1) for i in range(nz * NX * NC)])


def sub_swap(value):
    return lax.ppermute(value, "sub", [(0, 1), (1, 0)])


def gather_pieces(own, mark, nz):
    group = NX * NC
    order = near_first(nz)
    held = {0: own}
    for k in order[1:]:
        held[k] = z_shift(own, -k, nz)
    mark, *arrived = ahead_of(mark, *[held[k] for k in order[1:-1]])
    held.update(zip(order[1:-1], arrived))
    across = {}
    for k in order:
        across[k] = x_swap(held[k], nz)
    lanes = [(k * group, held[k]) for k in order], [(k * group + NC, across[k]) for k in order]
    pieces = lanes[0] + lanes[1]
    out = [(piece, [spot]) for spot, piece in pieces]
    batches = [list(pair) for pair in zip(*lanes)]
    for batch in batches[:-1] + [batches[-1][:1], batches[-1][1:]]:
        sent = [piece for _, piece in batch]
        sent = jnp.concatenate(sent) if len(sent) > 1 else sent[0]
        out.append((c_swap(sent, nz), [spot + 1 for spot, _ in batch]))
    return out, mark


def near_first(nz):
    return sorted(range(nz), key=lambda k: min(k, nz - k))


def ring_step(value, way, nz):
    count = NX * nz
    chip = lambda p: (p * NX if p < nz else (count - 1 - p) * NX + 1)
    pairs = [
        (chip(p) * NC + c, chip((p + way) % count) * NC + c)
        for p in range(count)
        for c in range(NC)
    ]
    return lax.ppermute(value, "front", pairs)


def ring_product(place, own, matrix, ranges, mark, nz):
    count = NX * nz
    at = Spots(nz)
    accs, waiting = [], None
    held = {0: own}

    def multiply(units, accs, ranges, last=False):
        blocks = [at.ring + j for j in units]
        pieces = list(units.values())
        return unit_product(place, blocks, at.core, pieces, matrix, mark, accs, ranges, last)

    for step in range(nz + 1):
        if step > 1:
            first, *arrived = ahead_of(accs[0], *held.values())
            accs = [first, *accs[1:]]
            held = dict(zip(held, arrived))
        following = {}
        if step < nz:
            following[(-step - 1) % count] = ring_step(held[(-step) % count], 1, nz)
            if step < nz - 1:
                following[step + 1] = ring_step(held[step], -1, nz)
        units = {j: [piece, c_swap(piece, nz)] for j, piece in held.items()}
        if waiting:
            accs, _ = multiply(waiting, accs, ranges)
        waiting, held = units, following
    outs = [
        multiply(waiting, [acc], [rows], True) for acc, rows in zip(accs, ranges)
    ]
    return [own for (own,), _ in outs], [own_b for _, (own_b,) in outs]


def far_first(nz):
    return near_first(nz)[::-1]


def scatter_sum(keep, send, load, nz):
    order = far_first(nz)
    moved = {k: c_swap(send[k], nz) for k in order}
    across, partial = {}, {}
    for k in order:
        far = (keep[k][1].astype(F32) + moved[k][1].astype(F32)).astype(BF16)
        across[k] = x_swap(far, nz)
        if k == order[-2]:
            mark = load(far)
    mark, across[order[0]] = ahead_of(mark, across[order[0]])
    for k in order:
        partial[k] = keep[k][0].astype(F32) + moved[k][0].astype(F32) + across[k].astype(F32)
    total = partial[0]
    leaving = {k: partial[k].astype(BF16) for k in order[:-1]}
    mark = load(leaving[order[-2]], mark)
    arrived = [z_shift(leaving[k], k, nz) for k in order[:-1]]
    mark, *arrived = ahead_of(mark, *arrived)
    for value in arrived:
        total = total + value.astype(F32)
    return total, mark


def places(nz):
    count = NX * nz
    table = []
    for me in range(count * NC):
        z, x, c = me // (NX * NC), (me // NC) % NX, me % NC
        near = [(x ^ xr) * NC + (c ^ cr) for xr in range(NX) for cr in range(NC)]
        blocks = [(z + k) % nz for k in range(nz)]
        row = [b * NX * NC + i for b in blocks for i in near]
        spot = z if x == 0 else count - 1 - z
        for j in range(count):
            p = (spot + j) % count
            row.append(p * NX if p < nz else (count - 1 - p) * NX + 1)
        pairs = [b * NX + (x ^ xr) for b in blocks for xr in range(NX)]
        table.append(row + blocks + near + [c, 1 - c] + pairs)
    return lax.dynamic_index_in_dim(
        jnp.asarray(np.array(table, np.int32)), lax.axis_index("front"), 0, keepdims=False
    )


class Spots:
    def __init__(self, nz):
        self.nz = nz
        group = NX * NC
        self.ring = nz * group
        self.blocks = self.ring + NX * nz
        self.near = self.blocks + nz
        self.core = self.near + group
        self.pairs = self.core + NC


def assemble(place, pieces, spots, whole):
    for piece, parts in zip(pieces, spots):
        rows = piece.shape[0] // len(parts)
        for i, spot in enumerate(parts):
            start = pl.multiple_of(place[spot] * rows, rows)
            whole[pl.ds(start, rows), :] = piece[i * rows : (i + 1) * rows, :]


def distribute(place, whole, keep, send):
    nz = len(keep)
    rows = keep[0].shape[1]
    for k in range(nz):
        for xr in range(NX):
            for cr, out in ((0, keep[k]), (1, send[k])):
                i = (k * NX + xr) * NC + cr
                out[xr] = whole[
                    pl.ds(pl.multiple_of(place[i] * rows, rows), rows), :
                ].astype(out.dtype)


def load_kernel(start, count, matrix, *refs):
    out, mark, arrived = refs[-3:]
    rows, width = out.shape
    height = rows // count
    copies = []
    for i in range(count):
        here = pl.ds(i * height, height)
        copies.append(
            pltpu.make_async_copy(
                matrix.at[here, pl.ds(start, width)], out.at[here, :], arrived.at[i]
            )
        )
    for copy in copies:
        copy.start()
    for copy in copies:
        copy.wait()
    mark[...] = jnp.zeros_like(mark)


def load_columns(matrix, start, width, *others):
    rows = matrix.shape[0]
    count = max(p for p in range(1, 13) if rows % (16 * p) == 0)
    return pl.pallas_call(
        functools.partial(load_kernel, start, count),
        out_shape=(
            pltpu.VMEM((rows, width), matrix.dtype),
            jax.ShapeDtypeStruct((8, 128), F32),
        ),
        in_specs=[HBM] + [ANY] * len(others),
        out_specs=(VMEM, VMEM),
        scratch_shapes=[pltpu.SemaphoreType.DMA((count,))],
        compiler_params=pltpu.CompilerParams(vmem_limit_bytes=VMEM_LIMIT),
        cost_estimate=pl.CostEstimate(
            flops=0, bytes_accessed=4 * rows * width, transcendentals=0
        ),
        name="load_columns",
    )(in_hbm(matrix), *others)


def ahead_of(mark, *values):
    return lax.optimization_barrier((mark, *values))


def whole_kernel(spots, step, place, *refs):
    pieces, (matrix, _, out, out_b, cols) = refs[: len(spots)], refs[len(spots) :]
    assemble(place, pieces, spots, cols)
    total = None
    for start in range(0, cols.shape[0], step):
        here = slice(start, start + step)
        product = jnp.dot(matrix[:, here], cols[here, :], preferred_element_type=F32)
        total = product if total is None else total + product
    out[...] = total
    out_b[...] = total.astype(BF16)


def whole_product(place, pieces, matrix, mark, step):
    rows, width = matrix.shape
    n = pieces[0][0].shape[1]
    return pl.pallas_call(
        functools.partial(whole_kernel, [spots for _, spots in pieces], step),
        out_shape=(jax.ShapeDtypeStruct((rows, n), F32), jax.ShapeDtypeStruct((rows, n), BF16)),
        in_specs=[SMEM] + [VMEM] * (len(pieces) + 1) + [ANY],
        out_specs=(VMEM, VMEM),
        scratch_shapes=[pltpu.VMEM((width, n), BF16)],
        compiler_params=pltpu.CompilerParams(vmem_limit_bytes=VMEM_LIMIT),
        cost_estimate=pl.CostEstimate(
            flops=2 * rows * width * n, bytes_accessed=2 * rows * width, transcendentals=0
        ),
        name="whole_product",
    )(place, *[piece for piece, _ in pieces], in_vmem(matrix), mark)


def bounds(matrix, depth):
    ends = [0]
    for columns in matrix:
        ends.append(ends[-1] + columns.shape[1] // depth)
    return list(zip(range(len(matrix)), ends, ends[1:]))


def unit_kernel(blocks, spots, count, fresh, last, parts, ranges, place, *refs):
    units = len(blocks)
    pieces, refs = refs[: units * count], refs[units * count :]
    accs, refs = ([], refs) if fresh else (refs[: len(ranges)], refs[len(ranges) :])
    matrix, refs = refs[:parts], refs[parts + 1 :]
    outs, cols = refs[: len(ranges)], refs[-1]
    rows = pieces[0].shape[0]
    depth = cols.shape[1]
    for i, piece in enumerate(pieces):
        at = place[spots + i % count]
        cols[i // count, pl.ds(pl.multiple_of(at * rows, rows), rows), :] = piece[...]
    for u in range(units):
        index = place[blocks[u]]
        for part, low, high in bounds(matrix, depth):

            @pl.when((index >= low) & (index < high))
            def _(u=u, part=part, index=index - low):
                here = pl.ds(pl.multiple_of(index * depth, 128), depth)
                for p, (start, height) in enumerate(ranges):
                    product = jnp.dot(
                        matrix[part][start : start + height, here],
                        cols[u],
                        preferred_element_type=F32,
                    )
                    if u:
                        outs[p][...] += product
                    elif fresh:
                        outs[p][...] = product
                    else:
                        outs[p][...] = accs[p][...] + product

    if last:
        for p in range(len(ranges)):
            refs[len(ranges) + p][...] = outs[p][...].astype(BF16)


def unit_product(place, blocks, spots, units, matrix, mark, accs, ranges, last):
    part, n = units[0][0].shape
    count = len(units[0])
    depth = count * part
    pieces = [piece for unit in units for piece in unit]
    rows = sum(height for _, height in ranges)
    parts = len(matrix)
    outs = pl.pallas_call(
        functools.partial(unit_kernel, blocks, spots, count, not accs, last, parts, ranges),
        out_shape=[jax.ShapeDtypeStruct((height, n), F32) for _, height in ranges]
        + [jax.ShapeDtypeStruct((height, n), BF16) for _, height in ranges] * last,
        in_specs=[SMEM] + [VMEM] * (len(pieces) + len(accs) + parts) + [ANY],
        out_specs=[VMEM] * (len(ranges) * (1 + last)),
        scratch_shapes=[pltpu.VMEM((len(units), depth, n), BF16)],
        compiler_params=pltpu.CompilerParams(vmem_limit_bytes=VMEM_LIMIT),
        cost_estimate=pl.CostEstimate(
            flops=2 * rows * depth * n * len(units),
            bytes_accessed=2 * rows * depth * len(units),
            transcendentals=0,
        ),
        name="unit_product",
    )(place, *pieces, *accs, *[in_vmem(m) for m in matrix], mark)
    return outs[: len(ranges)], outs[len(ranges) :]


def backward_kernel(ks, at, raw, given, ranges, parts, mode, others, place, *refs):
    raws, refs = refs[:raw], refs[raw:]
    vectors, refs = list(refs[:given]), refs[given:]
    matrix, refs = refs[:parts], refs[parts:]
    accs, refs = (refs[: len(ks)], refs[len(ks) :]) if mode == "added" else ([], refs)
    refs = refs[others:]
    if raw:
        vector = refs[-2 if mode else -1]
        total = raws[0][...] + raws[1][...].astype(F32)
        if raw == 3:
            total = raws[2][...] - total
        vector[...] = total.T.astype(BF16)
        vectors.append(vector)
    depth = sum(m.shape[1] for m in matrix) // at.nz
    half = depth // 2 if depth // 2 % 128 == 0 else depth
    for u, k in enumerate(ks):
        index = place[at.blocks + k]
        for part, low, high in bounds(matrix, depth):

            @pl.when((index >= low) & (index < high))
            def _(u=u, part=part, index=index - low):
                for start in range(0, depth, half):
                    here = pl.ds(pl.multiple_of(index * depth + start, 128), half)
                    total = accs[u][:, start : start + half] if accs else None
                    for vector, (first, height) in zip(vectors, ranges):
                        product = jnp.dot(
                            vector[...],
                            matrix[part][first : first + height, here],
                            preferred_element_type=F32,
                        )
                        total = product if total is None else total + product
                    if mode:
                        refs[-1][start : start + half, :] = total.T
                    else:
                        refs[u][:, start : start + half] = total

        if mode:
            whole, (keep, send) = refs[-1], refs[2 * u : 2 * u + 2]
            rows = keep.shape[1]
            for xr in range(NX):
                for cr, out in ((0, keep), (1, send)):
                    spot = pl.multiple_of(place[at.near + xr * NC + cr] * rows, rows)
                    out[xr] = whole[pl.ds(spot, rows), :].astype(out.dtype)


def backward_blocks(place, ks, raws, vectors, ranges, matrix, accs, final, others, nz):
    n = raws[0].shape[1] if raws else vectors[0].shape[0]
    depth = sum(m.shape[1] for m in matrix) // nz
    part = depth // (NX * NC)
    rows = sum(height for _, height in ranges)
    mode = ("added" if accs else "alone") if final else ""
    if final:
        shapes = [
            jax.ShapeDtypeStruct((NX, part, n), F32),
            jax.ShapeDtypeStruct((NX, part, n), BF16),
        ]
    else:
        shapes = [jax.ShapeDtypeStruct((n, depth), F32)]
    fresh = [jax.ShapeDtypeStruct((n, ranges[-1][1]), BF16)] if raws else []
    outs = pl.pallas_call(
        functools.partial(
            backward_kernel,
            ks,
            Spots(nz),
            len(raws),
            len(vectors),
            ranges,
            len(matrix),
            mode,
            len(others),
        ),
        out_shape=shapes * len(ks) + fresh,
        in_specs=[SMEM]
        + [VMEM] * (len(raws) + len(vectors) + len(matrix) + len(accs))
        + [ANY] * len(others),
        out_specs=[VMEM] * (len(shapes) * len(ks) + len(fresh)),
        scratch_shapes=[pltpu.VMEM((depth, n), F32)] * final,
        compiler_params=pltpu.CompilerParams(vmem_limit_bytes=LESS_VMEM),
        cost_estimate=pl.CostEstimate(
            flops=2 * rows * depth * n * len(ks),
            bytes_accessed=2 * rows * depth * len(ks),
            transcendentals=0,
        ),
        name="backward_blocks",
    )(place, *raws, *vectors, *[in_vmem(m) for m in matrix], *accs, *others)
    each = len(shapes)
    made = {k: outs[each * u : each * (u + 1)] for u, k in enumerate(ks)}
    return made, outs[-1] if raws else None


def product_scatter(multiply, groups, nz):
    keep, moved, across, left = {}, {}, {}, {}

    def cross(k):
        far = (keep[k][1] + moved[k][1].astype(F32)).astype(BF16)
        started.append(far)
        across[k] = x_swap(far, nz)

    def leave(k):
        partial = keep[k][0] + moved[k][0].astype(F32) + across[k].astype(F32)
        if k:
            partial = partial.astype(BF16)
            started.append(partial)
            partial = z_shift(partial, k, nz).astype(F32)
        left[k] = partial

    for ks, crossing, leaving in groups:
        started = []
        for k in crossing:
            cross(k)
        for k in leaving:
            leave(k)
        for k, (mine, send) in multiply(ks, started).items():
            keep[k] = mine
            moved[k] = c_swap(send, nz)
    started = []
    for k in far_first(nz):
        if k not in across:
            cross(k)
    for k in far_first(nz):
        if k not in left:
            leave(k)
    total = left[0]
    for k in far_first(nz)[:-1]:
        total = total + left[k]
    return total


def push_kernel(nz, place, block, own, arrived, coupling, mark, *refs):
    total_out, keep, send, (whole,) = refs[0], refs[1 : nz + 1], refs[nz + 1 : 2 * nz + 1], refs[2 * nz + 1 :]
    total = own[...] + arrived[...].astype(F32)
    total_out[...] = total
    pushed = jnp.dot(total.T.astype(BF16), coupling[...], preferred_element_type=F32).T
    whole[...] = jnp.zeros_like(whole)
    for j in range(coupling.shape[1] // RB):
        start = pl.multiple_of(block[j] * RB, RB)
        whole[pl.ds(start, RB), :] = pushed[j * RB : (j + 1) * RB, :].astype(BF16)
    distribute(place, whole, keep, send)


def push_product(place, block, own, arrived, coupling, mark, width, nz):
    n = own.shape[1]
    part = width // (nz * NX * NC)
    outs = pl.pallas_call(
        functools.partial(push_kernel, nz),
        out_shape=[jax.ShapeDtypeStruct(own.shape, F32)]
        + [jax.ShapeDtypeStruct((NX, part, n), BF16)] * (2 * nz),
        in_specs=[SMEM, SMEM, VMEM, VMEM, VMEM, ANY],
        out_specs=[VMEM] * (2 * nz + 1),
        scratch_shapes=[pltpu.VMEM((width, n), BF16)],
        compiler_params=pltpu.CompilerParams(vmem_limit_bytes=VMEM_LIMIT),
        name="push_product",
    )(place, block, own, arrived, coupling, mark)
    return outs[0], outs[1 : nz + 1], outs[nz + 1 :]


def pull_kernel(spots, place, block, *refs):
    pieces, (coupling, _, out, out_b, whole, picked) = refs[: len(spots)], refs[len(spots) :]
    assemble(place, pieces, spots, whole)
    for j in range(coupling.shape[1] // RB):
        start = pl.multiple_of(block[j] * RB, RB)
        picked[j * RB : (j + 1) * RB, :] = whole[pl.ds(start, RB), :]
    out[...] = jnp.dot(coupling[...], picked[...], preferred_element_type=F32)
    out_b[...] = out[...].astype(BF16)


def pull_product(place, block, pieces, coupling, mark, height):
    rows, width = coupling.shape
    n = pieces[0][0].shape[1]
    return pl.pallas_call(
        functools.partial(pull_kernel, [spots for _, spots in pieces]),
        out_shape=(
            jax.ShapeDtypeStruct((rows, n), F32),
            jax.ShapeDtypeStruct((rows, n), BF16),
        ),
        in_specs=[SMEM, SMEM] + [VMEM] * (len(pieces) + 1) + [ANY],
        out_specs=(VMEM, VMEM),
        scratch_shapes=[pltpu.VMEM((height, n), BF16), pltpu.VMEM((width, n), BF16)],
        compiler_params=pltpu.CompilerParams(vmem_limit_bytes=VMEM_LIMIT),
        name="pull_product",
    )(place, block, *[piece for piece, _ in pieces], coupling, mark)


def in_hbm(matrix):
    return pltpu.with_memory_space_constraint(matrix, pltpu.HBM)


def in_vmem(matrix):
    return pltpu.with_memory_space_constraint(matrix, pltpu.VMEM)


def two_level_body(rhs_root, rhs_level, root_inverse, level_inverse, coupling_t, coupling_rows):
    nz = lax.axis_size("front") // (NX * NC)
    width = root_inverse.shape[1]
    place = places(nz)
    block = coupling_rows[0] % (width // RB)

    level_vmem, mark = load_columns(level_inverse, 0, level_inverse.shape[1], place, block)
    pieces, mark = gather_pieces(rhs_level.astype(BF16), mark, nz)
    own, own_b = whole_product(place, pieces, level_vmem, mark, level_inverse.shape[1] // nz)
    arrived = sub_swap(own_b)
    blocks = width // nz
    first, mark = load_columns(root_inverse, 0, blocks, own_b)
    forward_level, keep, send = push_product(
        place, block, own, arrived, coupling_t, mark, width, nz
    )
    halves = [first]

    def load(*values):
        start = len(halves) * blocks
        size = blocks if len(halves) == 1 else width - start
        columns, mark = load_columns(root_inverse, start, size, *values)
        halves.append(columns)
        return mark

    update, mark = scatter_sum(keep, send, load, nz)
    shifted = rhs_root - update

    middle = root_inverse.shape[0] // 2
    upper, lower = (0, middle), (middle, middle)
    own, own_b = ring_product(
        place, shifted.astype(BF16), halves, [upper, lower], mark, nz
    )
    arrived = [sub_swap(value) for value in own_b]
    far = far_first(nz)
    others, mine = far[:-1], far[-1]
    accs, vector = backward_blocks(
        place, others, [own[0], arrived[0]], [], [upper], halves, [], False, [], nz
    )
    vectors = [vector]

    def multiply_root(ks, started):
        raws = [own[1], arrived[1]] if len(vectors) == 1 else []
        if ks == [mine]:
            made, _ = backward_blocks(
                place, ks, [], vectors, [upper, lower], halves, [], True, started, nz
            )
            return made
        added = [accs[k][0] for k in ks]
        made, vector = backward_blocks(
            place, ks, raws, vectors[1:], [lower], halves, added, True, started, nz
        )
        if raws:
            vectors.append(vector)
        return made

    groups = [([far[0]], [], []), ([far[1]], [], []), (far[2:-1], far[:1], [])]
    groups += [([mine], far[1:-1], far[:1])]
    root_potential = product_scatter(multiply_root, groups, nz)

    level_vmem, mark = load_columns(
        level_inverse, 0, level_inverse.shape[1], root_potential
    )
    pieces, mark = gather_pieces(root_potential.astype(BF16), mark, nz)
    own, own_b = pull_product(place, block, pieces, coupling_t, mark, width)
    raws = [own, sub_swap(own_b), forward_level]
    level_rows = [(0, level_inverse.shape[0])]
    vector = None

    def multiply_level(ks, started):
        nonlocal vector
        given = ([], [vector]) if vector is not None else (raws, [])
        made, new = backward_blocks(
            place, ks, *given, level_rows, [level_vmem], [], True, started, nz
        )
        vector = new if vector is None else vector
        return made

    groups = [(far[:1], [], []), (far[1:-1], [], []), ([mine], far[:-1], [])]
    level_potential = product_scatter(multiply_level, groups, nz)
    return (root_potential, level_potential)


def body(rhs_root, rhs_level, root_inverse, level_inverse, coupling_t, coupling_rows):
    fits = (
        lax.axis_size("sub") == 2
        and lax.axis_size("front") % (NX * NC) == 0
        and lax.axis_size("front") >= 3 * NX * NC
        and all(a.shape[0] % 16 == 0 for a in (rhs_root, rhs_level, root_inverse, level_inverse))
        and all(a.shape[1] % 128 == 0 for a in (rhs_root, root_inverse, level_inverse, coupling_t))
        and NC * rhs_root.shape[0] % 128 == 0
        and NX * NC * rhs_level.shape[0] % 128 == 0
        and (root_inverse.size + level_inverse.size) * 2 <= 40 * 1024 * 1024
        and root_inverse.shape[0] % 32 == 0
        and root_inverse.shape[1] % (4 * rhs_root.shape[0] * NC) == 0
    )
    chosen = two_level_body if fits else general_body
    return chosen(rhs_root, rhs_level, root_inverse, level_inverse, coupling_t, coupling_rows)


def solution(mesh):
    return jax.shard_map(
        body,
        mesh=mesh,
        in_specs=(
            P(("sub", "front"), None),
            P(("sub", "front"), None),
            P("front", "sub"),
            P("front", "sub"),
            P("front", "sub"),
            P("front", "sub"),
        ),
        out_specs=(P(("sub", "front"), None), P(("sub", "front"), None)),
        check_vma=False,
    )
```
